512 devices in a mesh: rep: 16 (over z_hi, y), fsdp: 32 (over z_lo, x, core).
Axes of the slice: x: 4, y: 4, z: 16 (z_hi: 4, z_lo: 4; z = z_hi * 4 + z_lo), core: 2. Of those that a mesh axis runs over, the one named last changes fastest.
Arguments:
- activations: bfloat16 [65536, 5120], P(('rep', 'fsdp')), may hold values from -6 to 6
- out_grad: bfloat16 [65536, 128], P(('rep', 'fsdp')), may hold values from -0.09375 to 0.09375
- momentum: float32 [16, 160, 64, 64], P('rep', 'fsdp'), may hold values from -6 to 6
- weight: float32 [160, 64, 64], P('fsdp'), may hold values from -6 to 6
- kept_tile: int32 [16, 160], P('rep', 'fsdp'), may hold values from 0 to 63
Outputs:
- new_momentum: float32 [16, 160, 64, 64], P('rep', 'fsdp')
- new_weight: float32 [160, 64, 64], P('fsdp')
The draws below stay inside these ranges and needn't reach their ends.
Inputs may be any that keep to these rules, and one draw needn't show every extreme that they name: `kept_tile`: tile number t names the tile in block row t // 8 and block column t % (8) of a span's coefficients.
All inputs are finite; a program needn't handle non-finite values.
Results may differ from the reference program's by a relative error of at most 0.0003.
Values sent between devices are 32-bit elements; how exact they have to be, the bound alone decides.
A program may use at most 64 MiB of HBM per device.

```python
import math
import jax
import jax.numpy as jnp
from jax import lax

D = 5120
ROWS = 128
TOK_DEV = 128
SPAN = 64
TILE = 8
NCHUNK = 160
REPS = 16
TOKENS = 65536
N_REP = 16
N_FSDP = 32


def plant(drawn, own_key, least, top_value):
    dims = drawn.shape
    spot = [jax.random.randint(jax.random.fold_in(own_key, axis), (), 0, dims[axis]) for axis in range(len(dims))]
    drawn = drawn.at[tuple(spot)].set(least)
    longest = dims.index(max(dims))
    spot[longest] = (spot[longest] + 1) % dims[longest]
    return drawn.at[tuple(spot)].set(top_value)


def shard_levels(stream_key, dims, shards, low, high):
    factor_of, own = 1.0, jax.random.fold_in(stream_key, 6)
    for axis_at, blocks in shards:
        heights = jnp.exp(jax.random.uniform(jax.random.fold_in(own, axis_at), (blocks,), jnp.float32, low / len(shards), high / len(shards)))
        factor_of = factor_of * jnp.repeat(heights, dims[axis_at] // blocks).reshape([-1 if axis == axis_at else 1 for axis in range(len(dims))])
    return factor_of


def noise(rng, extent, deviation, reach, shards=(), held_as=jnp.bfloat16):
    gain = shard_levels(rng, extent, shards, -0.22, 0.18) if shards else 1.0
    result = jax.random.normal(rng, extent, jnp.float32) * deviation * gain
    return jnp.minimum(jnp.maximum(result, -reach), reach).astype(held_as)


def setup_inputs(seed: int = 0) -> dict:
    key_list = jax.random.split(jax.random.key(seed), 6)
    activations = noise(key_list[0], (TOKENS, D), 1.0, 6.0, ((0, 512),))
    out_grad = noise(key_list[1], (TOKENS, ROWS), (TOK_DEV * N_FSDP) ** -0.5, 0.09375, ((0, 512),))
    momentum = noise(key_list[2], (REPS, NCHUNK, SPAN, SPAN), 1.0, 6.0, ((0, 16), (1, 32)), jnp.float32)
    weight = noise(key_list[3], (NCHUNK, SPAN, SPAN), 1.0, 6.0, ((0, 32),), jnp.float32)
    kept_tile = plant(jax.random.randint(key_list[4], (REPS, NCHUNK), 0, (SPAN // TILE) ** 2), jax.random.fold_in(key_list[4], 1), 0, ((SPAN // TILE) ** 2) - 1).astype(jnp.int32)
    return {"activations": activations, "out_grad": out_grad, "momentum": momentum, "weight": weight, "kept_tile": kept_tile}


decay_rate = 0.9
step_size = 0.5
epsilon = 1e-06

def dct_basis():
    freq = jnp.arange(SPAN, dtype=jnp.float32)[:, None]
    place = jnp.arange(SPAN, dtype=jnp.float32)[None, :]
    factor = jnp.where(freq == 0, math.sqrt(1.0 / SPAN), math.sqrt(2.0 / SPAN))
    return factor * jnp.cos(math.pi * (2.0 * place + 1.0) * freq / (2.0 * SPAN))

def selectors(index, blocks):
    per_side = SPAN // TILE
    levels = jnp.arange(per_side, dtype=jnp.int32)
    hot_a = ((index // per_side)[..., None] == levels).astype(jnp.float32)
    hot_b = ((index % per_side)[..., None] == levels).astype(jnp.float32)
    rows_a = jnp.einsum('gka,apu->gkpu', hot_a, blocks, precision=lax.Precision.HIGHEST)
    rows_b = jnp.einsum('gka,apu->gkpu', hot_b, blocks, precision=lax.Precision.HIGHEST)
    return (rows_a, rows_b)

def reference(activations, out_grad, momentum, weight, kept_tile):
    row_blocks = ROWS // SPAN
    col_blocks = D // SPAN
    acts = activations.reshape(N_REP, N_FSDP, TOK_DEV, D)
    grads = out_grad.reshape(N_REP, N_FSDP, TOK_DEV, ROWS)

    def group_sum(pair):

        def add_term(total, piece):
            term = jnp.dot(piece[1].T, piece[0], preferred_element_type=jnp.float32)
            return (total + term, None)
        total, _ = lax.scan(add_term, jnp.zeros((ROWS, D), jnp.float32), (pair[0], pair[1]))
        return total
    summed = lax.map(group_sum, (acts, grads))
    spans = summed.reshape(N_REP, row_blocks, SPAN, col_blocks, SPAN)
    spans = spans.transpose(0, 1, 3, 2, 4).reshape(N_REP, NCHUNK, SPAN, SPAN)
    state = decay_rate * momentum + spans
    basis = dct_basis()
    blocks = basis.reshape(SPAN // TILE, TILE, SPAN)
    rows_a, rows_b = selectors(kept_tile, blocks)
    tiles = jnp.einsum('gkpi,gkij,gkqj->gkpq', rows_a, state, rows_b, precision=lax.Precision.HIGHEST)
    decoded = jnp.einsum('gkpi,gkpq,gkqj->gkij', rows_a, tiles, rows_b, precision=lax.Precision.HIGHEST)
    new_momentum = state - decoded
    update = lax.optimization_barrier(jnp.sum(decoded, axis=0))
    spread = jnp.sqrt(lax.optimization_barrier(jnp.mean(update * update, axis=(1, 2), keepdims=True)) + epsilon)
    new_weight = weight - step_size * update / spread
    return (new_momentum, new_weight)
```

```python
import functools

import jax
import jax.numpy as jnp
import numpy as np
from jax import lax
from jax.experimental import pallas as pl
from jax.experimental.pallas import tpu as pltpu
from jax.sharding import PartitionSpec as P

SPAN = 64
TILE = 8
N_X = 4
N_ZLO = 4
N_REP = 16
SLAB = 160
HALF = SLAB // 2
TOK = 128
COLS = 5120
WIDE = 640
PARITY = 4 * WIDE

decay_rate = 0.9
step_size = 0.5
epsilon = 1e-06

MESH = pl.DeviceIdType.MESH
HI = lax.Precision.HIGHEST


def tables():
    u = np.arange(SPAN, dtype=np.float64)[:, None]
    x = np.arange(SPAN, dtype=np.float64)[None, :]
    s = np.where(u == 0, np.sqrt(1.0 / SPAN), np.sqrt(2.0 / SPAN))
    basis = s * np.cos(np.pi * (2.0 * x + 1.0) * u / (2.0 * SPAN))
    zero = np.zeros((SPAN, SPAN))
    rows = [
        np.concatenate([basis, zero], 1),
        np.concatenate([basis.T, zero], 1),
        np.block([[basis.T, zero], [zero, basis.T]]),
        np.block([[basis, zero], [zero, basis]]),
    ]
    return np.concatenate(rows, 0).astype(np.float32)


def dot32(a, b):
    return jnp.dot(a, b, precision=HI, preferred_element_type=jnp.float32)


def left(table, parts):
    wide = dot32(table, jnp.concatenate(parts, axis=1))
    return [wide[:, 128 * p : 128 * p + 128] for p in range(3)]


def right(parts, table):
    tall = dot32(jnp.concatenate(parts, axis=0), table)
    return [tall[SPAN * p : SPAN * p + SPAN] for p in range(3)]


def kernel(
    acts_h, outg_h, mom_h, wt_h, kept_h, cst_h,
    newm_h, neww_h,
    acts, outg, mom, wt, kept, cst,
    part, rx, x1, x0, x2, zr, every, outm, outw,
    lsem, osem, csend, crecv, xsend, xrecv, zsend, zrecv, gsend, grecv,
):
    rep = lax.axis_index("rep")
    f = lax.axis_index("fsdp")
    core = lax.rem(f, 2)
    x = lax.rem(f // 2, N_X)
    z = f // (2 * N_X)
    other = 1 - core
    xr, xl, xo = lax.rem(x + 1, N_X), lax.rem(x + 3, N_X), lax.rem(x + 2, N_X)

    def at(z_, x_, core_):
        return (rep, (z_ * N_X + x_) * 2 + core_)

    piece = [lax.rem(z + d, N_ZLO) for d in (1, 3, 2)] + [z]

    first = lax.rem(z + 1, 2)
    load_acts = []
    for k in range(2):
        par = first if k == 0 else 1 - first
        cols = pl.ds(pl.multiple_of(par * PARITY, 128), PARITY)
        load_acts.append(pltpu.make_async_copy(acts_h.at[:, cols], acts.at[:, cols], lsem.at[k]))
    load_outg = pltpu.make_async_copy(outg_h, outg, lsem.at[2])
    load_outg.start()
    load_acts[0].start()
    load_acts[1].start()
    small = [
        pltpu.make_async_copy(src, dst, lsem.at[3 + i])
        for i, (src, dst) in enumerate(((mom_h.at[0], mom), (wt_h, wt), (kept_h, kept), (cst_h, cst)))
    ]
    for copy in small:
        copy.start()

    barrier = pltpu.get_barrier_semaphore()
    near = [at(z, x, other), at(z, xr, core), at(z, xl, core)] + [at(piece[k], x, core) for k in range(3)]
    for peer in near:
        pl.semaphore_signal(barrier, inc=1, device_id=peer, device_id_type=MESH)

    def greet(i, carry):
        pl.semaphore_signal(
            barrier, inc=1, device_id=(lax.rem(rep + i, N_REP), f), device_id_type=MESH
        )
        return carry

    lax.fori_loop(1, N_REP, greet, 0)

    lane = lax.broadcasted_iota(jnp.int32, (32, 128), 1)

    def product(par, grads):
        def chunk(j, carry):
            base = pl.multiple_of(par * PARITY + j * WIDE, 128)
            prod = jnp.dot(grads, acts[:, pl.ds(base, WIDE)], preferred_element_type=jnp.float32)
            for h in range(2):
                blk = prod[SPAN * h : SPAN * h + SPAN]
                zz = 2 * h + par
                b2 = blk[:, 256:384]
                part[0, zz, j, 0:64] = blk[:, 0:128]
                part[0, zz, j, 64:128] = blk[:, 128:256]
                part[0, zz, j, 128:160] = jnp.where(lane < 64, b2[0:32], pltpu.roll(b2[32:64], 64, 1))
                part[1, zz, j, 0:64] = blk[:, 384:512]
                part[1, zz, j, 64:128] = blk[:, 512:640]
                part[1, zz, j, 128:160] = jnp.where(lane < 64, pltpu.roll(b2[0:32], 64, 1), b2[32:64])
            return carry

        lax.fori_loop(0, 4, chunk, 0)

    def swap(k):
        return pltpu.make_async_remote_copy(
            src_ref=part.at[other, piece[k]], dst_ref=rx.at[k],
            send_sem=csend.at[k], recv_sem=crecv.at[k],
            device_id=at(z, x, other), device_id_type=MESH,
        )

    A, B = pl.ds(0, HALF), pl.ds(HALF, HALF)

    def hop(k, kind, way):
        side = xr if way == 0 else xl
        slab = xo if kind == 1 else side
        rows = (B if way == 0 else A) if kind == 0 else (A if way == 0 else B)
        land = (x0, x1, x2)[kind]
        i = (k * 3 + kind) * 2 + way
        return pltpu.make_async_remote_copy(
            src_ref=part.at[core, piece[k], slab, rows], dst_ref=land.at[k, way],
            send_sem=xsend.at[i], recv_sem=xrecv.at[i],
            device_id=at(z, side, core), device_id_type=MESH,
        )

    def zhop(k):
        return pltpu.make_async_remote_copy(
            src_ref=part.at[core, piece[k], x], dst_ref=zr.at[k],
            send_sem=zsend.at[k], recv_sem=zrecv.at[k],
            device_id=at(piece[k], x, core), device_id_type=MESH,
        )

    def open_piece(k):
        swap(k).wait_recv()

        def add(j, carry):
            part[core, piece[k], j] = part[core, piece[k], j] + rx[k, j]
            return carry

        lax.fori_loop(0, N_X, add, 0)
        for kind in (1, 0):
            for way in range(2):
                hop(k, kind, way).start()

    def pass_on(k):
        for way in range(2):
            hop(k, 1, way).wait_recv()
            side, rows = (xr, A) if way == 0 else (xl, B)
            part[core, piece[k], side, rows] = part[core, piece[k], side, rows] + x1[k, way]
            hop(k, 2, way).start()

    def close_piece(k):
        for way in range(2):
            hop(k, 0, way).wait_recv()
            hop(k, 2, way).wait_recv()
        part[core, piece[k], x, A] = part[core, piece[k], x, A] + (x0[k, 1] + x2[k, 0])
        part[core, piece[k], x, B] = part[core, piece[k], x, B] + (x0[k, 0] + x2[k, 1])
        if k < 3:
            zhop(k).start()

    load_outg.wait()
    grads = outg[...].astype(jnp.float32).T.astype(jnp.bfloat16)
    load_acts[0].wait()
    product(first, grads)
    pl.semaphore_wait(barrier, len(near) + N_REP - 1)
    swap(0).start()
    swap(1).start()
    load_acts[1].wait()
    product(1 - first, grads)
    swap(2).start()
    swap(3).start()
    open_piece(0)
    open_piece(1)
    pass_on(0)
    open_piece(2)
    pass_on(1)
    close_piece(0)
    open_piece(3)
    pass_on(2)
    close_piece(1)
    pass_on(3)
    close_piece(2)

    for copy in small:
        copy.wait()
    order = [core, core + 1, core + 2, core + 3, 4 * other]
    numbers = [kept[0, s] for s in order]
    wide = lax.broadcasted_iota(jnp.int32, (SPAN, 128), 1)
    row = lax.broadcasted_iota(jnp.int32, (SPAN, 128), 0)
    place = (row // TILE) * TILE + lax.rem(wide, SPAN) // TILE

    def pairs(ref):
        zero = jnp.zeros((SPAN, SPAN), jnp.float32)
        return [
            jnp.concatenate([ref[order[0]], ref[order[1]]], axis=1),
            jnp.concatenate([ref[order[2]], ref[order[3]]], axis=1),
            jnp.concatenate([ref[order[4]], zero], axis=1),
        ]

    def unpair(ref, parts):
        ref[order[0]] = parts[0][:, :SPAN]
        ref[order[1]] = parts[0][:, SPAN:]
        ref[order[2]] = parts[1][:, :SPAN]
        ref[order[3]] = parts[1][:, SPAN:]
        ref[order[4]] = parts[2][:, :SPAN]

    carried = [decay_rate * m for m in pairs(mom)]
    keep = [
        place == jnp.where(wide < SPAN, numbers[2 * p], numbers[min(2 * p + 1, 4)]) for p in range(3)
    ]
    fwd_l, inv_l = cst[0:64, 0:64], cst[64:128, 0:64]
    fwd_r, inv_r = cst[128:256], cst[256:384]

    close_piece(3)
    for k in range(3):
        zhop(k).wait_recv()
    total = part[core, z, x] + (zr[0] + zr[1] + zr[2])
    tail = jnp.concatenate([total[128:160], pltpu.roll(total[128:160], 64, 1)], axis=0)
    state = [
        carried[0] + total[0:64],
        carried[1] + total[64:128],
        carried[2] + jnp.where(wide < SPAN, tail, 0.0),
    ]
    coef = right(left(fwd_l, state), fwd_r)
    kept_coef = [jnp.where(keep[p], coef[p], 0.0) for p in range(3)]

    lane8 = lax.broadcasted_iota(jnp.int32, (TILE, 128), 1)
    message = jnp.zeros((TILE, 128), jnp.float32)
    for j in range(5):
        tile = jnp.sum(kept_coef[j // 2].reshape(8, TILE, 128), axis=0)
        tile = jnp.where((lane8 < SPAN) == (j % 2 == 0), tile, 0.0)
        for shift in (8, 16, 32, 64):
            tile = tile + pltpu.roll(tile, shift, 1)
        message = jnp.where(lane8 // TILE == j, tile, message)
        message = jnp.where(lane8 == 40 + j, numbers[j].astype(jnp.float32), message)
    every[rep] = message

    def post(i):
        return pltpu.make_async_remote_copy(
            src_ref=every.at[rep], dst_ref=every.at[rep],
            send_sem=gsend.at[i], recv_sem=grecv.at[i],
            device_id=(lax.rem(rep + i, N_REP), f), device_id_type=MESH,
        )

    def arrival(i):
        slot = lax.rem(rep + N_REP - i, N_REP)
        return pltpu.make_async_remote_copy(
            src_ref=every.at[rep], dst_ref=every.at[slot],
            send_sem=gsend.at[i], recv_sem=grecv.at[i],
            device_id=(lax.rem(rep + i, N_REP), f), device_id_type=MESH,
        )

    def send_one(i, carry):
        post(i).start()
        return carry

    lax.fori_loop(1, N_REP, send_one, 0)

    decoded = left(inv_l, right(kept_coef, inv_r))
    unpair(outm, [state[p] - decoded[p] for p in range(3)])
    store_m = pltpu.make_async_copy(outm, newm_h.at[0], osem.at[0])
    store_m.start()
    weights = pairs(wt)

    def wait_one(i, carry):
        arrival(i).wait_recv()
        return carry

    lax.fori_loop(1, N_REP, wait_one, 0)

    src_tile = [8 * jnp.where(lane8 < SPAN, 2 * p, min(2 * p + 1, 4)) + lax.rem(lane8, 8) for p in range(3)]
    src_num = [40 + jnp.where(lane8 < SPAN, 2 * p, min(2 * p + 1, 4)) for p in range(3)]
    place_f = place.astype(jnp.float32).reshape(8, TILE, 128)

    def gather_one(g, sums):
        got = every[g]
        new = []
        for p in range(3):
            tile = jnp.take_along_axis(got, src_tile[p], axis=1)
            num = jnp.take_along_axis(got, src_num[p], axis=1)
            new.append(sums[p] + jnp.where(num[None] == place_f, tile[None], 0.0))
        return tuple(new)

    sums = lax.fori_loop(
        0, N_REP, gather_one, tuple(jnp.zeros((8, TILE, 128), jnp.float32) for _ in range(3))
    )
    update = left(inv_l, right([s.reshape(SPAN, 128) for s in sums], inv_r))
    fresh = []
    for p in range(3):
        square = jnp.sum(update[p] * update[p], axis=0, keepdims=True)
        low = wide[0:1] < SPAN
        mean_lo = jnp.sum(jnp.where(low, square, 0.0), axis=1, keepdims=True) / (SPAN * SPAN)
        mean_hi = jnp.sum(jnp.where(low, 0.0, square), axis=1, keepdims=True) / (SPAN * SPAN)
        spread = jnp.sqrt(jnp.where(low, mean_lo, mean_hi) + epsilon)
        fresh.append(weights[p] - step_size * update[p] / spread)
    unpair(outw, fresh)
    store_w = pltpu.make_async_copy(outw, neww_h, osem.at[1])
    store_w.start()

    for k in range(4):
        swap(k).wait_send()
        for kind in range(3):
            for way in range(2):
                hop(k, kind, way).wait_send()
        if k < 3:
            zhop(k).wait_send()

    def sent_one(i, carry):
        post(i).wait_send()
        return carry

    lax.fori_loop(1, N_REP, sent_one, 0)
    store_m.wait()
    store_w.wait()


def shards(activations, out_grad, momentum, weight, kept_tile):
    f32 = jnp.float32
    vm = pltpu.VMEM
    dma = pltpu.SemaphoreType.DMA
    return tuple(
        pl.pallas_call(
            kernel,
            out_shape=(
                jax.ShapeDtypeStruct(momentum.shape, f32),
                jax.ShapeDtypeStruct(weight.shape, f32),
            ),
            in_specs=[pl.BlockSpec(memory_space=pl.ANY)] * 6,
            out_specs=(pl.BlockSpec(memory_space=pl.ANY),) * 2,
            scratch_shapes=[
                vm((TOK, COLS), jnp.bfloat16),
                vm((TOK, TOK), jnp.bfloat16),
                vm((5, SPAN, SPAN), f32),
                vm((5, SPAN, SPAN), f32),
                pltpu.SMEM((1, 5), jnp.int32),
                vm((384, 128), f32),
                vm((2, N_ZLO, N_X, SLAB, 128), f32),
                vm((N_ZLO, N_X, SLAB, 128), f32),
                vm((4, 2, HALF, 128), f32),
                vm((4, 2, HALF, 128), f32),
                vm((4, 2, HALF, 128), f32),
                vm((3, SLAB, 128), f32),
                vm((N_REP, TILE, 128), f32),
                vm((5, SPAN, SPAN), f32),
                vm((5, SPAN, SPAN), f32),
                dma((7,)),
                dma((2,)),
                dma((4,)),
                dma((4,)),
                dma((24,)),
                dma((24,)),
                dma((3,)),
                dma((3,)),
                dma((N_REP,)),
                dma((N_REP,)),
            ],
            compiler_params=pltpu.CompilerParams(
                collective_id=0, has_side_effects=True, vmem_limit_bytes=62 * 1024 * 1024
            ),
            name="demo_step",
        )(activations, out_grad, momentum, weight, kept_tile, jnp.asarray(tables()))
    )


def solution(mesh):
    placed = (
        P(("rep", "fsdp"), None),
        P(("rep", "fsdp"), None),
        P("rep", "fsdp", None, None),
        P("fsdp", None, None),
        P("rep", "fsdp"),
    )
    return jax.shard_map(
        shards,
        mesh=mesh,
        in_specs=placed,
        out_specs=(P("rep", "fsdp", None, None), P("fsdp", None, None)),
        check_vma=False,
    )
```

```python
import jax
import jax.numpy as jnp
import ml_dtypes
import numpy as np
from jax import lax
from jax.experimental import pallas as pl
from jax.experimental.pallas import tpu as pltpu
from jax.sharding import PartitionSpec as P

SPAN = 64
TILE = 8
N_X = 4
N_ZLO = 4
N_REP = 16
SLAB = 160
HALF = SLAB // 2
TOK = 128
COLS = 5120
WIDE = 640
PARITY = 4 * WIDE

decay_rate = 0.9
step_size = 0.5
epsilon = 1e-06

MESH = pl.DeviceIdType.MESH


def tables():
    u = np.arange(SPAN, dtype=np.float64)[:, None]
    x = np.arange(SPAN, dtype=np.float64)[None, :]
    s = np.where(u == 0, np.sqrt(1.0 / SPAN), np.sqrt(2.0 / SPAN))
    basis = s * np.cos(np.pi * (2.0 * x + 1.0) * u / (2.0 * SPAN))
    zero = np.zeros((SPAN, SPAN))

    def halves(table):
        high = table.astype(ml_dtypes.bfloat16)
        return high, (table - high.astype(np.float64)).astype(ml_dtypes.bfloat16)

    def for_left(table):
        high, low = halves(np.concatenate([table, zero], 1))
        high, low = high[:, :SPAN], low[:, :SPAN]
        return np.concatenate([high, high, low, zero.astype(high.dtype)], 1)

    def for_right(table):
        high, low = halves(np.block([[table, zero], [zero, table]]))
        return np.concatenate([high, high, low], 0)

    lefts = np.concatenate([for_left(basis), for_left(basis.T)], 0)
    rights = np.concatenate([for_right(basis.T), for_right(basis)], 0)
    return lefts.astype(np.float32), rights.astype(np.float32)


def halve(a):
    high = a.astype(jnp.bfloat16)
    return high, (a - high.astype(jnp.float32)).astype(jnp.bfloat16)


def left(table, parts):
    high, low = halve(jnp.concatenate(parts, axis=1))
    data = jnp.concatenate([high, low, high], axis=0)
    wide = jnp.dot(table, data, preferred_element_type=jnp.float32)
    return [wide[:, 128 * p : 128 * p + 128] for p in range(3)]


def right(parts, table):
    high, low = halve(jnp.concatenate(parts, axis=0))
    data = jnp.concatenate([high, low, high], axis=1)
    tall = jnp.dot(data, table, preferred_element_type=jnp.float32)
    return [tall[SPAN * p : SPAN * p + SPAN] for p in range(3)]


def kernel(
    acts_h, outg_h, mom_h, wt_h, kept_h, lefts_h, rights_h,
    outm, outw,
    acts, outg, mom, wt, kept, lefts32, rights32, lefts, rights,
    part, rx, x1, x0, x2, zr, every,
    lsem, csend, crecv, xsend, xrecv, zsend, zrecv, gsend, grecv,
):
    rep = lax.axis_index("rep")
    f = lax.axis_index("fsdp")
    core = lax.rem(f, 2)
    x = lax.rem(f // 2, N_X)
    z = f // (2 * N_X)
    other = 1 - core
    xr, xl, xo = lax.rem(x + 1, N_X), lax.rem(x + 3, N_X), lax.rem(x + 2, N_X)

    def at(z_, x_, core_):
        return (rep, (z_ * N_X + x_) * 2 + core_)

    piece = [lax.rem(z + d, N_ZLO) for d in (1, 3, 2)] + [z]

    first = lax.rem(z + 1, 2)
    load_acts = []
    for k in range(2):
        par = first if k == 0 else 1 - first
        cols = pl.ds(pl.multiple_of(par * PARITY, 128), PARITY)
        load_acts.append(pltpu.make_async_copy(acts_h.at[:, cols], acts.at[:, cols], lsem.at[k]))
    load_outg = pltpu.make_async_copy(outg_h, outg, lsem.at[2])
    load_outg.start()
    load_acts[0].start()
    load_acts[1].start()
    small = [
        pltpu.make_async_copy(src, dst, lsem.at[3 + i])
        for i, (src, dst) in enumerate(((mom_h.at[0], mom), (wt_h, wt), (kept_h, kept), (lefts_h, lefts32), (rights_h, rights32)))
    ]
    for copy in small:
        copy.start()

    barrier = pltpu.get_barrier_semaphore()
    near = [at(z, x, other), at(z, xr, core), at(z, xl, core)] + [at(piece[k], x, core) for k in range(3)]
    for peer in near:
        pl.semaphore_signal(barrier, inc=1, device_id=peer, device_id_type=MESH)

    def greet(i, carry):
        pl.semaphore_signal(
            barrier, inc=1, device_id=(lax.rem(rep + i, N_REP), f), device_id_type=MESH
        )
        return carry

    lax.fori_loop(1, N_REP, greet, 0)

    lane = lax.broadcasted_iota(jnp.int32, (32, 128), 1)

    owners = [xo, xr, xl, x]

    def chunk(half, o, grads):
        par, j = (first if half == 0 else 1 - first), owners[o]
        base = pl.multiple_of(par * PARITY + j * WIDE, 128)
        prod = jnp.dot(grads, acts[:, pl.ds(base, WIDE)], preferred_element_type=jnp.float32)
        for h in range(2):
            blk = prod[SPAN * h : SPAN * h + SPAN]
            zz = 2 * h + par
            b2 = blk[:, 256:384]
            part[0, zz, j, 0:64] = blk[:, 0:128]
            part[0, zz, j, 64:128] = blk[:, 128:256]
            part[0, zz, j, 128:160] = jnp.where(lane < 64, b2[0:32], pltpu.roll(b2[32:64], 64, 1))
            part[1, zz, j, 0:64] = blk[:, 384:512]
            part[1, zz, j, 64:128] = blk[:, 512:640]
            part[1, zz, j, 128:160] = jnp.where(lane < 64, pltpu.roll(b2[0:32], 64, 1), b2[32:64])
        for k in (2 * half, 2 * half + 1):
            swap(k, o).start()

    def swap(k, o):
        return pltpu.make_async_remote_copy(
            src_ref=part.at[other, piece[k], owners[o]], dst_ref=rx.at[k, o],
            send_sem=csend.at[4 * k + o], recv_sem=crecv.at[4 * k + o],
            device_id=at(z, x, other), device_id_type=MESH,
        )

    A, B = pl.ds(0, HALF), pl.ds(HALF, HALF)

    def hop(k, kind, way):
        side = xr if way == 0 else xl
        slab = xo if kind == 1 else side
        rows = (B if way == 0 else A) if kind == 0 else (A if way == 0 else B)
        land = (x0, x1, x2)[kind]
        i = (k * 3 + kind) * 2 + way
        return pltpu.make_async_remote_copy(
            src_ref=part.at[core, piece[k], slab, rows], dst_ref=land.at[k, way],
            send_sem=xsend.at[i], recv_sem=xrecv.at[i],
            device_id=at(z, side, core), device_id_type=MESH,
        )

    def zhop(k):
        return pltpu.make_async_remote_copy(
            src_ref=part.at[core, piece[k], x], dst_ref=zr.at[k],
            send_sem=zsend.at[k], recv_sem=zrecv.at[k],
            device_id=at(piece[k], x, core), device_id_type=MESH,
        )

    def take(k, o):
        swap(k, o).wait_recv()
        slab = owners[o]
        part[core, piece[k], slab] = part[core, piece[k], slab] + rx[k, o]

    def open_far(k):
        take(k, 0)
        hop(k, 1, 0).start()
        hop(k, 1, 1).start()

    def open_near(k):
        for way in range(2):
            take(k, 1 + way)
            hop(k, 0, way).start()

    def pass_on(k):
        for way in range(2):
            hop(k, 1, way).wait_recv()
            side, rows = (xr, A) if way == 0 else (xl, B)
            part[core, piece[k], side, rows] = part[core, piece[k], side, rows] + x1[k, way]
            hop(k, 2, way).start()

    def close_piece(k):
        take(k, 3)
        for way in range(2):
            hop(k, 0, way).wait_recv()
            hop(k, 2, way).wait_recv()
        part[core, piece[k], x, A] = part[core, piece[k], x, A] + (x0[k, 1] + x2[k, 0])
        part[core, piece[k], x, B] = part[core, piece[k], x, B] + (x0[k, 0] + x2[k, 1])
        if k < 3:
            zhop(k).start()

    load_outg.wait()
    grads = outg[...].astype(jnp.float32).T.astype(jnp.bfloat16)
    load_acts[0].wait()
    pl.semaphore_wait(barrier, len(near) + N_REP - 1)
    chunk(0, 0, grads)
    chunk(0, 1, grads)
    chunk(0, 2, grads)
    open_far(0)
    open_far(1)
    chunk(0, 3, grads)
    open_near(0)
    open_near(1)
    load_acts[1].wait()
    chunk(1, 0, grads)
    pass_on(0)
    chunk(1, 1, grads)
    chunk(1, 2, grads)
    open_far(2)
    pass_on(1)
    open_far(3)
    chunk(1, 3, grads)
    open_near(2)
    close_piece(0)
    close_piece(1)
    pass_on(2)
    open_near(3)
    pass_on(3)
    close_piece(2)

    for copy in small:
        copy.wait()
    lefts[...] = lefts32[...].astype(jnp.bfloat16)
    rights[...] = rights32[...].astype(jnp.bfloat16)
    order = [core, core + 1, core + 2, core + 3, 4 * other]
    numbers = [kept[0, s] for s in order]
    wide = lax.broadcasted_iota(jnp.int32, (SPAN, 128), 1)
    row = lax.broadcasted_iota(jnp.int32, (SPAN, 128), 0)
    place = (row // TILE) * TILE + lax.rem(wide, SPAN) // TILE

    def pairs(ref):
        zero = jnp.zeros((SPAN, SPAN), jnp.float32)
        return [
            jnp.concatenate([ref[order[0]], ref[order[1]]], axis=1),
            jnp.concatenate([ref[order[2]], ref[order[3]]], axis=1),
            jnp.concatenate([ref[order[4]], zero], axis=1),
        ]

    def unpair(ref, parts):
        for j in range(5):
            half = parts[j // 2][:, SPAN * (j % 2) : SPAN * (j % 2) + SPAN]
            ref[order[j]] = half

    carried = [decay_rate * m for m in pairs(mom)]
    keep = [
        place == jnp.where(wide < SPAN, numbers[2 * p], numbers[min(2 * p + 1, 4)]) for p in range(3)
    ]
    fwd_l, inv_l = lefts[0:64, 0:192], lefts[64:128, 0:192]
    fwd_r, inv_r = rights[0:384], rights[384:768]

    close_piece(3)
    for k in range(3):
        zhop(k).wait_recv()
    total = part[core, z, x] + (zr[0] + zr[1] + zr[2])
    tail = jnp.concatenate([total[128:160], pltpu.roll(total[128:160], 64, 1)], axis=0)
    state = [
        carried[0] + total[0:64],
        carried[1] + total[64:128],
        carried[2] + jnp.where(wide < SPAN, tail, 0.0),
    ]
    coef = right(left(fwd_l, state), fwd_r)
    kept_coef = [jnp.where(keep[p], coef[p], 0.0) for p in range(3)]

    lane8 = lax.broadcasted_iota(jnp.int32, (TILE, 128), 1)
    message = jnp.zeros((TILE, 128), jnp.float32)
    for j in range(5):
        tile = jnp.sum(kept_coef[j // 2].reshape(8, TILE, 128), axis=0)
        tile = jnp.where((lane8 < SPAN) == (j % 2 == 0), tile, 0.0)
        for shift in (8, 16, 32, 64):
            tile = tile + pltpu.roll(tile, shift, 1)
        message = jnp.where(lax.rem(lane8, SPAN) // TILE == j, tile, message)
        message = jnp.where(lax.rem(lane8, SPAN) == 40 + j, numbers[j].astype(jnp.float32), message)
    every[rep] = jnp.where(lane8[0:4] < SPAN, message[0:4], message[4:8])

    def post(i):
        return pltpu.make_async_remote_copy(
            src_ref=every.at[rep], dst_ref=every.at[rep],
            send_sem=gsend, recv_sem=grecv,
            device_id=(lax.rem(rep + i, N_REP), f), device_id_type=MESH,
        )

    def all_posts():
        span = pl.ds(0, N_REP - 1)
        return pltpu.make_async_remote_copy(
            src_ref=every.at[span], dst_ref=every.at[span], send_sem=gsend, recv_sem=grecv,
            device_id=(lax.rem(rep + 1, N_REP), f), device_id_type=MESH,
        )

    def send_one(i, carry):
        post(i).start()
        return carry

    lax.fori_loop(1, N_REP, send_one, 0)

    decoded = left(inv_l, right(kept_coef, inv_r))
    unpair(outm.at[0], [state[p] - decoded[p] for p in range(3)])
    weights = pairs(wt)

    for k in range(4):
        for o in range(4):
            swap(k, o).wait_send()
        for kind in range(3):
            for way in range(2):
                hop(k, kind, way).wait_send()
        if k < 3:
            zhop(k).wait_send()
    all_posts().wait_send()
    all_posts().wait_recv()

    src_tile = [8 * jnp.where(lane8 < SPAN, 2 * p, min(2 * p + 1, 4)) + lax.rem(lane8, 8) for p in range(3)]
    src_num = [40 + jnp.where(lane8 < SPAN, 2 * p, min(2 * p + 1, 4)) for p in range(3)]
    place_f = place.astype(jnp.float32).reshape(8, TILE, 128)

    def gather_one(g, sums):
        got = every[g]
        got = jnp.concatenate([got, pltpu.roll(got, SPAN, 1)], axis=0)
        new = []
        for p in range(3):
            tile = jnp.take_along_axis(got, src_tile[p], axis=1)
            num = jnp.take_along_axis(got, src_num[p], axis=1)
            new.append(sums[p] + jnp.where(num[None] == place_f, tile[None], 0.0))
        return tuple(new)

    sums = lax.fori_loop(
        0, N_REP, gather_one, tuple(jnp.zeros((8, TILE, 128), jnp.float32) for _ in range(3)),
        unroll=True,
    )
    update = left(inv_l, right([s.reshape(SPAN, 128) for s in sums], inv_r))
    fresh = []
    for p in range(3):
        square = jnp.sum(update[p] * update[p], axis=0, keepdims=True)
        low = wide[0:1] < SPAN
        mean_lo = jnp.sum(jnp.where(low, square, 0.0), axis=1, keepdims=True) / (SPAN * SPAN)
        mean_hi = jnp.sum(jnp.where(low, 0.0, square), axis=1, keepdims=True) / (SPAN * SPAN)
        spread = jnp.sqrt(jnp.where(low, mean_lo, mean_hi) + epsilon)
        fresh.append(weights[p] - step_size * update[p] / spread)
    unpair(outw, fresh)


def shards(activations, out_grad, momentum, weight, kept_tile):
    f32 = jnp.float32
    vm = pltpu.VMEM
    dma = pltpu.SemaphoreType.DMA
    return tuple(
        pl.pallas_call(
            kernel,
            out_shape=(
                pltpu.VMEM(momentum.shape, f32),
                pltpu.VMEM(weight.shape, f32),
            ),
            in_specs=[pl.BlockSpec(memory_space=pltpu.HBM)] * 7,
            out_specs=(pl.BlockSpec(memory_space=pltpu.VMEM),) * 2,
            scratch_shapes=[
                vm((TOK, COLS), jnp.bfloat16),
                vm((TOK, TOK), jnp.bfloat16),
                vm((5, SPAN, SPAN), f32),
                vm((5, SPAN, SPAN), f32),
                pltpu.SMEM((1, 5), jnp.int32),
                vm((128, 256), f32),
                vm((768, 128), f32),
                vm((128, 256), jnp.bfloat16),
                vm((768, 128), jnp.bfloat16),
                vm((2, N_ZLO, N_X, SLAB, 128), f32),
                vm((N_ZLO, N_X, SLAB, 128), f32),
                vm((4, 2, HALF, 128), f32),
                vm((4, 2, HALF, 128), f32),
                vm((4, 2, HALF, 128), f32),
                vm((3, SLAB, 128), f32),
                vm((N_REP, TILE // 2, 128), f32),
                dma((8,)),
                dma((16,)),
                dma((16,)),
                dma((24,)),
                dma((24,)),
                dma((3,)),
                dma((3,)),
                dma,
                dma,
            ],
            compiler_params=pltpu.CompilerParams(
                collective_id=0, has_side_effects=True, vmem_limit_bytes=48 * 1024 * 1024
            ),
            name="demo_step",
        )(*(
            pltpu.with_memory_space_constraint(a, pltpu.HBM)
            for a in (activations, out_grad, momentum, weight, kept_tile, *map(jnp.asarray, tables()))
        ))
    )


def solution(mesh):
    placed = (
        P(("rep", "fsdp"), None),
        P(("rep", "fsdp"), None),
        P("rep", "fsdp", None, None),
        P("fsdp", None, None),
        P("rep", "fsdp"),
    )
    return jax.shard_map(
        shards,
        mesh=mesh,
        in_specs=placed,
        out_specs=(P("rep", "fsdp", None, None), P("fsdp", None, None)),
        check_vma=False,
    )
```

```python
import jax
import jax.numpy as jnp
import ml_dtypes
import numpy as np
from jax import lax
from jax.experimental import pallas as pl
from jax.experimental.pallas import tpu as pltpu
from jax.sharding import PartitionSpec as P

SPAN = 64
TILE = 8
N_X = 4
N_ZLO = 4
N_REP = 16
N_FSDP = 32
SLAB = 160
HALF = SLAB // 2
TOK = 128
COLS = 5120
WIDE = 640
PARITY = 4 * WIDE

decay_rate = 0.9
step_size = 0.5
epsilon = 1e-06

MESH = pl.DeviceIdType.MESH


def tables():
    u = np.arange(SPAN, dtype=np.float64)[:, None]
    x = np.arange(SPAN, dtype=np.float64)[None, :]
    s = np.where(u == 0, np.sqrt(1.0 / SPAN), np.sqrt(2.0 / SPAN))
    basis = s * np.cos(np.pi * (2.0 * x + 1.0) * u / (2.0 * SPAN))
    zero = np.zeros((SPAN, SPAN))

    def halves(table):
        high = table.astype(ml_dtypes.bfloat16)
        return high, (table - high.astype(np.float64)).astype(ml_dtypes.bfloat16)

    def for_left(table):
        high, low = halves(np.concatenate([table, zero], 1))
        high, low = high[:, :SPAN], low[:, :SPAN]
        return np.concatenate([high, high, low, zero.astype(high.dtype)], 1)

    def for_right(table):
        high, low = halves(np.block([[table, zero], [zero, table]]))
        return np.concatenate([high, high, low], 0)

    lefts = np.concatenate([for_left(basis), for_left(basis.T)], 0)
    rights = np.concatenate([for_right(basis.T), for_right(basis)], 0)
    return lefts.astype(np.float32), rights.astype(np.float32)


def halve(a):
    high = a.astype(jnp.bfloat16)
    return high, (a - high.astype(jnp.float32)).astype(jnp.bfloat16)


def left(table, parts):
    high, low = halve(jnp.concatenate(parts, axis=1))
    data = jnp.concatenate([high, low, high], axis=0)
    wide = jnp.dot(table, data, preferred_element_type=jnp.float32)
    return [wide[:, 128 * p : 128 * p + 128] for p in range(3)]


def right(parts, table):
    high, low = halve(jnp.concatenate(parts, axis=0))
    data = jnp.concatenate([high, low, high], axis=1)
    tall = jnp.dot(data, table, preferred_element_type=jnp.float32)
    return [tall[SPAN * p : SPAN * p + SPAN] for p in range(3)]


def kernel(
    acts_h, outg_h, mom_h, wt_h, kept_h, lefts_h, rights_h,
    outm, outw,
    acts, outg, mom, wt, kept, lefts32, rights32, lefts, rights,
    part, rx, x1, x0, x2, zr, turned, names, tmsg, tin, every,
    lsem, csend, crecv, xsend, xrecv, zsend, zrecv, nsend, nrecv, tsend, trecv, gsend, grecv,
):
    rep = lax.axis_index("rep")
    f = lax.axis_index("fsdp")
    core = lax.rem(f, 2)
    x = lax.rem(f // 2, N_X)
    z = f // (2 * N_X)
    other = 1 - core
    xr, xl, xo = lax.rem(x + 1, N_X), lax.rem(x + 3, N_X), lax.rem(x + 2, N_X)

    def at(z_, x_, core_):
        return (rep, (z_ * N_X + x_) * 2 + core_)

    piece = [lax.rem(z + d, N_ZLO) for d in (1, 3, 2)] + [z]

    first = lax.rem(z + 1, 2)
    load_acts = []
    for k in range(2):
        par = first if k == 0 else 1 - first
        cols = pl.ds(pl.multiple_of(par * PARITY, 128), PARITY)
        load_acts.append(pltpu.make_async_copy(acts_h.at[:, cols], acts.at[:, cols], lsem.at[k]))
    load_outg = pltpu.make_async_copy(outg_h, outg, lsem.at[2])
    load_outg.start()
    load_acts[0].start()
    load_acts[1].start()
    small = [
        pltpu.make_async_copy(src, dst, lsem.at[3 + i])
        for i, (src, dst) in enumerate(((mom_h.at[0], mom), (wt_h, wt), (kept_h, kept), (lefts_h, lefts32), (rights_h, rights32)))
    ]
    for copy in small:
        copy.start()

    barrier = pltpu.get_barrier_semaphore()

    def greet_group(i, carry):
        pl.semaphore_signal(
            barrier, inc=1, device_id=(rep, lax.rem(f + i, N_FSDP)), device_id_type=MESH
        )
        return carry

    def greet_peers(i, carry):
        pl.semaphore_signal(
            barrier, inc=1, device_id=(lax.rem(rep + i, N_REP), f), device_id_type=MESH
        )
        return carry

    lax.fori_loop(1, N_FSDP, greet_group, 0)
    lax.fori_loop(1, N_REP, greet_peers, 0)

    lane = lax.broadcasted_iota(jnp.int32, (32, 128), 1)

    owners = [xo, xr, xl, x]

    def chunk(half, o, grads):
        par, j = (first if half == 0 else 1 - first), owners[o]
        base = pl.multiple_of(par * PARITY + j * WIDE, 128)
        prod = jnp.dot(grads, acts[:, pl.ds(base, WIDE)], preferred_element_type=jnp.float32)
        for h in range(2):
            blk = prod[SPAN * h : SPAN * h + SPAN]
            zz = 2 * h + par
            b2 = blk[:, 256:384]
            part[0, zz, j, 0:64] = blk[:, 0:128]
            part[0, zz, j, 64:128] = blk[:, 128:256]
            part[0, zz, j, 128:160] = jnp.where(lane < 64, b2[0:32], pltpu.roll(b2[32:64], 64, 1))
            part[1, zz, j, 0:64] = blk[:, 384:512]
            part[1, zz, j, 64:128] = blk[:, 512:640]
            part[1, zz, j, 128:160] = jnp.where(lane < 64, pltpu.roll(b2[0:32], 64, 1), b2[32:64])
        for k in (2 * half, 2 * half + 1):
            swap(k, o).start()

    def swap(k, o):
        return pltpu.make_async_remote_copy(
            src_ref=part.at[other, piece[k], owners[o]], dst_ref=rx.at[k, o],
            send_sem=csend.at[4 * k + o], recv_sem=crecv.at[4 * k + o],
            device_id=at(z, x, other), device_id_type=MESH,
        )

    A, B = pl.ds(0, HALF), pl.ds(HALF, HALF)

    def hop(k, kind, way):
        side = xr if way == 0 else xl
        slab = xo if kind == 1 else side
        rows = (B if way == 0 else A) if kind == 0 else (A if way == 0 else B)
        land = (x0, x1, x2)[kind]
        i = (k * 3 + kind) * 2 + way
        return pltpu.make_async_remote_copy(
            src_ref=part.at[core, piece[k], slab, rows], dst_ref=land.at[k, way],
            send_sem=xsend.at[i], recv_sem=xrecv.at[i],
            device_id=at(z, side, core), device_id_type=MESH,
        )

    def zhop(k):
        return pltpu.make_async_remote_copy(
            src_ref=part.at[core, piece[k], x], dst_ref=zr.at[k],
            send_sem=zsend.at[k], recv_sem=zrecv.at[k],
            device_id=at(piece[k], x, core), device_id_type=MESH,
        )

    def take(k, o):
        swap(k, o).wait_recv()
        slab = owners[o]
        part[core, piece[k], slab] = part[core, piece[k], slab] + rx[k, o]

    def open_far(k):
        take(k, 0)
        hop(k, 1, 0).start()
        hop(k, 1, 1).start()

    def open_near(k):
        for way in range(2):
            take(k, 1 + way)
            hop(k, 0, way).start()

    def pass_on(k):
        for way in range(2):
            hop(k, 1, way).wait_recv()
            side, rows = (xr, A) if way == 0 else (xl, B)
            part[core, piece[k], side, rows] = part[core, piece[k], side, rows] + x1[k, way]
            hop(k, 2, way).start()

    def close_piece(k):
        take(k, 3)
        for way in range(2):
            hop(k, 0, way).wait_recv()
            hop(k, 2, way).wait_recv()
        part[core, piece[k], x, A] = part[core, piece[k], x, A] + (x0[k, 1] + x2[k, 0])
        part[core, piece[k], x, B] = part[core, piece[k], x, B] + (x0[k, 0] + x2[k, 1])
        if k < 3:
            zhop(k).start()

    order = [core, core + 1, core + 2, core + 3, 4 * other]
    lane1 = lax.broadcasted_iota(jnp.int32, (1, 128), 1)
    lane4 = lax.broadcasted_iota(jnp.int32, (4, 128), 1)
    lane8 = lax.broadcasted_iota(jnp.int32, (TILE, 128), 1)
    wide = lax.broadcasted_iota(jnp.int32, (SPAN, 128), 1)
    row = lax.broadcasted_iota(jnp.int32, (SPAN, 128), 0)
    place = (row // TILE) * TILE + lax.rem(wide, SPAN) // TILE
    upper = jnp.where(lane8 < SPAN, 0, SPAN)
    block = lax.rem(lane8, SPAN) // TILE

    def to_group(src, dst, send, recv, i):
        return pltpu.make_async_remote_copy(
            src_ref=src, dst_ref=dst, send_sem=send, recv_sem=recv,
            device_id=(rep, lax.rem(f + i, N_FSDP)), device_id_type=MESH,
        )

    def to_peer(src, dst, send, recv, i):
        return pltpu.make_async_remote_copy(
            src_ref=src, dst_ref=dst, send_sem=send, recv_sem=recv,
            device_id=(lax.rem(rep + i, N_REP), f), device_id_type=MESH,
        )

    def send_names():
        mine = jnp.zeros((1, 128), jnp.int32)
        for s in range(5):
            mine = jnp.where(lane1 == s, kept[0, s], mine)
        names[f] = mine

        def one(i, carry):
            to_group(names.at[f], names.at[f], nsend, nrecv, i).start()
            return carry

        lax.fori_loop(1, N_FSDP, one, 0)

    def all_names():
        ref = names.at[pl.ds(0, N_FSDP - 1)]
        return to_group(ref, ref, nsend, nrecv, 1)

    def pick_columns(tile, number):
        source = (number & 7) * TILE + lax.rem(lane8, TILE) + upper
        return jnp.take_along_axis(tile, source, axis=1)

    def merge(a, b, c):
        return jnp.where(block == 0, a, jnp.where(block == 1, b, c))

    def pack(tiles):
        return jnp.where(lax.rem(lane4, SPAN) < 24, tiles[0:4], pltpu.roll(tiles[4:8], 24, 1))

    def unpack(four):
        return jnp.concatenate([four, pltpu.roll(four, 104, 1)], axis=0)

    def group_tiles(m, carry):
        base = pl.multiple_of(m * WIDE, 128)
        both = jnp.dot(turned[...], acts[:, pl.ds(base, WIDE)], preferred_element_type=jnp.float32)
        both = both[0:128] + both[128:256]
        numbers, rows = [], []
        for h in range(2):
            owner = ((2 * h + m // 4) * N_X + lax.rem(m, 4)) * 2
            low = jnp.broadcast_to(names[owner], (TILE, 128))
            high = jnp.broadcast_to(names[owner + 1], (TILE, 128))
            ten = jnp.where(lane8 < 5, low, pltpu.roll(high, 5, 1))
            for p in range(5):
                number = jnp.take_along_axis(ten, jnp.where(lane8 < SPAN, 2 * p, 2 * p + 1), axis=1)
                high_part = number >> 3
                found = jnp.zeros((TILE, 128), jnp.float32)
                for a in range(8):
                    at_row = SPAN * h + TILE * a
                    found = found + jnp.where(
                        high_part == a, both[at_row : at_row + TILE, 128 * p : 128 * p + 128], 0.0
                    )
                numbers.append(number)
                rows.append(found)
        high, low = halve(jnp.concatenate(rows, axis=0))
        data = jnp.concatenate([high, low, high], axis=1)
        turned_rows = jnp.dot(data, rights[0:384], preferred_element_type=jnp.float32)
        for h in range(2):
            owner = ((2 * h + m // 4) * N_X + lax.rem(m, 4)) * 2
            t = [
                pick_columns(turned_rows[TILE * q : TILE * q + TILE], numbers[q])
                for q in range(5 * h, 5 * h + 5)
            ]
            tmsg[owner] = pack(merge(t[0], t[1], t[2]))
            tmsg[owner + 1] = pack(merge(t[3], t[4], pltpu.roll(t[2], SPAN, 1)))
        return carry

    def send_tiles():
        tin[f] = tmsg[f]

        def one(i, carry):
            to_group(tmsg.at[lax.rem(f + i, N_FSDP)], tin.at[f], tsend, trecv, i).start()
            return carry

        lax.fori_loop(1, N_FSDP, one, 0)

    def all_tiles():
        span = pl.ds(0, N_FSDP - 1)
        return to_group(tmsg.at[span], tin.at[span], tsend, trecv, 1)

    def pairs(ref):
        zero = jnp.zeros((SPAN, SPAN), jnp.float32)
        return [
            jnp.concatenate([ref[order[0]], ref[order[1]]], axis=1),
            jnp.concatenate([ref[order[2]], ref[order[3]]], axis=1),
            jnp.concatenate([ref[order[4]], zero], axis=1),
        ]

    def unpair(ref, parts):
        for j in range(5):
            half = parts[j // 2][:, SPAN * (j % 2) : SPAN * (j % 2) + SPAN]
            ref[order[j]] = half

    load_outg.wait()
    flat = outg[...]
    grads = flat.astype(jnp.float32).T.astype(jnp.bfloat16)
    load_acts[0].wait()
    pl.semaphore_wait(barrier, N_FSDP - 1 + N_REP - 1)
    chunk(0, 0, grads)
    chunk(0, 1, grads)
    chunk(0, 2, grads)
    open_far(0)
    open_far(1)
    chunk(0, 3, grads)
    open_near(0)
    open_near(1)
    for copy in small:
        copy.wait()
    send_names()
    load_acts[1].wait()
    chunk(1, 0, grads)
    pass_on(0)
    chunk(1, 1, grads)
    chunk(1, 2, grads)
    open_far(2)
    pass_on(1)
    open_far(3)
    chunk(1, 3, grads)
    open_near(2)

    lefts[...] = lefts32[...].astype(jnp.bfloat16)
    rights[...] = rights32[...].astype(jnp.bfloat16)
    fwd_l, inv_l = lefts[0:64, 0:192], lefts[64:128, 0:192]
    fwd_r, inv_r = rights[0:384], rights[384:768]
    spun = jnp.dot(flat, rights[0:128], preferred_element_type=jnp.float32)
    spun = spun + jnp.dot(flat, rights[256:384], preferred_element_type=jnp.float32)
    spun_high, spun_low = halve(spun.T)
    turned[0:128] = spun_high
    turned[128:256] = spun_low
    open_near(3)
    all_names().wait_recv()
    lax.fori_loop(0, 4, group_tiles, 0)
    close_piece(0)
    pass_on(2)
    lax.fori_loop(4, 8, group_tiles, 0)
    pass_on(3)
    close_piece(1)
    send_tiles()

    scalars = [kept[0, s] for s in order]
    carried = [decay_rate * m for m in pairs(mom)]
    own = [
        jnp.where(wide < SPAN, scalars[2 * p], scalars[min(2 * p + 1, 4)]) for p in range(3)
    ]
    coef = right(left(fwd_l, carried), fwd_r)
    found = [
        pick_columns(
            jnp.sum(jnp.where(place == own[p], coef[p], 0.0).reshape(8, TILE, 128), axis=0), own[p][0:8]
        )
        for p in range(3)
    ]
    from_momentum = merge(*found)
    close_piece(2)

    all_tiles().wait_recv()
    tiles = from_momentum + unpack(jnp.sum(tin[...], axis=0))
    message = pack(tiles)
    for j in range(5):
        spot = (lane4 == 56 + j) | (lane4 == 80 + j)
        message = jnp.where(spot, scalars[j].astype(jnp.float32), message)
    every[rep] = message

    def send_one(i, carry):
        to_peer(every.at[rep], every.at[rep], gsend, grecv, i).start()
        return carry

    lax.fori_loop(1, N_REP, send_one, 0)

    def all_posts():
        ref = every.at[pl.ds(0, N_REP - 1)]
        return to_peer(ref, ref, gsend, grecv, 1)

    src_tile = [upper + TILE * p + lax.rem(lane8, TILE) for p in range(3)]
    src_num = [56 + jnp.where(lane8 < SPAN, 2 * p, min(2 * p + 1, 4)) for p in range(3)]

    def spread_out(p):
        tile = jnp.take_along_axis(tiles, src_tile[p], axis=1)
        tall = jnp.broadcast_to(tile[None], (8, TILE, 128)).reshape(SPAN, 128)
        return jnp.where(place == own[p], tall, 0.0)

    decoded = left(inv_l, right([spread_out(p) for p in range(3)], inv_r))
    for p in range(3):
        carried[p] = carried[p] - decoded[p]
    weights = pairs(wt)
    for k in range(4):
        for o in range(4):
            swap(k, o).wait_send()
    all_names().wait_send()
    all_tiles().wait_send()
    all_posts().wait_send()
    all_posts().wait_recv()

    place_f = place.astype(jnp.float32).reshape(8, TILE, 128)

    def gather_one(g, sums):
        got = unpack(every[g])
        new = []
        for p in range(3):
            tile = jnp.take_along_axis(got, src_tile[p], axis=1)
            num = jnp.take_along_axis(got, src_num[p], axis=1)
            new.append(sums[p] + jnp.where(num[None] == place_f, tile[None], 0.0))
        return tuple(new)

    sums = lax.fori_loop(
        0, N_REP, gather_one, tuple(jnp.zeros((8, TILE, 128), jnp.float32) for _ in range(3)),
        unroll=True,
    )
    update = left(inv_l, right([s.reshape(SPAN, 128) for s in sums], inv_r))
    fresh = []
    for p in range(3):
        square = jnp.sum(update[p] * update[p], axis=0, keepdims=True)
        low = wide[0:1] < SPAN
        mean_lo = jnp.sum(jnp.where(low, square, 0.0), axis=1, keepdims=True) / (SPAN * SPAN)
        mean_hi = jnp.sum(jnp.where(low, 0.0, square), axis=1, keepdims=True) / (SPAN * SPAN)
        spread = jnp.sqrt(jnp.where(low, mean_lo, mean_hi) + epsilon)
        fresh.append(weights[p] - step_size * update[p] / spread)
    unpair(outw, fresh)

    close_piece(3)
    for k in range(4):
        for kind in range(3):
            for way in range(2):
                hop(k, kind, way).wait_send()
        if k < 3:
            zhop(k).wait_send()
    for k in range(3):
        zhop(k).wait_recv()
    total = part[core, z, x] + (zr[0] + zr[1] + zr[2])
    tail = jnp.concatenate([total[128:160], pltpu.roll(total[128:160], 64, 1)], axis=0)
    unpair(outm.at[0], [carried[0] + total[0:64], carried[1] + total[64:128], carried[2] + tail])


def shards(activations, out_grad, momentum, weight, kept_tile):
    f32 = jnp.float32
    vm = pltpu.VMEM
    dma = pltpu.SemaphoreType.DMA
    return tuple(
        pl.pallas_call(
            kernel,
            out_shape=(
                pltpu.VMEM(momentum.shape, f32),
                pltpu.VMEM(weight.shape, f32),
            ),
            in_specs=[pl.BlockSpec(memory_space=pltpu.HBM)] * 7,
            out_specs=(pl.BlockSpec(memory_space=pltpu.VMEM),) * 2,
            scratch_shapes=[
                vm((TOK, COLS), jnp.bfloat16),
                vm((TOK, TOK), jnp.bfloat16),
                vm((5, SPAN, SPAN), f32),
                vm((5, SPAN, SPAN), f32),
                pltpu.SMEM((1, 5), jnp.int32),
                vm((128, 256), f32),
                vm((768, 128), f32),
                vm((128, 256), jnp.bfloat16),
                vm((768, 128), jnp.bfloat16),
                vm((2, N_ZLO, N_X, SLAB, 128), f32),
                vm((N_ZLO, N_X, SLAB, 128), f32),
                vm((4, 2, HALF, 128), f32),
                vm((4, 2, HALF, 128), f32),
                vm((4, 2, HALF, 128), f32),
                vm((3, SLAB, 128), f32),
                vm((2 * TOK, TOK), jnp.bfloat16),
                vm((N_FSDP, 1, 128), jnp.int32),
                vm((N_FSDP, TILE // 2, 128), f32),
                vm((N_FSDP, TILE // 2, 128), f32),
                vm((N_REP, TILE // 2, 128), f32),
                dma((8,)),
                dma((16,)),
                dma((16,)),
                dma((24,)),
                dma((24,)),
                dma((3,)),
                dma((3,)),
                dma,
                dma,
                dma,
                dma,
                dma,
                dma,
            ],
            compiler_params=pltpu.CompilerParams(
                collective_id=0, has_side_effects=True, vmem_limit_bytes=48 * 1024 * 1024
            ),
            name="demo_step",
        )(*(
            pltpu.with_memory_space_constraint(a, pltpu.HBM)
            for a in (activations, out_grad, momentum, weight, kept_tile, *map(jnp.asarray, tables()))
        ))
    )


def solution(mesh):
    placed = (
        P(("rep", "fsdp"), None),
        P(("rep", "fsdp"), None),
        P("rep", "fsdp", None, None),
        P("fsdp", None, None),
        P("rep", "fsdp"),
    )
    return jax.shard_map(
        shards,
        mesh=mesh,
        in_specs=placed,
        out_specs=(P("rep", "fsdp", None, None), P("fsdp", None, None)),
        check_vma=False,
    )
```

```python
import jax
import jax.numpy as jnp
import ml_dtypes
import numpy as np
from jax import lax
from jax.experimental import pallas as pl
from jax.experimental.pallas import tpu as pltpu
from jax.sharding import PartitionSpec as P

SPAN = 64
TILE = 8
N_X = 4
N_ZLO = 4
N_REP = 16
N_FSDP = 32
SLAB = 160
HALF = SLAB // 2
TOK = 128
COLS = 5120
WIDE = 640
PARITY = 4 * WIDE

decay_rate = 0.9
step_size = 0.5
epsilon = 1e-06

MESH = pl.DeviceIdType.MESH


def tables():
    u = np.arange(SPAN, dtype=np.float64)[:, None]
    x = np.arange(SPAN, dtype=np.float64)[None, :]
    s = np.where(u == 0, np.sqrt(1.0 / SPAN), np.sqrt(2.0 / SPAN))
    basis = s * np.cos(np.pi * (2.0 * x + 1.0) * u / (2.0 * SPAN))
    zero = np.zeros((SPAN, SPAN))

    def halves(table):
        high = table.astype(ml_dtypes.bfloat16)
        return high, (table - high.astype(np.float64)).astype(ml_dtypes.bfloat16)

    def for_left(table):
        high, low = halves(np.concatenate([table, zero], 1))
        high, low = high[:, :SPAN], low[:, :SPAN]
        return np.concatenate([high, high, low, zero.astype(high.dtype)], 1)

    def for_right(table):
        high, low = halves(np.block([[table, zero], [zero, table]]))
        return np.concatenate([high, high, low], 0)

    lefts = np.concatenate([for_left(basis), for_left(basis.T)], 0)
    rights = np.concatenate([for_right(basis.T), for_right(basis)], 0)
    return lefts.astype(np.float32), rights.astype(np.float32)


def halve(a):
    high = a.astype(jnp.bfloat16)
    return high, (a - high.astype(jnp.float32)).astype(jnp.bfloat16)


def left(table, parts):
    high, low = halve(jnp.concatenate(parts, axis=1))
    data = jnp.concatenate([high, low, high], axis=0)
    wide = jnp.dot(table, data, preferred_element_type=jnp.float32)
    return [wide[:, 128 * p : 128 * p + 128] for p in range(3)]


def right(parts, table):
    high, low = halve(jnp.concatenate(parts, axis=0))
    data = jnp.concatenate([high, low, high], axis=1)
    tall = jnp.dot(data, table, preferred_element_type=jnp.float32)
    return [tall[SPAN * p : SPAN * p + SPAN] for p in range(3)]


def wrap(i, n):
    return jnp.where(i >= n, i - n, i)


def kernel(
    acts_h, outg_h, mom_h, wt_h, kept_h, lefts_h, rights_h,
    outm, outw,
    acts, outg, mom, wt, kept, lefts32, rights32, lefts, rights,
    part, rx, x1, x0, x2, zr, turned, names, tmsg, tin, every,
    lsem, csend, crecv, xsend, xrecv, zsend, zrecv, nsend, nrecv, tsend, trecv, gsend, grecv,
):
    rep = lax.axis_index("rep")
    f = lax.axis_index("fsdp")
    core = lax.rem(f, 2)
    x = lax.rem(f // 2, N_X)
    z = f // (2 * N_X)
    other = 1 - core
    xr, xl, xo = lax.rem(x + 1, N_X), lax.rem(x + 3, N_X), lax.rem(x + 2, N_X)

    def at(z_, x_, core_):
        return (rep, (z_ * N_X + x_) * 2 + core_)

    piece = [lax.rem(z + d, N_ZLO) for d in (1, 3, 2)] + [z]

    first = lax.rem(z + 1, 2)
    load_acts = []
    for k in range(2):
        par = first if k == 0 else 1 - first
        cols = pl.ds(pl.multiple_of(par * PARITY, 128), PARITY)
        load_acts.append(pltpu.make_async_copy(acts_h.at[:, cols], acts.at[:, cols], lsem.at[k]))
    load_outg = pltpu.make_async_copy(outg_h, outg, lsem.at[2])
    load_outg.start()
    load_acts[0].start()
    load_acts[1].start()
    small = [
        pltpu.make_async_copy(src, dst, lsem.at[3 + i])
        for i, (src, dst) in enumerate(((mom_h.at[0], mom), (wt_h, wt), (kept_h, kept), (lefts_h, lefts32), (rights_h, rights32)))
    ]
    for copy in small:
        copy.start()

    barrier = pltpu.get_barrier_semaphore()

    def greet_group(i, carry):
        pl.semaphore_signal(
            barrier, inc=1, device_id=(rep, wrap(f + i, N_FSDP)), device_id_type=MESH
        )
        return carry

    def greet_peers(i, carry):
        pl.semaphore_signal(
            barrier, inc=1, device_id=(wrap(rep + i, N_REP), f), device_id_type=MESH
        )
        return carry

    lax.fori_loop(1, N_FSDP, greet_group, 0)
    lax.fori_loop(1, N_REP, greet_peers, 0)

    lane = lax.broadcasted_iota(jnp.int32, (32, 128), 1)

    owners = [xo, xr, xl, x]

    def chunk(half, o, grads):
        par, j = (first if half == 0 else 1 - first), owners[o]
        base = pl.multiple_of(par * PARITY + j * WIDE, 128)
        prod = jnp.dot(grads, acts[:, pl.ds(base, WIDE)], preferred_element_type=jnp.float32)
        for h in range(2):
            blk = prod[SPAN * h : SPAN * h + SPAN]
            zz = 2 * h + par
            b2 = blk[:, 256:384]
            part[0, zz, j, 0:64] = blk[:, 0:128]
            part[0, zz, j, 64:128] = blk[:, 128:256]
            part[0, zz, j, 128:160] = jnp.where(lane < 64, b2[0:32], pltpu.roll(b2[32:64], 64, 1))
            part[1, zz, j, 0:64] = blk[:, 384:512]
            part[1, zz, j, 64:128] = blk[:, 512:640]
            part[1, zz, j, 128:160] = jnp.where(lane < 64, pltpu.roll(b2[0:32], 64, 1), b2[32:64])
        for k in (2 * half, 2 * half + 1):
            swap(k, o).start()

    def swap(k, o):
        return pltpu.make_async_remote_copy(
            src_ref=part.at[other, piece[k], owners[o]], dst_ref=rx.at[k, o],
            send_sem=csend.at[4 * k + o], recv_sem=crecv.at[4 * k + o],
            device_id=at(z, x, other), device_id_type=MESH,
        )

    A, B = pl.ds(0, HALF), pl.ds(HALF, HALF)

    def hop(k, kind, way):
        side = xr if way == 0 else xl
        slab = xo if kind == 1 else side
        rows = (B if way == 0 else A) if kind == 0 else (A if way == 0 else B)
        land = (x0, x1, x2)[kind]
        i = (k * 3 + kind) * 2 + way
        return pltpu.make_async_remote_copy(
            src_ref=part.at[core, piece[k], slab, rows], dst_ref=land.at[k, way],
            send_sem=xsend.at[i], recv_sem=xrecv.at[i],
            device_id=at(z, side, core), device_id_type=MESH,
        )

    def zhop(k):
        return pltpu.make_async_remote_copy(
            src_ref=part.at[core, piece[k], x], dst_ref=zr.at[k],
            send_sem=zsend.at[k], recv_sem=zrecv.at[k],
            device_id=at(piece[k], x, core), device_id_type=MESH,
        )

    def take(k, o):
        swap(k, o).wait_recv()
        slab = owners[o]
        part[core, piece[k], slab] = part[core, piece[k], slab] + rx[k, o]

    def open_far(k):
        take(k, 0)
        hop(k, 1, 0).start()
        hop(k, 1, 1).start()

    def open_near(k):
        for way in range(2):
            take(k, 1 + way)
            hop(k, 0, way).start()

    def pass_on(k):
        for way in range(2):
            hop(k, 1, way).wait_recv()
            side, rows = (xr, A) if way == 0 else (xl, B)
            part[core, piece[k], side, rows] = part[core, piece[k], side, rows] + x1[k, way]
            hop(k, 2, way).start()

    def close_piece(k):
        take(k, 3)
        for way in range(2):
            hop(k, 0, way).wait_recv()
            hop(k, 2, way).wait_recv()
        part[core, piece[k], x, A] = part[core, piece[k], x, A] + (x0[k, 1] + x2[k, 0])
        part[core, piece[k], x, B] = part[core, piece[k], x, B] + (x0[k, 0] + x2[k, 1])
        if k < 3:
            zhop(k).start()

    order = [core, core + 1, core + 2, core + 3, 4 * other]
    lane1 = lax.broadcasted_iota(jnp.int32, (1, 128), 1)
    lane4 = lax.broadcasted_iota(jnp.int32, (4, 128), 1)
    lane8 = lax.broadcasted_iota(jnp.int32, (TILE, 128), 1)
    wide = lax.broadcasted_iota(jnp.int32, (SPAN, 128), 1)
    row = lax.broadcasted_iota(jnp.int32, (SPAN, 128), 0)
    place = (row // TILE) * TILE + lax.rem(wide, SPAN) // TILE
    upper = jnp.where(lane8 < SPAN, 0, SPAN)
    block = lax.rem(lane8, SPAN) // TILE

    def to_group(src, dst, send, recv, i):
        return pltpu.make_async_remote_copy(
            src_ref=src, dst_ref=dst, send_sem=send, recv_sem=recv,
            device_id=(rep, wrap(f + i, N_FSDP)), device_id_type=MESH,
        )

    def to_peer(src, dst, send, recv, i):
        return pltpu.make_async_remote_copy(
            src_ref=src, dst_ref=dst, send_sem=send, recv_sem=recv,
            device_id=(wrap(rep + i, N_REP), f), device_id_type=MESH,
        )

    def send_names():
        mine = jnp.zeros((1, 128), jnp.int32)
        for s in range(5):
            mine = jnp.where(lane1 == s, kept[0, s], mine)
        names[f] = mine

        def one(i, carry):
            to_group(names.at[f], names.at[f], nsend, nrecv, i).start()
            return carry

        lax.fori_loop(1, N_FSDP, one, 0)

    def all_names():
        ref = names.at[pl.ds(0, N_FSDP - 1)]
        return to_group(ref, ref, nsend, nrecv, 1)

    def pick_columns(tile, number):
        source = (number & 7) * TILE + lax.rem(lane8, TILE) + upper
        return jnp.take_along_axis(tile, source, axis=1)

    def merge(a, b, c):
        return jnp.where(block == 0, a, jnp.where(block == 1, b, c))

    def pack(tiles):
        return jnp.where(lax.rem(lane4, SPAN) < 24, tiles[0:4], pltpu.roll(tiles[4:8], 24, 1))

    def unpack(four):
        return jnp.concatenate([four, pltpu.roll(four, 104, 1)], axis=0)

    def group_tiles(m, carry):
        base = pl.multiple_of(m * WIDE, 128)
        both = jnp.dot(turned[...], acts[:, pl.ds(base, WIDE)], preferred_element_type=jnp.float32)
        both = both[0:128] + both[128:256]
        numbers, rows = [], []
        for h in range(2):
            owner = ((2 * h + m // 4) * N_X + lax.rem(m, 4)) * 2
            low = jnp.broadcast_to(names[owner], (TILE, 128))
            high = jnp.broadcast_to(names[owner + 1], (TILE, 128))
            ten = jnp.where(lane8 < 5, low, pltpu.roll(high, 5, 1))
            for p in range(5):
                number = jnp.take_along_axis(ten, jnp.where(lane8 < SPAN, 2 * p, 2 * p + 1), axis=1)
                high_part = number >> 3
                found = jnp.zeros((TILE, 128), jnp.float32)
                for a in range(8):
                    at_row = SPAN * h + TILE * a
                    found = found + jnp.where(
                        high_part == a, both[at_row : at_row + TILE, 128 * p : 128 * p + 128], 0.0
                    )
                numbers.append(number)
                rows.append(found)
        high, low = halve(jnp.concatenate(rows, axis=0))
        data = jnp.concatenate([high, low, high], axis=1)
        turned_rows = jnp.dot(data, rights[0:384], preferred_element_type=jnp.float32)
        for h in range(2):
            owner = ((2 * h + m // 4) * N_X + lax.rem(m, 4)) * 2
            t = [
                pick_columns(turned_rows[TILE * q : TILE * q + TILE], numbers[q])
                for q in range(5 * h, 5 * h + 5)
            ]
            tmsg[owner] = pack(merge(t[0], t[1], t[2]))
            tmsg[owner + 1] = pack(merge(t[3], t[4], pltpu.roll(t[2], SPAN, 1)))
        return carry

    def two_chunks(i, carry):
        group_tiles(2 * i, carry)
        return group_tiles(2 * i + 1, carry)

    def send_tiles():
        tin[f] = tmsg[f]

        def one(i, carry):
            to_group(tmsg.at[wrap(f + i, N_FSDP)], tin.at[f], tsend, trecv, i).start()
            return carry

        lax.fori_loop(1, N_FSDP, one, 0)

    def all_tiles():
        span = pl.ds(0, N_FSDP - 1)
        return to_group(tmsg.at[span], tin.at[span], tsend, trecv, 1)

    def pairs(ref):
        zero = jnp.zeros((SPAN, SPAN), jnp.float32)
        return [
            jnp.concatenate([ref[order[0]], ref[order[1]]], axis=1),
            jnp.concatenate([ref[order[2]], ref[order[3]]], axis=1),
            jnp.concatenate([ref[order[4]], zero], axis=1),
        ]

    def unpair(ref, parts):
        for j in range(5):
            half = parts[j // 2][:, SPAN * (j % 2) : SPAN * (j % 2) + SPAN]
            ref[order[j]] = half

    load_outg.wait()
    flat = outg[...]
    grads = flat.astype(jnp.float32).T.astype(jnp.bfloat16)
    load_acts[0].wait()
    pl.semaphore_wait(barrier, N_FSDP - 1 + N_REP - 1)
    chunk(0, 0, grads)
    chunk(0, 1, grads)
    chunk(0, 2, grads)
    open_far(0)
    open_far(1)
    chunk(0, 3, grads)
    open_near(0)
    open_near(1)
    for copy in small:
        copy.wait()
    send_names()
    load_acts[1].wait()
    chunk(1, 0, grads)
    pass_on(0)
    chunk(1, 1, grads)
    chunk(1, 2, grads)
    open_far(2)
    pass_on(1)
    open_far(3)
    chunk(1, 3, grads)
    open_near(2)

    lefts[...] = lefts32[...].astype(jnp.bfloat16)
    rights[...] = rights32[...].astype(jnp.bfloat16)
    fwd_l, inv_l = lefts[0:64, 0:192], lefts[64:128, 0:192]
    fwd_r, inv_r = rights[0:384], rights[384:768]
    spun = jnp.dot(flat, rights[0:128], preferred_element_type=jnp.float32)
    spun = spun + jnp.dot(flat, rights[256:384], preferred_element_type=jnp.float32)
    spun_high, spun_low = halve(spun.T)
    turned[0:128] = spun_high
    turned[128:256] = spun_low
    open_near(3)
    all_names().wait_recv()
    lax.fori_loop(0, 2, two_chunks, 0)
    pass_on(2)
    lax.fori_loop(2, 4, two_chunks, 0)
    send_tiles()
    pass_on(3)
    close_piece(0)

    scalars = [kept[0, s] for s in order]
    carried = [decay_rate * m for m in pairs(mom)]
    own = [
        jnp.where(wide < SPAN, scalars[2 * p], scalars[min(2 * p + 1, 4)]) for p in range(3)
    ]
    coef = right(left(fwd_l, carried), fwd_r)
    found = [
        pick_columns(
            jnp.sum(jnp.where(place == own[p], coef[p], 0.0).reshape(8, TILE, 128), axis=0), own[p][0:8]
        )
        for p in range(3)
    ]
    from_momentum = merge(*found)

    all_tiles().wait_recv()
    tiles = from_momentum + unpack(jnp.sum(tin[...], axis=0))
    message = pack(tiles)
    for j in range(5):
        spot = (lane4 == 56 + j) | (lane4 == 80 + j)
        message = jnp.where(spot, scalars[j].astype(jnp.float32), message)
    every[rep] = message

    def send_one(i, carry):
        to_peer(every.at[rep], every.at[rep], gsend, grecv, i).start()
        return carry

    lax.fori_loop(1, N_REP, send_one, 0)

    def all_posts():
        ref = every.at[pl.ds(0, N_REP - 1)]
        return to_peer(ref, ref, gsend, grecv, 1)

    close_piece(1)
    close_piece(2)
    src_tile = [upper + TILE * p + lax.rem(lane8, TILE) for p in range(3)]
    src_num = [56 + jnp.where(lane8 < SPAN, 2 * p, min(2 * p + 1, 4)) for p in range(3)]

    def spread_out(p):
        tile = jnp.take_along_axis(tiles, src_tile[p], axis=1)
        tall = jnp.broadcast_to(tile[None], (8, TILE, 128)).reshape(SPAN, 128)
        return jnp.where(place == own[p], tall, 0.0)

    decoded = left(inv_l, right([spread_out(p) for p in range(3)], inv_r))
    for p in range(3):
        carried[p] = carried[p] - decoded[p]
    weights = pairs(wt)
    for k in range(4):
        for o in range(4):
            swap(k, o).wait_send()
    all_names().wait_send()
    all_tiles().wait_send()
    all_posts().wait_send()
    all_posts().wait_recv()

    place_f = place.astype(jnp.float32).reshape(8, TILE, 128)

    def gather_one(g, sums):
        got = unpack(every[g])
        new = []
        for p in range(3):
            tile = jnp.take_along_axis(got, src_tile[p], axis=1)
            num = jnp.take_along_axis(got, src_num[p], axis=1)
            new.append(sums[p] + jnp.where(num[None] == place_f, tile[None], 0.0))
        return tuple(new)

    sums = lax.fori_loop(
        0, N_REP, gather_one, tuple(jnp.zeros((8, TILE, 128), jnp.float32) for _ in range(3)),
        unroll=True,
    )
    update = left(inv_l, right([s.reshape(SPAN, 128) for s in sums], inv_r))
    fresh = []
    for p in range(3):
        square = jnp.sum(update[p] * update[p], axis=0, keepdims=True)
        low = wide[0:1] < SPAN
        mean_lo = jnp.sum(jnp.where(low, square, 0.0), axis=1, keepdims=True) / (SPAN * SPAN)
        mean_hi = jnp.sum(jnp.where(low, 0.0, square), axis=1, keepdims=True) / (SPAN * SPAN)
        spread = jnp.sqrt(jnp.where(low, mean_lo, mean_hi) + epsilon)
        fresh.append(weights[p] - step_size * update[p] / spread)
    unpair(outw, fresh)

    close_piece(3)
    for k in range(4):
        for kind in range(3):
            for way in range(2):
                hop(k, kind, way).wait_send()
        if k < 3:
            zhop(k).wait_send()
    for k in range(3):
        zhop(k).wait_recv()
    total = part[core, z, x] + (zr[0] + zr[1] + zr[2])
    tail = jnp.concatenate([total[128:160], pltpu.roll(total[128:160], 64, 1)], axis=0)
    unpair(outm.at[0], [carried[0] + total[0:64], carried[1] + total[64:128], carried[2] + tail])


def shards(activations, out_grad, momentum, weight, kept_tile):
    f32 = jnp.float32
    vm = pltpu.VMEM
    dma = pltpu.SemaphoreType.DMA
    return tuple(
        pl.pallas_call(
            kernel,
            out_shape=(
                pltpu.VMEM(momentum.shape, f32),
                pltpu.VMEM(weight.shape, f32),
            ),
            in_specs=[pl.BlockSpec(memory_space=pltpu.HBM)] * 7,
            out_specs=(pl.BlockSpec(memory_space=pltpu.VMEM),) * 2,
            scratch_shapes=[
                vm((TOK, COLS), jnp.bfloat16),
                vm((TOK, TOK), jnp.bfloat16),
                vm((5, SPAN, SPAN), f32),
                vm((5, SPAN, SPAN), f32),
                pltpu.SMEM((1, 5), jnp.int32),
                vm((128, 256), f32),
                vm((768, 128), f32),
                vm((128, 256), jnp.bfloat16),
                vm((768, 128), jnp.bfloat16),
                vm((2, N_ZLO, N_X, SLAB, 128), f32),
                vm((N_ZLO, N_X, SLAB, 128), f32),
                vm((4, 2, HALF, 128), f32),
                vm((4, 2, HALF, 128), f32),
                vm((4, 2, HALF, 128), f32),
                vm((3, SLAB, 128), f32),
                vm((2 * TOK, TOK), jnp.bfloat16),
                vm((N_FSDP, 1, 128), jnp.int32),
                vm((N_FSDP, TILE // 2, 128), f32),
                vm((N_FSDP, TILE // 2, 128), f32),
                vm((N_REP, TILE // 2, 128), f32),
                dma((8,)),
                dma((16,)),
                dma((16,)),
                dma((24,)),
                dma((24,)),
                dma((3,)),
                dma((3,)),
                dma,
                dma,
                dma,
                dma,
                dma,
                dma,
            ],
            compiler_params=pltpu.CompilerParams(
                collective_id=0, has_side_effects=True, vmem_limit_bytes=48 * 1024 * 1024
            ),
            name="demo_step",
        )(*(
            pltpu.with_memory_space_constraint(a, pltpu.HBM)
            for a in (activations, out_grad, momentum, weight, kept_tile, *map(jnp.asarray, tables()))
        ))
    )


def solution(mesh):
    placed = (
        P(("rep", "fsdp"), None),
        P(("rep", "fsdp"), None),
        P("rep", "fsdp", None, None),
        P("fsdp", None, None),
        P("rep", "fsdp"),
    )
    return jax.shard_map(
        shards,
        mesh=mesh,
        in_specs=placed,
        out_specs=(P("rep", "fsdp", None, None), P("fsdp", None, None)),
        check_vma=False,
    )
```

```python
import jax
import jax.numpy as jnp
import ml_dtypes
import numpy as np
from jax import lax
from jax.experimental import pallas as pl
from jax.experimental.pallas import tpu as pltpu
from jax.sharding import PartitionSpec as P

SPAN = 64
TILE = 8
N_X = 4
N_ZLO = 4
N_REP = 16
N_FSDP = 32
SLAB = 160
HALF = SLAB // 2
TOK = 128
COLS = 5120
WIDE = 640
PARITY = 4 * WIDE

decay_rate = 0.9
step_size = 0.5
epsilon = 1e-06

MESH = pl.DeviceIdType.MESH


def tables():
    u = np.arange(SPAN, dtype=np.float64)[:, None]
    x = np.arange(SPAN, dtype=np.float64)[None, :]
    s = np.where(u == 0, np.sqrt(1.0 / SPAN), np.sqrt(2.0 / SPAN))
    basis = s * np.cos(np.pi * (2.0 * x + 1.0) * u / (2.0 * SPAN))
    zero = np.zeros((SPAN, SPAN))

    def halves(table):
        high = table.astype(ml_dtypes.bfloat16)
        return high, (table - high.astype(np.float64)).astype(ml_dtypes.bfloat16)

    def for_left(table):
        high, low = halves(np.concatenate([table, zero], 1))
        high, low = high[:, :SPAN], low[:, :SPAN]
        return np.concatenate([high, high, low, zero.astype(high.dtype)], 1)

    def for_right(table):
        high, low = halves(np.block([[table, zero], [zero, table]]))
        return np.block([[high, low], [high, np.zeros_like(low)]])

    lefts = np.concatenate([for_left(basis), for_left(basis.T)], 0)
    rights = np.concatenate([for_right(basis.T), for_right(basis)], 0)
    return lefts.astype(np.float32), rights.astype(np.float32)


def halve(a):
    high = a.astype(jnp.bfloat16)
    return high, (a - high.astype(jnp.float32)).astype(jnp.bfloat16)


def left(table, parts):
    high, low = halve(jnp.concatenate(parts, axis=1))
    data = jnp.concatenate([high, low, high], axis=0)
    wide = jnp.dot(table, data, preferred_element_type=jnp.float32)
    return [wide[:, 128 * p : 128 * p + 128] for p in range(3)]


def right(parts, table):
    high, low = halve(jnp.concatenate(parts, axis=0))
    tall = jnp.dot(jnp.concatenate([high, low], axis=1), table, preferred_element_type=jnp.float32)
    tall = tall[:, :128] + tall[:, 128:]
    return [tall[SPAN * p : SPAN * p + SPAN] for p in range(3)]


def wrap(i, n):
    return jnp.where(i >= n, i - n, i)


def kernel(
    acts_h, outg_h, mom_h, wt_h, kept_h, lefts_h, rights_h,
    outm, outw,
    acts, outg, mom, wt, kept, lefts32, rights32, lefts, rights,
    part, rx, x1, x0, x2, zr, turned, names, tmsg, tin, every,
    lsem, csend, crecv, xsend, xrecv, zsend, zrecv, nsend, nrecv, tsend, trecv, gsend, grecv, told,
):
    rep = lax.axis_index("rep")
    f = lax.axis_index("fsdp")
    core = lax.rem(f, 2)
    x = lax.rem(f // 2, N_X)
    z = f // (2 * N_X)
    other = 1 - core
    xr, xl, xo = lax.rem(x + 1, N_X), lax.rem(x + 3, N_X), lax.rem(x + 2, N_X)

    def at(z_, x_, core_):
        return (rep, (z_ * N_X + x_) * 2 + core_)

    piece = [lax.rem(z + d, N_ZLO) for d in (1, 3, 2)] + [z]

    first = lax.rem(z + 1, 2)
    load_acts = []
    for k in range(2):
        par = first if k == 0 else 1 - first
        cols = pl.ds(pl.multiple_of(par * PARITY, 128), PARITY)
        load_acts.append(pltpu.make_async_copy(acts_h.at[:, cols], acts.at[:, cols], lsem.at[k]))
    load_outg = pltpu.make_async_copy(outg_h, outg, lsem.at[2])
    load_outg.start()
    load_acts[0].start()
    load_acts[1].start()
    small = [
        pltpu.make_async_copy(src, dst, lsem.at[3 + i])
        for i, (src, dst) in enumerate(((mom_h.at[0], mom), (wt_h, wt), (kept_h, kept), (lefts_h, lefts32), (rights_h, rights32)))
    ]
    for copy in small:
        copy.start()

    barrier = pltpu.get_barrier_semaphore()

    def greet_group(i, carry):
        pl.semaphore_signal(
            barrier, inc=1, device_id=(rep, wrap(f - core + 2 * i, N_FSDP)), device_id_type=MESH
        )
        return carry

    def greet_peers(i, carry):
        pl.semaphore_signal(
            barrier, inc=1, device_id=(wrap(rep + i, N_REP), f), device_id_type=MESH
        )
        return carry

    lax.fori_loop(1 - core, N_FSDP // 2, greet_group, 0)

    lane = lax.broadcasted_iota(jnp.int32, (32, 128), 1)

    owners = [xo, xr, xl, x]

    def chunk(half, o, grads):
        par, j = (first if half == 0 else 1 - first), owners[o]
        base = pl.multiple_of(par * PARITY + j * WIDE, 128)
        prod = jnp.dot(grads, acts[:, pl.ds(base, WIDE)], preferred_element_type=jnp.float32)
        for h in range(2):
            blk = prod[SPAN * h : SPAN * h + SPAN]
            zz = 2 * h + par
            b2 = blk[:, 256:384]
            part[0, zz, j, 0:64] = blk[:, 0:128]
            part[0, zz, j, 64:128] = blk[:, 128:256]
            part[0, zz, j, 128:160] = jnp.where(lane < 64, b2[0:32], pltpu.roll(b2[32:64], 64, 1))
            part[1, zz, j, 0:64] = blk[:, 384:512]
            part[1, zz, j, 64:128] = blk[:, 512:640]
            part[1, zz, j, 128:160] = jnp.where(lane < 64, pltpu.roll(b2[0:32], 64, 1), b2[32:64])
        for k in (2 * half, 2 * half + 1):
            swap(k, o).start()

    def swap(k, o):
        return pltpu.make_async_remote_copy(
            src_ref=part.at[other, piece[k], owners[o]], dst_ref=rx.at[k, o],
            send_sem=csend.at[4 * k + o], recv_sem=crecv.at[4 * k + o],
            device_id=at(z, x, other), device_id_type=MESH,
        )

    A, B = pl.ds(0, HALF), pl.ds(HALF, HALF)

    def hop(k, kind, way):
        side = xr if way == 0 else xl
        slab = xo if kind == 1 else side
        rows = (B if way == 0 else A) if kind == 0 else (A if way == 0 else B)
        land = (x0, x1, x2)[kind]
        i = (k * 3 + kind) * 2 + way
        return pltpu.make_async_remote_copy(
            src_ref=part.at[core, piece[k], slab, rows], dst_ref=land.at[k, way],
            send_sem=xsend.at[i], recv_sem=xrecv.at[i],
            device_id=at(z, side, core), device_id_type=MESH,
        )

    def zhop(k):
        return pltpu.make_async_remote_copy(
            src_ref=part.at[core, piece[k], x], dst_ref=zr.at[k],
            send_sem=zsend.at[k], recv_sem=zrecv.at[k],
            device_id=at(piece[k], x, core), device_id_type=MESH,
        )

    def take(k, o):
        swap(k, o).wait_recv()
        slab = owners[o]
        part[core, piece[k], slab] = part[core, piece[k], slab] + rx[k, o]

    def open_far(k):
        take(k, 0)
        hop(k, 1, 0).start()
        hop(k, 1, 1).start()

    def open_near(k):
        for way in range(2):
            take(k, 1 + way)
            hop(k, 0, way).start()

    def pass_on(k):
        for way in range(2):
            hop(k, 1, way).wait_recv()
            side, rows = (xr, A) if way == 0 else (xl, B)
            part[core, piece[k], side, rows] = part[core, piece[k], side, rows] + x1[k, way]
            hop(k, 2, way).start()

    def close_piece(k):
        take(k, 3)
        for way in range(2):
            hop(k, 0, way).wait_recv()
            hop(k, 2, way).wait_recv()
        part[core, piece[k], x, A] = part[core, piece[k], x, A] + (x0[k, 1] + x2[k, 0])
        part[core, piece[k], x, B] = part[core, piece[k], x, B] + (x0[k, 0] + x2[k, 1])
        if k < 3:
            zhop(k).start()

    order = [core, core + 1, core + 2, core + 3, 4 * other]
    lane1 = lax.broadcasted_iota(jnp.int32, (1, 128), 1)
    lane4 = lax.broadcasted_iota(jnp.int32, (4, 128), 1)
    lane8 = lax.broadcasted_iota(jnp.int32, (TILE, 128), 1)
    wide = lax.broadcasted_iota(jnp.int32, (SPAN, 128), 1)
    row = lax.broadcasted_iota(jnp.int32, (SPAN, 128), 0)
    place = (row // TILE) * TILE + lax.rem(wide, SPAN) // TILE
    upper = jnp.where(lane8 < SPAN, 0, SPAN)
    block = lax.rem(lane8, SPAN) // TILE

    def to_group(src, dst, send, recv, i):
        return pltpu.make_async_remote_copy(
            src_ref=src, dst_ref=dst, send_sem=send, recv_sem=recv,
            device_id=(rep, wrap(f + i, N_FSDP)), device_id_type=MESH,
        )

    def to_peer(src, dst, send, recv, i):
        return pltpu.make_async_remote_copy(
            src_ref=src, dst_ref=dst, send_sem=send, recv_sem=recv,
            device_id=(wrap(rep + i, N_REP), f), device_id_type=MESH,
        )

    def send_names():
        mine = jnp.zeros((1, 128), jnp.int32)
        for s in range(5):
            mine = jnp.where(lane1 == s, kept[0, s], mine)
        names[f] = mine

        def one(i, carry):
            to_group(names.at[f], names.at[f], nsend, nrecv, i).start()
            return carry

        lax.fori_loop(1, N_FSDP, one, 0)

    def all_names():
        ref = names.at[pl.ds(0, N_FSDP - 1)]
        return to_group(ref, ref, nsend, nrecv, 1)

    def pick_columns(tile, number):
        source = (number & 7) * TILE + lax.rem(lane8, TILE) + upper
        return jnp.take_along_axis(tile, source, axis=1)

    def merge(a, b, c):
        return jnp.where(block == 0, a, jnp.where(block == 1, b, c))

    def pack(tiles):
        return jnp.where(lax.rem(lane4, SPAN) < 24, tiles[0:4], pltpu.roll(tiles[4:8], 24, 1))

    def unpack(four):
        return jnp.concatenate([four, pltpu.roll(four, 104, 1)], axis=0)

    def two_chunks(i, carry):
        numbers, rows = [], []
        for c in range(2):
            m = 2 * i + c
            piece_acts = acts[:, pl.ds(pl.multiple_of(m * WIDE, 128), WIDE)]
            both = jnp.dot(
                turned[...], jnp.concatenate([piece_acts, piece_acts], axis=0),
                preferred_element_type=jnp.float32,
            )
            for h in range(2):
                owner = ((2 * h + m // 4) * N_X + lax.rem(m, 4)) * 2
                low = jnp.broadcast_to(names[owner], (TILE, 128))
                high = jnp.broadcast_to(names[owner + 1], (TILE, 128))
                ten = jnp.where(lane8 < 5, low, pltpu.roll(high, 5, 1))
                for p in range(5):
                    number = jnp.take_along_axis(ten, 2 * p + jnp.where(lane8 < SPAN, 0, 1), axis=1)
                    high_part = number >> 3
                    found = both[SPAN * h : SPAN * h + TILE, 128 * p : 128 * p + 128]
                    for a in range(1, 8):
                        at_row = SPAN * h + TILE * a
                        found = jnp.where(
                            high_part == a, both[at_row : at_row + TILE, 128 * p : 128 * p + 128], found
                        )
                    numbers.append(number)
                    rows.append(found)
        high, low = halve(jnp.concatenate(rows, axis=0))
        out = jnp.dot(
            jnp.concatenate([high, low], axis=1), rights[0:256], preferred_element_type=jnp.float32
        )
        out = out[:, :128] + out[:, 128:]
        for c in range(2):
            m = 2 * i + c
            for h in range(2):
                owner = ((2 * h + m // 4) * N_X + lax.rem(m, 4)) * 2
                base = 10 * c + 5 * h
                t = [
                    pick_columns(out[TILE * q : TILE * q + TILE], numbers[q])
                    for q in range(base, base + 5)
                ]
                tmsg[owner] = pack(merge(t[0], t[1], t[2]))
                tmsg[owner + 1] = pack(merge(t[3], t[4], pltpu.roll(t[2], SPAN, 1)))
        return carry

    def send_tiles():
        tin[f] = tmsg[f]

        def one(i, carry):
            to_group(tmsg.at[wrap(f + i, N_FSDP)], tin.at[f], tsend, trecv, i).start()
            return carry

        lax.fori_loop(1, N_FSDP, one, 0)

    def all_tiles():
        span = pl.ds(0, N_FSDP - 1)
        return to_group(tmsg.at[span], tin.at[span], tsend, trecv, 1)

    def pairs(ref):
        zero = jnp.zeros((SPAN, SPAN), jnp.float32)
        return [
            jnp.concatenate([ref[order[0]], ref[order[1]]], axis=1),
            jnp.concatenate([ref[order[2]], ref[order[3]]], axis=1),
            jnp.concatenate([ref[order[4]], zero], axis=1),
        ]

    def unpair(ref, parts):
        for j in range(5):
            half = parts[j // 2][:, SPAN * (j % 2) : SPAN * (j % 2) + SPAN]
            ref[order[j]] = half

    load_outg.wait()
    flat = outg[...]
    grads = flat.astype(jnp.float32).T.astype(jnp.bfloat16)
    for copy in small:
        copy.wait()
    lefts[...] = lefts32[...].astype(jnp.bfloat16)
    rights[...] = rights32[...].astype(jnp.bfloat16)
    fwd_l, inv_l = lefts[0:64, 0:192], lefts[64:128, 0:192]
    fwd_r, inv_r = rights[0:256], rights[256:512]
    spun = jnp.dot(flat, rights[0:128], preferred_element_type=jnp.float32)
    spun_high, spun_low = halve((spun[:, :128] + spun[:, 128:]).T)
    turned[:, :128] = spun_high
    turned[:, 128:] = spun_low
    load_acts[0].wait()
    sibling = (rep, f + 1 - 2 * core)

    @pl.when(core == 0)
    def _():
        pl.semaphore_wait(barrier, N_FSDP - 1)
        pl.semaphore_signal(told, inc=1, device_id=sibling, device_id_type=MESH)

    @pl.when(core == 1)
    def _():
        pl.semaphore_wait(told, 1)
        lax.fori_loop(1, N_REP, greet_peers, 0)

    send_names()
    for o in range(3):
        chunk(0, o, grads)
    open_far(0)
    open_far(1)
    chunk(0, 3, grads)
    open_near(0)
    open_near(1)
    load_acts[1].wait()
    all_names().wait_recv()
    lax.fori_loop(0, 4, two_chunks, 0)
    send_tiles()
    for o in range(4):
        chunk(1, o, grads)

    scalars = [kept[0, s] for s in order]
    carried = [decay_rate * m for m in pairs(mom)]
    own = [
        jnp.where(wide < SPAN, scalars[2 * p], scalars[min(2 * p + 1, 4)]) for p in range(3)
    ]
    coef = right(left(fwd_l, carried), fwd_r)
    found = [
        pick_columns(
            jnp.sum(jnp.where(place == own[p], coef[p], 0.0).reshape(8, TILE, 128), axis=0), own[p][0:8]
        )
        for p in range(3)
    ]
    from_momentum = merge(*found)
    open_far(2)
    open_far(3)
    open_near(2)
    open_near(3)

    @pl.when(core == 1)
    def _():
        pl.semaphore_wait(barrier, N_REP - 1)
        pl.semaphore_signal(told, inc=1, device_id=sibling, device_id_type=MESH)

    @pl.when(core == 0)
    def _():
        pl.semaphore_wait(told, 1)

    all_tiles().wait_recv()
    tiles = from_momentum + unpack(jnp.sum(tin[...], axis=0))
    message = pack(tiles)
    for j in range(5):
        spot = (lane4 == 56 + j) | (lane4 == 80 + j)
        message = jnp.where(spot, scalars[j].astype(jnp.float32), message)
    every[rep] = message

    def send_one(i, carry):
        to_peer(every.at[rep], every.at[rep], gsend, grecv, i).start()
        return carry

    lax.fori_loop(1, N_REP, send_one, 0)

    def all_posts():
        ref = every.at[pl.ds(0, N_REP - 1)]
        return to_peer(ref, ref, gsend, grecv, 1)

    pass_on(0)
    pass_on(1)
    pass_on(2)
    close_piece(0)
    pass_on(3)
    close_piece(1)
    close_piece(2)
    src_tile = [upper + TILE * p + lax.rem(lane8, TILE) for p in range(3)]
    src_num = [56 + jnp.where(lane8 < SPAN, 2 * p, min(2 * p + 1, 4)) for p in range(3)]

    def spread_out(p):
        tile = jnp.take_along_axis(tiles, src_tile[p], axis=1)
        tall = jnp.broadcast_to(tile[None], (8, TILE, 128)).reshape(SPAN, 128)
        return jnp.where(place == own[p], tall, 0.0)

    decoded = left(inv_l, right([spread_out(p) for p in range(3)], inv_r))
    for p in range(3):
        carried[p] = carried[p] - decoded[p]
    weights = pairs(wt)
    close_piece(3)
    total = part[core, z, x]
    tail = jnp.concatenate([total[128:160], pltpu.roll(total[128:160], 64, 1)], axis=0)
    for p, grown in enumerate((total[0:64], total[64:128], tail)):
        carried[p] = carried[p] + grown
    for k in range(4):
        for o in range(4):
            swap(k, o).wait_send()
        for kind in range(3):
            for way in range(2):
                hop(k, kind, way).wait_send()
    for k in range(3):
        zhop(k).wait()
    rest = zr[0] + zr[1] + zr[2]
    tail = jnp.concatenate([rest[128:160], pltpu.roll(rest[128:160], 64, 1)], axis=0)
    unpair(outm.at[0], [carried[0] + rest[0:64], carried[1] + rest[64:128], carried[2] + tail])
    all_names().wait_send()
    all_tiles().wait_send()
    all_posts().wait_send()
    all_posts().wait_recv()

    place_f = place.astype(jnp.float32).reshape(8, TILE, 128)

    def gather_one(g, sums):
        got = unpack(every[g])
        new = []
        for p in range(3):
            tile = jnp.take_along_axis(got, src_tile[p], axis=1)
            num = jnp.take_along_axis(got, src_num[p], axis=1)
            new.append(sums[p] + jnp.where(num[None] == place_f, tile[None], 0.0))
        return tuple(new)

    sums = lax.fori_loop(
        0, N_REP, gather_one, tuple(jnp.zeros((8, TILE, 128), jnp.float32) for _ in range(3)),
        unroll=True,
    )
    update = left(inv_l, right([s.reshape(SPAN, 128) for s in sums], inv_r))
    fresh = []
    for p in range(3):
        square = jnp.sum(update[p] * update[p], axis=0, keepdims=True)
        low = wide[0:1] < SPAN
        mean_lo = jnp.sum(jnp.where(low, square, 0.0), axis=1, keepdims=True) / (SPAN * SPAN)
        mean_hi = jnp.sum(jnp.where(low, 0.0, square), axis=1, keepdims=True) / (SPAN * SPAN)
        spread = jnp.sqrt(jnp.where(low, mean_lo, mean_hi) + epsilon)
        fresh.append(weights[p] - step_size * update[p] / spread)
    unpair(outw, fresh)


def shards(activations, out_grad, momentum, weight, kept_tile):
    f32 = jnp.float32
    vm = pltpu.VMEM
    dma = pltpu.SemaphoreType.DMA
    return tuple(
        pl.pallas_call(
            kernel,
            out_shape=(
                pltpu.VMEM(momentum.shape, f32),
                pltpu.VMEM(weight.shape, f32),
            ),
            in_specs=[pl.BlockSpec(memory_space=pltpu.HBM)] * 7,
            out_specs=(pl.BlockSpec(memory_space=pltpu.VMEM),) * 2,
            scratch_shapes=[
                vm((TOK, COLS), jnp.bfloat16),
                vm((TOK, TOK), jnp.bfloat16),
                vm((5, SPAN, SPAN), f32),
                vm((5, SPAN, SPAN), f32),
                pltpu.SMEM((1, 5), jnp.int32),
                vm((128, 256), f32),
                vm((512, 256), f32),
                vm((128, 256), jnp.bfloat16),
                vm((512, 256), jnp.bfloat16),
                vm((2, N_ZLO, N_X, SLAB, 128), f32),
                vm((N_ZLO, N_X, SLAB, 128), f32),
                vm((4, 2, HALF, 128), f32),
                vm((4, 2, HALF, 128), f32),
                vm((4, 2, HALF, 128), f32),
                vm((3, SLAB, 128), f32),
                vm((TOK, 2 * TOK), jnp.bfloat16),
                vm((N_FSDP, 1, 128), jnp.int32),
                vm((N_FSDP, TILE // 2, 128), f32),
                vm((N_FSDP, TILE // 2, 128), f32),
                vm((N_REP, TILE // 2, 128), f32),
                dma((8,)),
                dma((16,)),
                dma((16,)),
                dma((24,)),
                dma((24,)),
                dma((3,)),
                dma((3,)),
                dma,
                dma,
                dma,
                dma,
                dma,
                dma,
                pltpu.SemaphoreType.REGULAR,
            ],
            compiler_params=pltpu.CompilerParams(
                collective_id=0, has_side_effects=True, vmem_limit_bytes=48 * 1024 * 1024
            ),
            name="demo_step",
        )(*(
            pltpu.with_memory_space_constraint(a, pltpu.HBM)
            for a in (activations, out_grad, momentum, weight, kept_tile, *map(jnp.asarray, tables()))
        ))
    )


def solution(mesh):
    placed = (
        P(("rep", "fsdp"), None),
        P(("rep", "fsdp"), None),
        P("rep", "fsdp", None, None),
        P("fsdp", None, None),
        P("rep", "fsdp"),
    )
    return jax.shard_map(
        shards,
        mesh=mesh,
        in_specs=placed,
        out_specs=(P("rep", "fsdp", None, None), P("fsdp", None, None)),
        check_vma=False,
    )
```

```python
import jax
import jax.numpy as jnp
import ml_dtypes
import numpy as np
from jax import lax
from jax.experimental import pallas as pl
from jax.experimental.pallas import tpu as pltpu
from jax.sharding import PartitionSpec as P

SPAN = 64
TILE = 8
N_X = 4
N_ZLO = 4
N_REP = 16
N_FSDP = 32
HUB = 1
SLAB = 160
HALF = SLAB // 2
TOK = 128
COLS = 5120
WIDE = 640
PARITY = 4 * WIDE

decay_rate = 0.9
step_size = 0.5
epsilon = 1e-06

MESH = pl.DeviceIdType.MESH


def tables():
    u = np.arange(SPAN, dtype=np.float64)[:, None]
    x = np.arange(SPAN, dtype=np.float64)[None, :]
    s = np.where(u == 0, np.sqrt(1.0 / SPAN), np.sqrt(2.0 / SPAN))
    basis = s * np.cos(np.pi * (2.0 * x + 1.0) * u / (2.0 * SPAN))
    zero = np.zeros((SPAN, SPAN))

    def halves(table):
        high = table.astype(ml_dtypes.bfloat16)
        return high, (table - high.astype(np.float64)).astype(ml_dtypes.bfloat16)

    def for_left(table):
        high, low = halves(np.concatenate([table, zero], 1))
        high, low = high[:, :SPAN], low[:, :SPAN]
        return np.concatenate([high, high, low, zero.astype(high.dtype)], 1)

    def for_right(table):
        high, low = halves(np.block([[table, zero], [zero, table]]))
        return np.block([[high, low], [high, np.zeros_like(low)]])

    lefts = np.concatenate([for_left(basis), for_left(basis.T)], 0)
    rights = np.concatenate([for_right(basis.T), for_right(basis)], 0)
    return lefts.astype(np.float32), rights.astype(np.float32)


def halve(a):
    high = a.astype(jnp.bfloat16)
    return high, (a - high.astype(jnp.float32)).astype(jnp.bfloat16)


def left(table, parts):
    high, low = halve(jnp.concatenate(parts, axis=1))
    data = jnp.concatenate([high, low, high], axis=0)
    wide = jnp.dot(table, data, preferred_element_type=jnp.float32)
    return [wide[:, 128 * p : 128 * p + 128] for p in range(3)]


def right(parts, table):
    high, low = halve(jnp.concatenate(parts, axis=0))
    tall = jnp.dot(jnp.concatenate([high, low], axis=1), table, preferred_element_type=jnp.float32)
    tall = tall[:, :128] + tall[:, 128:]
    return [tall[SPAN * p : SPAN * p + SPAN] for p in range(3)]


def wrap(i, n):
    return jnp.where(i >= n, i - n, i)


def kernel(
    acts_h, outg_h, mom_h, wt_h, kept_h, lefts_h, rights_h,
    outm, outw,
    acts, outg, mom, wt, kept, lefts32, rights32, lefts, rights,
    part, rx, x1, x0, x2, zr, turned, names, tmsg, tin, every,
    lsem, csend, crecv, xsend, xrecv, zsend, zrecv, nsend, nrecv, tsend, trecv, gsend, grecv, told,
):
    rep = lax.axis_index("rep")
    f = lax.axis_index("fsdp")
    core = lax.rem(f, 2)
    x = lax.rem(f // 2, N_X)
    z = f // (2 * N_X)
    other = 1 - core
    xr, xl, xo = lax.rem(x + 1, N_X), lax.rem(x + 3, N_X), lax.rem(x + 2, N_X)

    def at(z_, x_, core_):
        return (rep, (z_ * N_X + x_) * 2 + core_)

    piece = [lax.rem(z + d, N_ZLO) for d in (1, 3, 2)] + [z]

    first = lax.rem(z + 1, 2)
    load_acts = []
    for k in range(2):
        par = first if k == 0 else 1 - first
        cols = pl.ds(pl.multiple_of(par * PARITY, 128), PARITY)
        load_acts.append(pltpu.make_async_copy(acts_h.at[:, cols], acts.at[:, cols], lsem.at[k]))
    load_outg = pltpu.make_async_copy(outg_h, outg, lsem.at[2])
    load_outg.start()
    load_acts[0].start()
    load_acts[1].start()
    small = [
        pltpu.make_async_copy(src, dst, lsem.at[3 + i])
        for i, (src, dst) in enumerate(((mom_h.at[0], mom), (wt_h, wt), (kept_h, kept), (lefts_h, lefts32), (rights_h, rights32)))
    ]
    for copy in small:
        copy.start()

    barrier = pltpu.get_barrier_semaphore()

    def greet_group(i, carry):
        member = wrap(f + i, N_FSDP)

        @pl.when(member != HUB)
        def _():
            pl.semaphore_signal(barrier, inc=1, device_id=(rep, member), device_id_type=MESH)

        return carry

    def greet_peers(i, carry):
        pl.semaphore_signal(
            barrier, inc=1, device_id=(wrap(rep + i, N_REP), f), device_id_type=MESH
        )
        return carry

    lax.fori_loop(1, N_FSDP, greet_group, 0)

    lane = lax.broadcasted_iota(jnp.int32, (32, 128), 1)

    owners = [xo, xr, xl, x]

    def chunk(half, o, grads):
        par, j = (first if half == 0 else 1 - first), owners[o]
        base = pl.multiple_of(par * PARITY + j * WIDE, 128)
        prod = jnp.dot(grads, acts[:, pl.ds(base, WIDE)], preferred_element_type=jnp.float32)
        for h in range(2):
            blk = prod[SPAN * h : SPAN * h + SPAN]
            zz = 2 * h + par
            b2 = blk[:, 256:384]
            part[0, zz, j, 0:64] = blk[:, 0:128]
            part[0, zz, j, 64:128] = blk[:, 128:256]
            part[0, zz, j, 128:160] = jnp.where(lane < 64, b2[0:32], pltpu.roll(b2[32:64], 64, 1))
            part[1, zz, j, 0:64] = blk[:, 384:512]
            part[1, zz, j, 64:128] = blk[:, 512:640]
            part[1, zz, j, 128:160] = jnp.where(lane < 64, pltpu.roll(b2[0:32], 64, 1), b2[32:64])
        for k in (2 * half, 2 * half + 1):
            swap(k, o).start()

    def swap(k, o):
        return pltpu.make_async_remote_copy(
            src_ref=part.at[other, piece[k], owners[o]], dst_ref=rx.at[k, o],
            send_sem=csend.at[4 * k + o], recv_sem=crecv.at[4 * k + o],
            device_id=at(z, x, other), device_id_type=MESH,
        )

    A, B = pl.ds(0, HALF), pl.ds(HALF, HALF)

    def hop(k, kind, way):
        side = xr if way == 0 else xl
        slab = xo if kind == 1 else side
        rows = (B if way == 0 else A) if kind == 0 else (A if way == 0 else B)
        land = (x0, x1, x2)[kind]
        i = (k * 3 + kind) * 2 + way
        return pltpu.make_async_remote_copy(
            src_ref=part.at[core, piece[k], slab, rows], dst_ref=land.at[k, way],
            send_sem=xsend.at[i], recv_sem=xrecv.at[i],
            device_id=at(z, side, core), device_id_type=MESH,
        )

    def zhop(k):
        return pltpu.make_async_remote_copy(
            src_ref=part.at[core, piece[k], x], dst_ref=zr.at[k],
            send_sem=zsend.at[k], recv_sem=zrecv.at[k],
            device_id=at(piece[k], x, core), device_id_type=MESH,
        )

    def take(k, o):
        swap(k, o).wait_recv()
        slab = owners[o]
        part[core, piece[k], slab] = part[core, piece[k], slab] + rx[k, o]

    def open_far(k):
        take(k, 0)
        hop(k, 1, 0).start()
        hop(k, 1, 1).start()

    def open_near(k):
        for way in range(2):
            take(k, 1 + way)
            hop(k, 0, way).start()

    def pass_on(k):
        for way in range(2):
            hop(k, 1, way).wait_recv()
            side, rows = (xr, A) if way == 0 else (xl, B)
            part[core, piece[k], side, rows] = part[core, piece[k], side, rows] + x1[k, way]
            hop(k, 2, way).start()

    def close_piece(k):
        take(k, 3)
        for way in range(2):
            hop(k, 0, way).wait_recv()
            hop(k, 2, way).wait_recv()
        part[core, piece[k], x, A] = part[core, piece[k], x, A] + (x0[k, 1] + x2[k, 0])
        part[core, piece[k], x, B] = part[core, piece[k], x, B] + (x0[k, 0] + x2[k, 1])
        if k < 3:
            zhop(k).start()

    order = [core, core + 1, core + 2, core + 3, 4 * other]
    lane1 = lax.broadcasted_iota(jnp.int32, (1, 128), 1)
    lane4 = lax.broadcasted_iota(jnp.int32, (4, 128), 1)
    lane8 = lax.broadcasted_iota(jnp.int32, (TILE, 128), 1)
    wide = lax.broadcasted_iota(jnp.int32, (SPAN, 128), 1)
    row = lax.broadcasted_iota(jnp.int32, (SPAN, 128), 0)
    place = (row // TILE) * TILE + lax.rem(wide, SPAN) // TILE
    upper = jnp.where(lane8 < SPAN, 0, SPAN)
    block = lax.rem(lane8, SPAN) // TILE

    def to_group(src, dst, send, recv, i):
        return pltpu.make_async_remote_copy(
            src_ref=src, dst_ref=dst, send_sem=send, recv_sem=recv,
            device_id=(rep, wrap(f + i, N_FSDP)), device_id_type=MESH,
        )

    def to_peer(src, dst, send, recv, i):
        return pltpu.make_async_remote_copy(
            src_ref=src, dst_ref=dst, send_sem=send, recv_sem=recv,
            device_id=(wrap(rep + i, N_REP), f), device_id_type=MESH,
        )

    def send_names():
        mine = jnp.zeros((1, 128), jnp.int32)
        for s in range(5):
            mine = jnp.where(lane1 == s, kept[0, s], mine)
        names[f] = mine

        def one(i, carry):
            to_group(names.at[f], names.at[f], nsend, nrecv, i).start()
            return carry

        lax.fori_loop(1, N_FSDP, one, 0)

    def all_names():
        ref = names.at[pl.ds(0, N_FSDP - 1)]
        return to_group(ref, ref, nsend, nrecv, 1)

    def pick_columns(tile, number):
        source = (number & 7) * TILE + lax.rem(lane8, TILE) + upper
        return jnp.take_along_axis(tile, source, axis=1)

    def merge(a, b, c):
        return jnp.where(block == 0, a, jnp.where(block == 1, b, c))

    def pack(tiles):
        return jnp.where(lax.rem(lane4, SPAN) < 24, tiles[0:4], pltpu.roll(tiles[4:8], 24, 1))

    def unpack(four):
        return jnp.concatenate([four, pltpu.roll(four, 104, 1)], axis=0)

    def two_chunks(i, carry):
        numbers, rows = [], []
        for c in range(2):
            m = 2 * i + c
            piece_acts = acts[:, pl.ds(pl.multiple_of(m * WIDE, 128), WIDE)]
            both = jnp.dot(
                turned[...], jnp.concatenate([piece_acts, piece_acts], axis=0),
                preferred_element_type=jnp.float32,
            )
            for h in range(2):
                owner = ((2 * h + m // 4) * N_X + lax.rem(m, 4)) * 2
                low = jnp.broadcast_to(names[owner], (TILE, 128))
                high = jnp.broadcast_to(names[owner + 1], (TILE, 128))
                ten = jnp.where(lane8 < 5, low, pltpu.roll(high, 5, 1))
                for p in range(5):
                    number = jnp.take_along_axis(ten, 2 * p + jnp.where(lane8 < SPAN, 0, 1), axis=1)
                    high_part = number >> 3
                    found = both[SPAN * h : SPAN * h + TILE, 128 * p : 128 * p + 128]
                    for a in range(1, 8):
                        at_row = SPAN * h + TILE * a
                        found = jnp.where(
                            high_part == a, both[at_row : at_row + TILE, 128 * p : 128 * p + 128], found
                        )
                    numbers.append(number)
                    rows.append(found)
        high, low = halve(jnp.concatenate(rows, axis=0))
        out = jnp.dot(
            jnp.concatenate([high, low], axis=1), rights[0:256], preferred_element_type=jnp.float32
        )
        out = out[:, :128] + out[:, 128:]
        for c in range(2):
            m = 2 * i + c
            for h in range(2):
                owner = ((2 * h + m // 4) * N_X + lax.rem(m, 4)) * 2
                base = 10 * c + 5 * h
                t = [
                    pick_columns(out[TILE * q : TILE * q + TILE], numbers[q])
                    for q in range(base, base + 5)
                ]
                tmsg[owner] = pack(merge(t[0], t[1], t[2]))
                tmsg[owner + 1] = pack(merge(t[3], t[4], pltpu.roll(t[2], SPAN, 1)))
        return carry

    def send_tiles():
        tin[f] = tmsg[f]

        def one(i, carry):
            to_group(tmsg.at[wrap(f + i, N_FSDP)], tin.at[f], tsend, trecv, i).start()
            return carry

        lax.fori_loop(1, N_FSDP, one, 0)

    def all_tiles():
        span = pl.ds(0, N_FSDP - 1)
        return to_group(tmsg.at[span], tin.at[span], tsend, trecv, 1)

    def pairs(ref):
        zero = jnp.zeros((SPAN, SPAN), jnp.float32)
        return [
            jnp.concatenate([ref[order[0]], ref[order[1]]], axis=1),
            jnp.concatenate([ref[order[2]], ref[order[3]]], axis=1),
            jnp.concatenate([ref[order[4]], zero], axis=1),
        ]

    def unpair(ref, parts):
        for j in range(5):
            half = parts[j // 2][:, SPAN * (j % 2) : SPAN * (j % 2) + SPAN]
            ref[order[j]] = half

    @pl.when(f != HUB)
    def _():
        pl.semaphore_wait(barrier, N_FSDP - 1)

    @pl.when(f == HUB - 1)
    def _():
        pl.semaphore_signal(told, inc=1, device_id=(rep, HUB), device_id_type=MESH)

    @pl.when(f == HUB)
    def _():
        pl.semaphore_wait(told, 1)
        lax.fori_loop(1, N_REP, greet_peers, 0)

    small[2].wait()
    send_names()
    load_outg.wait()
    flat = outg[...]
    grads = flat.astype(jnp.float32).T.astype(jnp.bfloat16)
    load_acts[0].wait()
    for o in range(3):
        chunk(0, o, grads)
    for i in (0, 1, 3, 4):
        small[i].wait()
    lefts[...] = lefts32[...].astype(jnp.bfloat16)
    rights[...] = rights32[...].astype(jnp.bfloat16)
    fwd_l, inv_l = lefts[0:64, 0:192], lefts[64:128, 0:192]
    fwd_r, inv_r = rights[0:256], rights[256:512]
    spun = jnp.dot(flat, rights[0:128], preferred_element_type=jnp.float32)
    spun_high, spun_low = halve((spun[:, :128] + spun[:, 128:]).T)
    turned[:, :128] = spun_high
    turned[:, 128:] = spun_low
    chunk(0, 3, grads)
    open_far(0)
    open_far(1)
    open_near(0)
    open_near(1)
    load_acts[1].wait()
    all_names().wait_recv()
    lax.fori_loop(0, 4, two_chunks, 0)
    send_tiles()

    def tell(i, carry):
        member = wrap(f + i, N_FSDP)
        pl.semaphore_signal(told, inc=1, device_id=(rep, member), device_id_type=MESH)
        return carry

    @pl.when(f == HUB)
    def _():
        pl.semaphore_wait(barrier, N_REP - 1)
        lax.fori_loop(1, N_FSDP, tell, 0)

    pass_on(0)
    pass_on(1)
    for o in range(4):
        chunk(1, o, grads)

    scalars = [kept[0, s] for s in order]
    carried = [decay_rate * m for m in pairs(mom)]
    own = [
        jnp.where(wide < SPAN, scalars[2 * p], scalars[min(2 * p + 1, 4)]) for p in range(3)
    ]
    coef = right(left(fwd_l, carried), fwd_r)
    found = [
        pick_columns(
            jnp.sum(jnp.where(place == own[p], coef[p], 0.0).reshape(8, TILE, 128), axis=0), own[p][0:8]
        )
        for p in range(3)
    ]
    from_momentum = merge(*found)

    all_tiles().wait_recv()
    tiles = from_momentum + unpack(jnp.sum(tin[...], axis=0))
    message = pack(tiles)
    for j in range(5):
        spot = (lane4 == 56 + j) | (lane4 == 80 + j)
        message = jnp.where(spot, scalars[j].astype(jnp.float32), message)
    every[rep] = message

    @pl.when(f != HUB)
    def _():
        pl.semaphore_wait(told, 1)

    def send_one(i, carry):
        to_peer(every.at[rep], every.at[rep], gsend, grecv, i).start()
        return carry

    lax.fori_loop(1, N_REP, send_one, 0)

    def all_posts():
        ref = every.at[pl.ds(0, N_REP - 1)]
        return to_peer(ref, ref, gsend, grecv, 1)

    open_far(2)
    open_far(3)
    open_near(2)
    open_near(3)
    pass_on(2)
    close_piece(0)
    pass_on(3)
    close_piece(1)
    close_piece(2)
    src_tile = [upper + TILE * p + lax.rem(lane8, TILE) for p in range(3)]
    src_num = [56 + jnp.where(lane8 < SPAN, 2 * p, min(2 * p + 1, 4)) for p in range(3)]

    def spread_out(p):
        tile = jnp.take_along_axis(tiles, src_tile[p], axis=1)
        tall = jnp.broadcast_to(tile[None], (8, TILE, 128)).reshape(SPAN, 128)
        return jnp.where(place == own[p], tall, 0.0)

    decoded = left(inv_l, right([spread_out(p) for p in range(3)], inv_r))
    for p in range(3):
        carried[p] = carried[p] - decoded[p]
    weights = pairs(wt)
    close_piece(3)
    total = part[core, z, x]
    tail = jnp.concatenate([total[128:160], pltpu.roll(total[128:160], 64, 1)], axis=0)
    for p, grown in enumerate((total[0:64], total[64:128], tail)):
        carried[p] = carried[p] + grown
    for k in range(4):
        for o in range(4):
            swap(k, o).wait_send()
        for kind in range(3):
            for way in range(2):
                hop(k, kind, way).wait_send()
    for k in range(3):
        zhop(k).wait()
    rest = zr[0] + zr[1] + zr[2]
    tail = jnp.concatenate([rest[128:160], pltpu.roll(rest[128:160], 64, 1)], axis=0)
    unpair(outm.at[0], [carried[0] + rest[0:64], carried[1] + rest[64:128], carried[2] + tail])
    all_names().wait_send()
    all_tiles().wait_send()
    all_posts().wait_send()
    all_posts().wait_recv()

    place_f = place.astype(jnp.float32).reshape(8, TILE, 128)

    def gather_one(g, sums):
        got = unpack(every[g])
        new = []
        for p in range(3):
            tile = jnp.take_along_axis(got, src_tile[p], axis=1)
            num = jnp.take_along_axis(got, src_num[p], axis=1)
            new.append(sums[p] + jnp.where(num[None] == place_f, tile[None], 0.0))
        return tuple(new)

    sums = lax.fori_loop(
        0, N_REP, gather_one, tuple(jnp.zeros((8, TILE, 128), jnp.float32) for _ in range(3)),
        unroll=True,
    )
    update = left(inv_l, right([s.reshape(SPAN, 128) for s in sums], inv_r))
    fresh = []
    for p in range(3):
        square = jnp.sum(update[p] * update[p], axis=0, keepdims=True)
        low = wide[0:1] < SPAN
        mean_lo = jnp.sum(jnp.where(low, square, 0.0), axis=1, keepdims=True) / (SPAN * SPAN)
        mean_hi = jnp.sum(jnp.where(low, 0.0, square), axis=1, keepdims=True) / (SPAN * SPAN)
        spread = jnp.sqrt(jnp.where(low, mean_lo, mean_hi) + epsilon)
        fresh.append(weights[p] - step_size * update[p] / spread)
    unpair(outw, fresh)


def shards(activations, out_grad, momentum, weight, kept_tile):
    f32 = jnp.float32
    vm = pltpu.VMEM
    dma = pltpu.SemaphoreType.DMA
    return tuple(
        pl.pallas_call(
            kernel,
            out_shape=(
                pltpu.VMEM(momentum.shape, f32),
                pltpu.VMEM(weight.shape, f32),
            ),
            in_specs=[pl.BlockSpec(memory_space=pltpu.HBM)] * 7,
            out_specs=(pl.BlockSpec(memory_space=pltpu.VMEM),) * 2,
            scratch_shapes=[
                vm((TOK, COLS), jnp.bfloat16),
                vm((TOK, TOK), jnp.bfloat16),
                vm((5, SPAN, SPAN), f32),
                vm((5, SPAN, SPAN), f32),
                pltpu.SMEM((1, 5), jnp.int32),
                vm((128, 256), f32),
                vm((512, 256), f32),
                vm((128, 256), jnp.bfloat16),
                vm((512, 256), jnp.bfloat16),
                vm((2, N_ZLO, N_X, SLAB, 128), f32),
                vm((N_ZLO, N_X, SLAB, 128), f32),
                vm((4, 2, HALF, 128), f32),
                vm((4, 2, HALF, 128), f32),
                vm((4, 2, HALF, 128), f32),
                vm((3, SLAB, 128), f32),
                vm((TOK, 2 * TOK), jnp.bfloat16),
                vm((N_FSDP, 1, 128), jnp.int32),
                vm((N_FSDP, TILE // 2, 128), f32),
                vm((N_FSDP, TILE // 2, 128), f32),
                vm((N_REP, TILE // 2, 128), f32),
                dma((8,)),
                dma((16,)),
                dma((16,)),
                dma((24,)),
                dma((24,)),
                dma((3,)),
                dma((3,)),
                dma,
                dma,
                dma,
                dma,
                dma,
                dma,
                pltpu.SemaphoreType.REGULAR,
            ],
            compiler_params=pltpu.CompilerParams(
                collective_id=0, has_side_effects=True, vmem_limit_bytes=48 * 1024 * 1024
            ),
            name="demo_step",
        )(*(
            pltpu.with_memory_space_constraint(a, pltpu.HBM)
            for a in (activations, out_grad, momentum, weight, kept_tile, *map(jnp.asarray, tables()))
        ))
    )


def solution(mesh):
    placed = (
        P(("rep", "fsdp"), None),
        P(("rep", "fsdp"), None),
        P("rep", "fsdp", None, None),
        P("fsdp", None, None),
        P("rep", "fsdp"),
    )
    return jax.shard_map(
        shards,
        mesh=mesh,
        in_specs=placed,
        out_specs=(P("rep", "fsdp", None, None), P("fsdp", None, None)),
        check_vma=False,
    )
```

```python
import jax
import jax.numpy as jnp
import ml_dtypes
import numpy as np
from jax import lax
from jax.experimental import pallas as pl
from jax.experimental.pallas import tpu as pltpu
from jax.sharding import PartitionSpec as P

SPAN = 64
TILE = 8
N_X = 4
N_ZLO = 4
N_REP = 16
N_FSDP = 32
HUB = 1
SLAB = 160
HALF = SLAB // 2
TOK = 128
COLS = 5120
WIDE = 640
PARITY = 4 * WIDE

decay_rate = 0.9
step_size = 0.5
epsilon = 1e-06

MESH = pl.DeviceIdType.MESH


def tables():
    u = np.arange(SPAN, dtype=np.float64)[:, None]
    x = np.arange(SPAN, dtype=np.float64)[None, :]
    s = np.where(u == 0, np.sqrt(1.0 / SPAN), np.sqrt(2.0 / SPAN))
    basis = s * np.cos(np.pi * (2.0 * x + 1.0) * u / (2.0 * SPAN))
    zero = np.zeros((SPAN, SPAN))

    def halves(table):
        high = table.astype(ml_dtypes.bfloat16)
        return high, (table - high.astype(np.float64)).astype(ml_dtypes.bfloat16)

    def for_left(table):
        high, low = halves(np.concatenate([table, zero], 1))
        high, low = high[:, :SPAN], low[:, :SPAN]
        return np.concatenate([high, high, low, zero.astype(high.dtype)], 1)

    def for_right(table):
        high, low = halves(np.block([[table, zero], [zero, table]]))
        return np.block([[high, low], [high, np.zeros_like(low)]])

    lefts = np.concatenate([for_left(basis), for_left(basis.T)], 0)
    rights = np.concatenate([for_right(basis.T), for_right(basis)], 0)
    return lefts.astype(np.float32), rights.astype(np.float32)


def halve(a):
    high = a.astype(jnp.bfloat16)
    return high, (a - high.astype(jnp.float32)).astype(jnp.bfloat16)


def left(table, parts):
    high, low = halve(jnp.concatenate(parts, axis=1))
    data = jnp.concatenate([high, low, high], axis=0)
    wide = jnp.dot(table, data, preferred_element_type=jnp.float32)
    return [wide[:, 128 * p : 128 * p + 128] for p in range(3)]


def right(parts, table):
    high, low = halve(jnp.concatenate(parts, axis=0))
    tall = jnp.dot(jnp.concatenate([high, low], axis=1), table, preferred_element_type=jnp.float32)
    tall = tall[:, :128] + tall[:, 128:]
    return [tall[SPAN * p : SPAN * p + SPAN] for p in range(3)]


def wrap(i, n):
    return jnp.where(i >= n, i - n, i)


def kernel(
    acts_h, outg_h, mom_h, wt_h, kept_h, lefts_h, rights_h,
    outm, outw,
    acts, outg, mom, wt, kept, lefts32, rights32, lefts, rights,
    part, rx, x1, x0, x2, zr, turned, names, tmsg, tin, every,
    lsem, csend, crecv, xsend, xrecv, zsend, zrecv, nsend, nrecv, tsend, trecv, gsend, grecv, told,
):
    rep = lax.axis_index("rep")
    f = lax.axis_index("fsdp")
    core = lax.rem(f, 2)
    x = lax.rem(f // 2, N_X)
    z = f // (2 * N_X)
    other = 1 - core
    xr, xl, xo = lax.rem(x + 1, N_X), lax.rem(x + 3, N_X), lax.rem(x + 2, N_X)

    def at(z_, x_, core_):
        return (rep, (z_ * N_X + x_) * 2 + core_)

    piece = [lax.rem(z + d, N_ZLO) for d in (1, 3, 2)] + [z]

    first = lax.rem(z + 1, 2)
    load_acts = []
    for k in range(2):
        par = first if k == 0 else 1 - first
        cols = pl.ds(pl.multiple_of(par * PARITY, 128), PARITY)
        load_acts.append(pltpu.make_async_copy(acts_h.at[:, cols], acts.at[:, cols], lsem.at[k]))
    load_outg = pltpu.make_async_copy(outg_h, outg, lsem.at[2])
    load_outg.start()
    load_acts[0].start()
    load_acts[1].start()
    small = [
        pltpu.make_async_copy(src, dst, lsem.at[3 + i])
        for i, (src, dst) in enumerate(((mom_h.at[0], mom), (wt_h, wt), (kept_h, kept), (lefts_h, lefts32), (rights_h, rights32)))
    ]
    for copy in small:
        copy.start()

    barrier = pltpu.get_barrier_semaphore()

    def greet_group(i, carry):
        member = wrap(f + i, N_FSDP)

        @pl.when(member != HUB)
        def _():
            pl.semaphore_signal(barrier, inc=1, device_id=(rep, member), device_id_type=MESH)

        return carry

    def greet_peers(i, carry):
        pl.semaphore_signal(
            barrier, inc=1, device_id=(wrap(rep + i, N_REP), f), device_id_type=MESH
        )
        return carry

    lax.fori_loop(1, N_FSDP, greet_group, 0)

    lane = lax.broadcasted_iota(jnp.int32, (32, 128), 1)

    owners = [xo, xr, xl, x]

    def chunk(half, o, grads):
        par, j = (first if half == 0 else 1 - first), owners[o]
        base = pl.multiple_of(par * PARITY + j * WIDE, 128)
        prod = jnp.dot(grads, acts[:, pl.ds(base, WIDE)], preferred_element_type=jnp.float32)
        for h in range(2):
            blk = prod[SPAN * h : SPAN * h + SPAN]
            zz = 2 * h + par
            b2 = blk[:, 256:384]
            part[0, zz, j, 0:64] = blk[:, 0:128]
            part[0, zz, j, 64:128] = blk[:, 128:256]
            part[0, zz, j, 128:160] = jnp.where(lane < 64, b2[0:32], pltpu.roll(b2[32:64], 64, 1))
            part[1, zz, j, 0:64] = blk[:, 384:512]
            part[1, zz, j, 64:128] = blk[:, 512:640]
            part[1, zz, j, 128:160] = jnp.where(lane < 64, pltpu.roll(b2[0:32], 64, 1), b2[32:64])
        for k in (2 * half, 2 * half + 1):
            swap(k, o).start()

    def swap(k, o):
        return pltpu.make_async_remote_copy(
            src_ref=part.at[other, piece[k], owners[o]], dst_ref=rx.at[k, o],
            send_sem=csend.at[4 * k + o], recv_sem=crecv.at[4 * k + o],
            device_id=at(z, x, other), device_id_type=MESH,
        )

    A, B = pl.ds(0, HALF), pl.ds(HALF, HALF)

    def hop(k, kind, way):
        side = xr if way == 0 else xl
        slab = xo if kind == 1 else side
        rows = (B if way == 0 else A) if kind == 0 else (A if way == 0 else B)
        land = (x0, x1, x2)[kind]
        i = (k * 3 + kind) * 2 + way
        return pltpu.make_async_remote_copy(
            src_ref=part.at[core, piece[k], slab, rows], dst_ref=land.at[k, way],
            send_sem=xsend.at[i], recv_sem=xrecv.at[i],
            device_id=at(z, side, core), device_id_type=MESH,
        )

    def zhop(k):
        return pltpu.make_async_remote_copy(
            src_ref=part.at[core, piece[k], x], dst_ref=zr.at[k],
            send_sem=zsend.at[k], recv_sem=zrecv.at[k],
            device_id=at(piece[k], x, core), device_id_type=MESH,
        )

    def take(k, o):
        swap(k, o).wait_recv()
        slab = owners[o]
        part[core, piece[k], slab] = part[core, piece[k], slab] + rx[k, o]

    def open_far(k):
        take(k, 0)
        hop(k, 1, 0).start()
        hop(k, 1, 1).start()

    def open_near(k):
        for way in range(2):
            take(k, 1 + way)
            hop(k, 0, way).start()

    def pass_on(k):
        for way in range(2):
            hop(k, 1, way).wait_recv()
            side, rows = (xr, A) if way == 0 else (xl, B)
            part[core, piece[k], side, rows] = part[core, piece[k], side, rows] + x1[k, way]
            hop(k, 2, way).start()

    def close_piece(k):
        take(k, 3)
        for way in range(2):
            hop(k, 0, way).wait_recv()
            hop(k, 2, way).wait_recv()
        part[core, piece[k], x, A] = part[core, piece[k], x, A] + (x0[k, 1] + x2[k, 0])
        part[core, piece[k], x, B] = part[core, piece[k], x, B] + (x0[k, 0] + x2[k, 1])
        if k < 3:
            zhop(k).start()

    order = [core, core + 1, core + 2, core + 3, 4 * other]
    lane1 = lax.broadcasted_iota(jnp.int32, (1, 128), 1)
    lane4 = lax.broadcasted_iota(jnp.int32, (4, 128), 1)
    lane8 = lax.broadcasted_iota(jnp.int32, (TILE, 128), 1)
    wide = lax.broadcasted_iota(jnp.int32, (SPAN, 128), 1)
    row = lax.broadcasted_iota(jnp.int32, (SPAN, 128), 0)
    place = (row // TILE) * TILE + lax.rem(wide, SPAN) // TILE
    upper = jnp.where(lane8 < SPAN, 0, SPAN)
    block = lax.rem(lane8, SPAN) // TILE

    def to_group(src, dst, send, recv, i):
        return pltpu.make_async_remote_copy(
            src_ref=src, dst_ref=dst, send_sem=send, recv_sem=recv,
            device_id=(rep, wrap(f + i, N_FSDP)), device_id_type=MESH,
        )

    def to_peer(src, dst, send, recv, i):
        return pltpu.make_async_remote_copy(
            src_ref=src, dst_ref=dst, send_sem=send, recv_sem=recv,
            device_id=(wrap(rep + i, N_REP), f), device_id_type=MESH,
        )

    def send_names():
        mine = jnp.zeros((1, 128), jnp.int32)
        for s in range(5):
            mine = jnp.where(lane1 == s, kept[0, s], mine)
        names[f] = mine

        def one(i, carry):
            to_group(names.at[f], names.at[f], nsend, nrecv, i).start()
            return carry

        lax.fori_loop(1, N_FSDP, one, 0)

    def all_names():
        ref = names.at[pl.ds(0, N_FSDP - 1)]
        return to_group(ref, ref, nsend, nrecv, 1)

    def pick_columns(tile, number):
        source = (number & 7) * TILE + lax.rem(lane8, TILE) + upper
        return jnp.take_along_axis(tile, source, axis=1)

    def merge(a, b, c):
        return jnp.where(block == 0, a, jnp.where(block == 1, b, c))

    def pack(tiles):
        return jnp.where(lax.rem(lane4, SPAN) < 24, tiles[0:4], pltpu.roll(tiles[4:8], 24, 1))

    def unpack(four):
        return jnp.concatenate([four, pltpu.roll(four, 104, 1)], axis=0)

    def two_chunks(i, carry):
        numbers, rows = [], []
        for c in range(2):
            m = 2 * i + c
            piece_acts = acts[:, pl.ds(pl.multiple_of(m * WIDE, 128), WIDE)]
            both = jnp.dot(
                turned[...], jnp.concatenate([piece_acts, piece_acts], axis=0),
                preferred_element_type=jnp.float32,
            )
            for h in range(2):
                owner = ((2 * h + m // 4) * N_X + lax.rem(m, 4)) * 2
                low = jnp.broadcast_to(names[owner], (TILE, 128))
                high = jnp.broadcast_to(names[owner + 1], (TILE, 128))
                ten = jnp.where(lane8 < 5, low, pltpu.roll(high, 5, 1))
                for p in range(5):
                    number = jnp.take_along_axis(ten, 2 * p + jnp.where(lane8 < SPAN, 0, 1), axis=1)
                    high_part = number >> 3
                    found = both[SPAN * h : SPAN * h + TILE, 128 * p : 128 * p + 128]
                    for a in range(1, 8):
                        at_row = SPAN * h + TILE * a
                        found = jnp.where(
                            high_part == a, both[at_row : at_row + TILE, 128 * p : 128 * p + 128], found
                        )
                    numbers.append(number)
                    rows.append(found)
        high, low = halve(jnp.concatenate(rows, axis=0))
        out = jnp.dot(
            jnp.concatenate([high, low], axis=1), rights[0:256], preferred_element_type=jnp.float32
        )
        out = out[:, :128] + out[:, 128:]
        for c in range(2):
            m = 2 * i + c
            for h in range(2):
                owner = ((2 * h + m // 4) * N_X + lax.rem(m, 4)) * 2
                base = 10 * c + 5 * h
                t = [
                    pick_columns(out[TILE * q : TILE * q + TILE], numbers[q])
                    for q in range(base, base + 5)
                ]
                tmsg[owner] = pack(merge(t[0], t[1], t[2]))
                tmsg[owner + 1] = pack(merge(t[3], t[4], pltpu.roll(t[2], SPAN, 1)))
        return carry

    def send_tiles():
        tin[f] = tmsg[f]

        def one(i, carry):
            to_group(tmsg.at[wrap(f + i, N_FSDP)], tin.at[f], tsend, trecv, i).start()
            return carry

        lax.fori_loop(1, N_FSDP, one, 0)

    def all_tiles():
        span = pl.ds(0, N_FSDP - 1)
        return to_group(tmsg.at[span], tin.at[span], tsend, trecv, 1)

    def pairs(ref):
        zero = jnp.zeros((SPAN, SPAN), jnp.float32)
        return [
            jnp.concatenate([ref[order[0]], ref[order[1]]], axis=1),
            jnp.concatenate([ref[order[2]], ref[order[3]]], axis=1),
            jnp.concatenate([ref[order[4]], zero], axis=1),
        ]

    def unpair(ref, parts):
        for j in range(5):
            half = parts[j // 2][:, SPAN * (j % 2) : SPAN * (j % 2) + SPAN]
            ref[order[j]] = half

    @pl.when(f != HUB)
    def _():
        pl.semaphore_wait(barrier, N_FSDP - 1)

    @pl.when(f == HUB - 1)
    def _():
        pl.semaphore_signal(told, inc=1, device_id=(rep, HUB), device_id_type=MESH)

    @pl.when(f == HUB)
    def _():
        pl.semaphore_wait(told, 1)
        lax.fori_loop(1, N_REP, greet_peers, 0)

    small[2].wait()
    send_names()
    load_outg.wait()
    flat = outg[...]
    grads = flat.astype(jnp.float32).T.astype(jnp.bfloat16)
    load_acts[0].wait()
    for o in range(3):
        chunk(0, o, grads)
    for i in (0, 1, 3, 4):
        small[i].wait()
    lefts[...] = lefts32[...].astype(jnp.bfloat16)
    rights[...] = rights32[...].astype(jnp.bfloat16)
    fwd_l, inv_l = lefts[0:64, 0:192], lefts[64:128, 0:192]
    fwd_r, inv_r = rights[0:256], rights[256:512]
    spun = jnp.dot(flat, rights[0:128], preferred_element_type=jnp.float32)
    spun_high, spun_low = halve((spun[:, :128] + spun[:, 128:]).T)
    turned[:, :128] = spun_high
    turned[:, 128:] = spun_low
    chunk(0, 3, grads)
    open_far(0)
    open_far(1)
    open_near(0)
    open_near(1)
    load_acts[1].wait()
    all_names().wait_recv()
    lax.fori_loop(0, 4, two_chunks, 0)
    send_tiles()

    def tell(i, carry):
        member = wrap(f + i, N_FSDP)
        pl.semaphore_signal(told, inc=1, device_id=(rep, member), device_id_type=MESH)
        return carry

    pass_on(0)
    pass_on(1)
    for o in range(4):
        chunk(1, o, grads)
    open_far(2)
    open_far(3)
    open_near(2)
    open_near(3)

    @pl.when(f == HUB)
    def _():
        pl.semaphore_wait(barrier, N_REP - 1)
        lax.fori_loop(1, N_FSDP, tell, 0)

    scalars = [kept[0, s] for s in order]
    carried = [decay_rate * m for m in pairs(mom)]
    own = [
        jnp.where(wide < SPAN, scalars[2 * p], scalars[min(2 * p + 1, 4)]) for p in range(3)
    ]
    coef = right(left(fwd_l, carried), fwd_r)
    found = [
        pick_columns(
            jnp.sum(jnp.where(place == own[p], coef[p], 0.0).reshape(8, TILE, 128), axis=0), own[p][0:8]
        )
        for p in range(3)
    ]
    from_momentum = merge(*found)

    all_tiles().wait_recv()
    tiles = from_momentum + unpack(jnp.sum(tin[...], axis=0))
    message = pack(tiles)
    for j in range(5):
        spot = (lane4 == 56 + j) | (lane4 == 80 + j)
        message = jnp.where(spot, scalars[j].astype(jnp.float32), message)
    every[rep] = message

    @pl.when(f != HUB)
    def _():
        pl.semaphore_wait(told, 1)

    def send_one(i, carry):
        to_peer(every.at[rep], every.at[rep], gsend, grecv, i).start()
        return carry

    lax.fori_loop(1, N_REP, send_one, 0)

    def all_posts():
        ref = every.at[pl.ds(0, N_REP - 1)]
        return to_peer(ref, ref, gsend, grecv, 1)

    pass_on(2)
    close_piece(0)
    pass_on(3)
    close_piece(1)
    close_piece(2)
    src_tile = [upper + TILE * p + lax.rem(lane8, TILE) for p in range(3)]
    src_num = [56 + jnp.where(lane8 < SPAN, 2 * p, min(2 * p + 1, 4)) for p in range(3)]

    def spread_out(p):
        tile = jnp.take_along_axis(tiles, src_tile[p], axis=1)
        tall = jnp.broadcast_to(tile[None], (8, TILE, 128)).reshape(SPAN, 128)
        return jnp.where(place == own[p], tall, 0.0)

    decoded = left(inv_l, right([spread_out(p) for p in range(3)], inv_r))
    for p in range(3):
        carried[p] = carried[p] - decoded[p]
    weights = pairs(wt)
    close_piece(3)
    total = part[core, z, x]
    tail = jnp.concatenate([total[128:160], pltpu.roll(total[128:160], 64, 1)], axis=0)
    for p, grown in enumerate((total[0:64], total[64:128], tail)):
        carried[p] = carried[p] + grown
    for k in range(4):
        for o in range(4):
            swap(k, o).wait_send()
        for kind in range(3):
            for way in range(2):
                hop(k, kind, way).wait_send()
    for k in range(3):
        zhop(k).wait()
    rest = zr[0] + zr[1] + zr[2]
    tail = jnp.concatenate([rest[128:160], pltpu.roll(rest[128:160], 64, 1)], axis=0)
    unpair(outm.at[0], [carried[0] + rest[0:64], carried[1] + rest[64:128], carried[2] + tail])
    all_names().wait_send()
    all_tiles().wait_send()
    all_posts().wait_send()
    all_posts().wait_recv()

    place_f = place.astype(jnp.float32).reshape(8, TILE, 128)

    def gather_one(g, sums):
        got = unpack(every[g])
        new = []
        for p in range(3):
            tile = jnp.take_along_axis(got, src_tile[p], axis=1)
            num = jnp.take_along_axis(got, src_num[p], axis=1)
            new.append(sums[p] + jnp.where(num[None] == place_f, tile[None], 0.0))
        return tuple(new)

    sums = lax.fori_loop(
        0, N_REP, gather_one, tuple(jnp.zeros((8, TILE, 128), jnp.float32) for _ in range(3)),
        unroll=True,
    )
    update = left(inv_l, right([s.reshape(SPAN, 128) for s in sums], inv_r))
    fresh = []
    for p in range(3):
        square = jnp.sum(update[p] * update[p], axis=0, keepdims=True)
        low = wide[0:1] < SPAN
        mean_lo = jnp.sum(jnp.where(low, square, 0.0), axis=1, keepdims=True) / (SPAN * SPAN)
        mean_hi = jnp.sum(jnp.where(low, 0.0, square), axis=1, keepdims=True) / (SPAN * SPAN)
        spread = jnp.sqrt(jnp.where(low, mean_lo, mean_hi) + epsilon)
        fresh.append(weights[p] - step_size * update[p] / spread)
    unpair(outw, fresh)


def shards(activations, out_grad, momentum, weight, kept_tile):
    f32 = jnp.float32
    vm = pltpu.VMEM
    dma = pltpu.SemaphoreType.DMA
    return tuple(
        pl.pallas_call(
            kernel,
            out_shape=(
                pltpu.VMEM(momentum.shape, f32),
                pltpu.VMEM(weight.shape, f32),
            ),
            in_specs=[pl.BlockSpec(memory_space=pltpu.HBM)] * 7,
            out_specs=(pl.BlockSpec(memory_space=pltpu.VMEM),) * 2,
            scratch_shapes=[
                vm((TOK, COLS), jnp.bfloat16),
                vm((TOK, TOK), jnp.bfloat16),
                vm((5, SPAN, SPAN), f32),
                vm((5, SPAN, SPAN), f32),
                pltpu.SMEM((1, 5), jnp.int32),
                vm((128, 256), f32),
                vm((512, 256), f32),
                vm((128, 256), jnp.bfloat16),
                vm((512, 256), jnp.bfloat16),
                vm((2, N_ZLO, N_X, SLAB, 128), f32),
                vm((N_ZLO, N_X, SLAB, 128), f32),
                vm((4, 2, HALF, 128), f32),
                vm((4, 2, HALF, 128), f32),
                vm((4, 2, HALF, 128), f32),
                vm((3, SLAB, 128), f32),
                vm((TOK, 2 * TOK), jnp.bfloat16),
                vm((N_FSDP, 1, 128), jnp.int32),
                vm((N_FSDP, TILE // 2, 128), f32),
                vm((N_FSDP, TILE // 2, 128), f32),
                vm((N_REP, TILE // 2, 128), f32),
                dma((8,)),
                dma((16,)),
                dma((16,)),
                dma((24,)),
                dma((24,)),
                dma((3,)),
                dma((3,)),
                dma,
                dma,
                dma,
                dma,
                dma,
                dma,
                pltpu.SemaphoreType.REGULAR,
            ],
            compiler_params=pltpu.CompilerParams(
                collective_id=0, has_side_effects=True, vmem_limit_bytes=48 * 1024 * 1024
            ),
            name="demo_step",
        )(*(
            pltpu.with_memory_space_constraint(a, pltpu.HBM)
            for a in (activations, out_grad, momentum, weight, kept_tile, *map(jnp.asarray, tables()))
        ))
    )


def solution(mesh):
    placed = (
        P(("rep", "fsdp"), None),
        P(("rep", "fsdp"), None),
        P("rep", "fsdp", None, None),
        P("fsdp", None, None),
        P("rep", "fsdp"),
    )
    return jax.shard_map(
        shards,
        mesh=mesh,
        in_specs=placed,
        out_specs=(P("rep", "fsdp", None, None), P("fsdp", None, None)),
        check_vma=False,
    )
```

```python
import jax
import jax.numpy as jnp
import ml_dtypes
import numpy as np
from jax import lax
from jax.experimental import pallas as pl
from jax.experimental.pallas import tpu as pltpu
from jax.sharding import PartitionSpec as P

SPAN = 64
TILE = 8
N_X = 4
N_ZLO = 4
N_REP = 16
N_FSDP = 32
HUB = 1
SLAB = 160
HALF = SLAB // 2
TOK = 128
COLS = 5120
WIDE = 640
PARITY = 4 * WIDE

decay_rate = 0.9
step_size = 0.5
epsilon = 1e-06

MESH = pl.DeviceIdType.MESH


def tables():
    u = np.arange(SPAN, dtype=np.float64)[:, None]
    x = np.arange(SPAN, dtype=np.float64)[None, :]
    s = np.where(u == 0, np.sqrt(1.0 / SPAN), np.sqrt(2.0 / SPAN))
    basis = s * np.cos(np.pi * (2.0 * x + 1.0) * u / (2.0 * SPAN))
    zero = np.zeros((SPAN, SPAN))

    def halves(table):
        high = table.astype(ml_dtypes.bfloat16)
        return high, (table - high.astype(np.float64)).astype(ml_dtypes.bfloat16)

    def for_left(table):
        high, low = halves(np.concatenate([table, zero], 1))
        high, low = high[:, :SPAN], low[:, :SPAN]
        return np.concatenate([high, high, low, zero.astype(high.dtype)], 1)

    def for_right(table):
        high, low = halves(np.block([[table, zero], [zero, table]]))
        return np.block([[high, low], [high, np.zeros_like(low)]])

    lefts = np.concatenate([for_left(basis), for_left(basis.T)], 0)
    rights = np.concatenate([for_right(basis.T), for_right(basis)], 0)
    return lefts.astype(np.float32), rights.astype(np.float32)


def halve(a):
    high = a.astype(jnp.bfloat16)
    return high, (a - high.astype(jnp.float32)).astype(jnp.bfloat16)


def left(table, parts):
    high, low = halve(jnp.concatenate(parts, axis=1))
    data = jnp.concatenate([high, low, high], axis=0)
    wide = jnp.dot(table, data, preferred_element_type=jnp.float32)
    return [wide[:, 128 * p : 128 * p + 128] for p in range(3)]


def right(parts, table):
    high, low = halve(jnp.concatenate(parts, axis=0))
    tall = jnp.dot(jnp.concatenate([high, low], axis=1), table, preferred_element_type=jnp.float32)
    tall = tall[:, :128] + tall[:, 128:]
    return [tall[SPAN * p : SPAN * p + SPAN] for p in range(3)]


def wrap(i, n):
    return jnp.where(i >= n, i - n, i)


def kernel(
    acts_h, outg_h, mom_h, wt_h, kept_h, lefts_h, rights_h,
    outm, outw,
    acts, outg, mom, wt, kept, lefts32, rights32, lefts, rights,
    part, rx, x1, x0, x2, zr, turned, names, tmsg, tin, every,
    lsem, csend, crecv, xsend, xrecv, zsend, zrecv, nsend, nrecv, tsend, trecv, gsend, grecv, told,
):
    rep = lax.axis_index("rep")
    f = lax.axis_index("fsdp")
    core = lax.rem(f, 2)
    x = lax.rem(f // 2, N_X)
    z = f // (2 * N_X)
    other = 1 - core
    xr, xl, xo = lax.rem(x + 1, N_X), lax.rem(x + 3, N_X), lax.rem(x + 2, N_X)

    def at(z_, x_, core_):
        return (rep, (z_ * N_X + x_) * 2 + core_)

    piece = [lax.rem(z + d, N_ZLO) for d in (1, 3, 2)] + [z]

    first = lax.rem(z + 1, 2)
    load_acts = []
    for k in range(2):
        par = first if k == 0 else 1 - first
        cols = pl.ds(pl.multiple_of(par * PARITY, 128), PARITY)
        load_acts.append(pltpu.make_async_copy(acts_h.at[:, cols], acts.at[:, cols], lsem.at[k]))
    load_outg = pltpu.make_async_copy(outg_h, outg, lsem.at[2])
    load_outg.start()
    load_acts[0].start()
    load_acts[1].start()
    small = [
        pltpu.make_async_copy(src, dst, lsem.at[3 + i])
        for i, (src, dst) in enumerate(((mom_h.at[0], mom), (wt_h, wt), (kept_h, kept), (lefts_h, lefts32), (rights_h, rights32)))
    ]
    for copy in small:
        copy.start()

    barrier = pltpu.get_barrier_semaphore()

    def greet_group(i, carry):
        member = wrap(f + i, N_FSDP)

        @pl.when(member != HUB)
        def _():
            pl.semaphore_signal(barrier, inc=1, device_id=(rep, member), device_id_type=MESH)

        return carry

    def greet_peers(i, carry):
        pl.semaphore_signal(
            barrier, inc=1, device_id=(wrap(rep + i, N_REP), f), device_id_type=MESH
        )
        return carry

    lax.fori_loop(1, N_FSDP, greet_group, 0)

    lane = lax.broadcasted_iota(jnp.int32, (32, 128), 1)

    owners = [xo, xr, xl, x]

    def chunk(half, o, grads):
        par, j = (first if half == 0 else 1 - first), owners[o]
        base = pl.multiple_of(par * PARITY + j * WIDE, 128)
        prod = jnp.dot(grads, acts[:, pl.ds(base, WIDE)], preferred_element_type=jnp.float32)
        for h in range(2):
            blk = prod[SPAN * h : SPAN * h + SPAN]
            zz = 2 * h + par
            b2 = blk[:, 256:384]
            part[0, zz, j, 0:64] = blk[:, 0:128]
            part[0, zz, j, 64:128] = blk[:, 128:256]
            part[0, zz, j, 128:160] = jnp.where(lane < 64, b2[0:32], pltpu.roll(b2[32:64], 64, 1))
            part[1, zz, j, 0:64] = blk[:, 384:512]
            part[1, zz, j, 64:128] = blk[:, 512:640]
            part[1, zz, j, 128:160] = jnp.where(lane < 64, pltpu.roll(b2[0:32], 64, 1), b2[32:64])
        for k in (2 * half, 2 * half + 1):
            swap(k, o).start()

    def swap(k, o):
        return pltpu.make_async_remote_copy(
            src_ref=part.at[other, piece[k], owners[o]], dst_ref=rx.at[k, o],
            send_sem=csend.at[4 * k + o], recv_sem=crecv.at[4 * k + o],
            device_id=at(z, x, other), device_id_type=MESH,
        )

    A, B = pl.ds(0, HALF), pl.ds(HALF, HALF)

    def hop(k, kind, way):
        side = xr if way == 0 else xl
        slab = xo if kind == 1 else side
        rows = (B if way == 0 else A) if kind == 0 else (A if way == 0 else B)
        land = (x0, x1, x2)[kind]
        i = (k * 3 + kind) * 2 + way
        return pltpu.make_async_remote_copy(
            src_ref=part.at[core, piece[k], slab, rows], dst_ref=land.at[k, way],
            send_sem=xsend.at[i], recv_sem=xrecv.at[i],
            device_id=at(z, side, core), device_id_type=MESH,
        )

    def zhop(k):
        return pltpu.make_async_remote_copy(
            src_ref=part.at[core, piece[k], x], dst_ref=zr.at[k],
            send_sem=zsend.at[k], recv_sem=zrecv.at[k],
            device_id=at(piece[k], x, core), device_id_type=MESH,
        )

    def take(k, o):
        swap(k, o).wait_recv()
        slab = owners[o]
        part[core, piece[k], slab] = part[core, piece[k], slab] + rx[k, o]

    def open_far(k):
        take(k, 0)
        hop(k, 1, 0).start()
        hop(k, 1, 1).start()

    def open_near(k):
        for way in range(2):
            take(k, 1 + way)
            hop(k, 0, way).start()

    def pass_on(k):
        for way in range(2):
            hop(k, 1, way).wait_recv()
            side, rows = (xr, A) if way == 0 else (xl, B)
            part[core, piece[k], side, rows] = part[core, piece[k], side, rows] + x1[k, way]
            hop(k, 2, way).start()

    def close_piece(k):
        take(k, 3)
        for way in range(2):
            hop(k, 0, way).wait_recv()
            hop(k, 2, way).wait_recv()
        part[core, piece[k], x, A] = part[core, piece[k], x, A] + (x0[k, 1] + x2[k, 0])
        part[core, piece[k], x, B] = part[core, piece[k], x, B] + (x0[k, 0] + x2[k, 1])
        if k < 3:
            zhop(k).start()

    order = [core, core + 1, core + 2, core + 3, 4 * other]
    lane1 = lax.broadcasted_iota(jnp.int32, (1, 128), 1)
    lane4 = lax.broadcasted_iota(jnp.int32, (4, 128), 1)
    lane8 = lax.broadcasted_iota(jnp.int32, (TILE, 128), 1)
    wide = lax.broadcasted_iota(jnp.int32, (SPAN, 128), 1)
    row = lax.broadcasted_iota(jnp.int32, (SPAN, 128), 0)
    place = (row // TILE) * TILE + lax.rem(wide, SPAN) // TILE
    upper = jnp.where(lane8 < SPAN, 0, SPAN)
    block = lax.rem(lane8, SPAN) // TILE

    def to_group(src, dst, send, recv, i):
        return pltpu.make_async_remote_copy(
            src_ref=src, dst_ref=dst, send_sem=send, recv_sem=recv,
            device_id=(rep, wrap(f + i, N_FSDP)), device_id_type=MESH,
        )

    def to_peer(src, dst, send, recv, i):
        return pltpu.make_async_remote_copy(
            src_ref=src, dst_ref=dst, send_sem=send, recv_sem=recv,
            device_id=(wrap(rep + i, N_REP), f), device_id_type=MESH,
        )

    def send_names():
        mine = jnp.zeros((1, 128), jnp.int32)
        for s in range(5):
            mine = jnp.where(lane1 == s, kept[0, s], mine)
        names[f] = mine

        def one(i, carry):
            to_group(names.at[f], names.at[f], nsend, nrecv, i).start()
            return carry

        lax.fori_loop(1, N_FSDP, one, 0)

    def all_names():
        ref = names.at[pl.ds(0, N_FSDP - 1)]
        return to_group(ref, ref, nsend, nrecv, 1)

    def pick_columns(tile, number):
        source = (number & 7) * TILE + lax.rem(lane8, TILE) + upper
        return jnp.take_along_axis(tile, source, axis=1)

    def merge(a, b, c):
        return jnp.where(block == 0, a, jnp.where(block == 1, b, c))

    def pack(tiles):
        return jnp.where(lax.rem(lane4, SPAN) < 24, tiles[0:4], pltpu.roll(tiles[4:8], 24, 1))

    def unpack(four):
        return jnp.concatenate([four, pltpu.roll(four, 104, 1)], axis=0)

    def two_chunks(i, carry):
        numbers, rows = [], []
        for c in range(2):
            m = 2 * i + c
            piece_acts = acts[:, pl.ds(pl.multiple_of(m * WIDE, 128), WIDE)]
            both = jnp.dot(
                turned[...], jnp.concatenate([piece_acts, piece_acts], axis=0),
                preferred_element_type=jnp.float32,
            )
            for h in range(2):
                owner = ((2 * h + m // 4) * N_X + lax.rem(m, 4)) * 2
                low = jnp.broadcast_to(names[owner], (TILE, 128))
                high = jnp.broadcast_to(names[owner + 1], (TILE, 128))
                ten = jnp.where(lane8 < 5, low, pltpu.roll(high, 5, 1))
                for p in range(5):
                    number = jnp.take_along_axis(ten, 2 * p + jnp.where(lane8 < SPAN, 0, 1), axis=1)
                    high_part = number >> 3
                    found = both[SPAN * h : SPAN * h + TILE, 128 * p : 128 * p + 128]
                    for a in range(1, 8):
                        at_row = SPAN * h + TILE * a
                        found = jnp.where(
                            high_part == a, both[at_row : at_row + TILE, 128 * p : 128 * p + 128], found
                        )
                    numbers.append(number)
                    rows.append(found)
        high, low = halve(jnp.concatenate(rows, axis=0))
        out = jnp.dot(
            jnp.concatenate([high, low], axis=1), rights[0:256], preferred_element_type=jnp.float32
        )
        out = out[:, :128] + out[:, 128:]
        for c in range(2):
            m = 2 * i + c
            for h in range(2):
                owner = ((2 * h + m // 4) * N_X + lax.rem(m, 4)) * 2
                base = 10 * c + 5 * h
                t = [
                    pick_columns(out[TILE * q : TILE * q + TILE], numbers[q])
                    for q in range(base, base + 5)
                ]
                tmsg[owner] = pack(merge(t[0], t[1], t[2]))
                tmsg[owner + 1] = pack(merge(t[3], t[4], pltpu.roll(t[2], SPAN, 1)))
        return carry

    def send_tiles():
        tin[f] = tmsg[f]

        def one(i, carry):
            to_group(tmsg.at[wrap(f + i, N_FSDP)], tin.at[f], tsend, trecv, i).start()
            return carry

        lax.fori_loop(1, N_FSDP, one, 0)

    def all_tiles():
        span = pl.ds(0, N_FSDP - 1)
        return to_group(tmsg.at[span], tin.at[span], tsend, trecv, 1)

    def pairs(ref):
        zero = jnp.zeros((SPAN, SPAN), jnp.float32)
        return [
            jnp.concatenate([ref[order[0]], ref[order[1]]], axis=1),
            jnp.concatenate([ref[order[2]], ref[order[3]]], axis=1),
            jnp.concatenate([ref[order[4]], zero], axis=1),
        ]

    def unpair(ref, parts):
        for j in range(5):
            half = parts[j // 2][:, SPAN * (j % 2) : SPAN * (j % 2) + SPAN]
            ref[order[j]] = half

    @pl.when(f != HUB)
    def _():
        pl.semaphore_wait(barrier, N_FSDP - 1)

    @pl.when(f == HUB - 1)
    def _():
        pl.semaphore_signal(told, inc=1, device_id=(rep, HUB), device_id_type=MESH)

    @pl.when(f == HUB)
    def _():
        pl.semaphore_wait(told, 1)
        lax.fori_loop(1, N_REP, greet_peers, 0)

    small[2].wait()
    send_names()
    load_outg.wait()
    flat = outg[...]
    grads = flat.astype(jnp.float32).T.astype(jnp.bfloat16)
    load_acts[0].wait()
    for o in range(3):
        chunk(0, o, grads)
    for i in (0, 1, 3, 4):
        small[i].wait()
    lefts[...] = lefts32[...].astype(jnp.bfloat16)
    rights[...] = rights32[...].astype(jnp.bfloat16)
    fwd_l, inv_l = lefts[0:64, 0:192], lefts[64:128, 0:192]
    fwd_r, inv_r = rights[0:256], rights[256:512]
    spun = jnp.dot(flat, rights[0:128], preferred_element_type=jnp.float32)
    spun_high, spun_low = halve((spun[:, :128] + spun[:, 128:]).T)
    turned[:, :128] = spun_high
    turned[:, 128:] = spun_low
    chunk(0, 3, grads)
    open_far(0)
    open_far(1)
    open_near(0)
    open_near(1)
    load_acts[1].wait()
    all_names().wait_recv()
    lax.fori_loop(0, 4, two_chunks, 0)
    send_tiles()

    def tell(i, carry):
        member = wrap(f + i, N_FSDP)
        pl.semaphore_signal(told, inc=1, device_id=(rep, member), device_id_type=MESH)
        return carry

    def second_half():
        pass_on(0)
        pass_on(1)
        chunk(1, 2, grads)
        chunk(1, 3, grads)
        open_far(2)
        open_far(3)
        open_near(2)
        open_near(3)

    chunk(1, 0, grads)
    chunk(1, 1, grads)
    pl.when(rep < N_REP // 4)(second_half)

    @pl.when(f == HUB)
    def _():
        pl.semaphore_wait(barrier, N_REP - 1)
        lax.fori_loop(1, N_FSDP, tell, 0)

    scalars = [kept[0, s] for s in order]
    carried = [decay_rate * m for m in pairs(mom)]
    own = [
        jnp.where(wide < SPAN, scalars[2 * p], scalars[min(2 * p + 1, 4)]) for p in range(3)
    ]
    coef = right(left(fwd_l, carried), fwd_r)
    found = [
        pick_columns(
            jnp.sum(jnp.where(place == own[p], coef[p], 0.0).reshape(8, TILE, 128), axis=0), own[p][0:8]
        )
        for p in range(3)
    ]
    from_momentum = merge(*found)

    all_tiles().wait_recv()
    tiles = from_momentum + unpack(jnp.sum(tin[...], axis=0))
    message = pack(tiles)
    for j in range(5):
        spot = (lane4 == 56 + j) | (lane4 == 80 + j)
        message = jnp.where(spot, scalars[j].astype(jnp.float32), message)
    every[rep] = message

    @pl.when(f != HUB)
    def _():
        pl.semaphore_wait(told, 1)

    def send_one(i, carry):
        to_peer(every.at[rep], every.at[rep], gsend, grecv, i).start()
        return carry

    lax.fori_loop(1, N_REP, send_one, 0)

    def all_posts():
        ref = every.at[pl.ds(0, N_REP - 1)]
        return to_peer(ref, ref, gsend, grecv, 1)

    pl.when(rep >= N_REP // 4)(second_half)
    pass_on(2)
    close_piece(0)
    pass_on(3)
    close_piece(1)
    close_piece(2)
    src_tile = [upper + TILE * p + lax.rem(lane8, TILE) for p in range(3)]
    src_num = [56 + jnp.where(lane8 < SPAN, 2 * p, min(2 * p + 1, 4)) for p in range(3)]

    def spread_out(p):
        tile = jnp.take_along_axis(tiles, src_tile[p], axis=1)
        tall = jnp.broadcast_to(tile[None], (8, TILE, 128)).reshape(SPAN, 128)
        return jnp.where(place == own[p], tall, 0.0)

    decoded = left(inv_l, right([spread_out(p) for p in range(3)], inv_r))
    for p in range(3):
        carried[p] = carried[p] - decoded[p]
    weights = pairs(wt)
    close_piece(3)
    total = part[core, z, x]
    tail = jnp.concatenate([total[128:160], pltpu.roll(total[128:160], 64, 1)], axis=0)
    for p, grown in enumerate((total[0:64], total[64:128], tail)):
        carried[p] = carried[p] + grown
    for k in range(4):
        for o in range(4):
            swap(k, o).wait_send()
        for kind in range(3):
            for way in range(2):
                hop(k, kind, way).wait_send()
    for k in range(3):
        zhop(k).wait()
    rest = zr[0] + zr[1] + zr[2]
    tail = jnp.concatenate([rest[128:160], pltpu.roll(rest[128:160], 64, 1)], axis=0)
    unpair(outm.at[0], [carried[0] + rest[0:64], carried[1] + rest[64:128], carried[2] + tail])
    all_names().wait_send()
    all_tiles().wait_send()
    all_posts().wait_send()
    all_posts().wait_recv()

    place_f = place.astype(jnp.float32).reshape(8, TILE, 128)

    def gather_one(g, sums):
        got = unpack(every[g])
        new = []
        for p in range(3):
            tile = jnp.take_along_axis(got, src_tile[p], axis=1)
            num = jnp.take_along_axis(got, src_num[p], axis=1)
            new.append(sums[p] + jnp.where(num[None] == place_f, tile[None], 0.0))
        return tuple(new)

    sums = lax.fori_loop(
        0, N_REP, gather_one, tuple(jnp.zeros((8, TILE, 128), jnp.float32) for _ in range(3)),
        unroll=True,
    )
    update = left(inv_l, right([s.reshape(SPAN, 128) for s in sums], inv_r))
    fresh = []
    for p in range(3):
        square = jnp.sum(update[p] * update[p], axis=0, keepdims=True)
        low = wide[0:1] < SPAN
        mean_lo = jnp.sum(jnp.where(low, square, 0.0), axis=1, keepdims=True) / (SPAN * SPAN)
        mean_hi = jnp.sum(jnp.where(low, 0.0, square), axis=1, keepdims=True) / (SPAN * SPAN)
        spread = jnp.sqrt(jnp.where(low, mean_lo, mean_hi) + epsilon)
        fresh.append(weights[p] - step_size * update[p] / spread)
    unpair(outw, fresh)


def shards(activations, out_grad, momentum, weight, kept_tile):
    f32 = jnp.float32
    vm = pltpu.VMEM
    dma = pltpu.SemaphoreType.DMA
    return tuple(
        pl.pallas_call(
            kernel,
            out_shape=(
                pltpu.VMEM(momentum.shape, f32),
                pltpu.VMEM(weight.shape, f32),
            ),
            in_specs=[pl.BlockSpec(memory_space=pltpu.HBM)] * 7,
            out_specs=(pl.BlockSpec(memory_space=pltpu.VMEM),) * 2,
            scratch_shapes=[
                vm((TOK, COLS), jnp.bfloat16),
                vm((TOK, TOK), jnp.bfloat16),
                vm((5, SPAN, SPAN), f32),
                vm((5, SPAN, SPAN), f32),
                pltpu.SMEM((1, 5), jnp.int32),
                vm((128, 256), f32),
                vm((512, 256), f32),
                vm((128, 256), jnp.bfloat16),
                vm((512, 256), jnp.bfloat16),
                vm((2, N_ZLO, N_X, SLAB, 128), f32),
                vm((N_ZLO, N_X, SLAB, 128), f32),
                vm((4, 2, HALF, 128), f32),
                vm((4, 2, HALF, 128), f32),
                vm((4, 2, HALF, 128), f32),
                vm((3, SLAB, 128), f32),
                vm((TOK, 2 * TOK), jnp.bfloat16),
                vm((N_FSDP, 1, 128), jnp.int32),
                vm((N_FSDP, TILE // 2, 128), f32),
                vm((N_FSDP, TILE // 2, 128), f32),
                vm((N_REP, TILE // 2, 128), f32),
                dma((8,)),
                dma((16,)),
                dma((16,)),
                dma((24,)),
                dma((24,)),
                dma((3,)),
                dma((3,)),
                dma,
                dma,
                dma,
                dma,
                dma,
                dma,
                pltpu.SemaphoreType.REGULAR,
            ],
            compiler_params=pltpu.CompilerParams(
                collective_id=0, has_side_effects=True, vmem_limit_bytes=48 * 1024 * 1024
            ),
            name="demo_step",
        )(*(
            pltpu.with_memory_space_constraint(a, pltpu.HBM)
            for a in (activations, out_grad, momentum, weight, kept_tile, *map(jnp.asarray, tables()))
        ))
    )


def solution(mesh):
    placed = (
        P(("rep", "fsdp"), None),
        P(("rep", "fsdp"), None),
        P("rep", "fsdp", None, None),
        P("fsdp", None, None),
        P("rep", "fsdp"),
    )
    return jax.shard_map(
        shards,
        mesh=mesh,
        in_specs=placed,
        out_specs=(P("rep", "fsdp", None, None), P("fsdp", None, None)),
        check_vma=False,
    )
```

```python
import jax
import jax.numpy as jnp
import ml_dtypes
import numpy as np
from jax import lax
from jax.experimental import pallas as pl
from jax.experimental.pallas import tpu as pltpu
from jax.sharding import PartitionSpec as P

SPAN = 64
TILE = 8
N_X = 4
N_ZLO = 4
N_REP = 16
N_FSDP = 32
HUB = 1
SLAB = 160
HALF = SLAB // 2
TOK = 128
COLS = 5120
WIDE = 640
PARITY = 4 * WIDE

decay_rate = 0.9
step_size = 0.5
epsilon = 1e-06

MESH = pl.DeviceIdType.MESH


def tables():
    u = np.arange(SPAN, dtype=np.float64)[:, None]
    x = np.arange(SPAN, dtype=np.float64)[None, :]
    s = np.where(u == 0, np.sqrt(1.0 / SPAN), np.sqrt(2.0 / SPAN))
    basis = s * np.cos(np.pi * (2.0 * x + 1.0) * u / (2.0 * SPAN))
    zero = np.zeros((SPAN, SPAN))

    def halves(table):
        high = table.astype(ml_dtypes.bfloat16)
        return high, (table - high.astype(np.float64)).astype(ml_dtypes.bfloat16)

    def for_left(table):
        high, low = halves(np.concatenate([table, zero], 1))
        high, low = high[:, :SPAN], low[:, :SPAN]
        return np.concatenate([high, high, low, zero.astype(high.dtype)], 1)

    def for_right(table):
        high, low = halves(np.block([[table, zero], [zero, table]]))
        return np.block([[high, low], [high, np.zeros_like(low)]])

    lefts = np.concatenate([for_left(basis), for_left(basis.T)], 0)
    rights = np.concatenate([for_right(basis.T), for_right(basis)], 0)
    return lefts.astype(np.float32), rights.astype(np.float32)


def halve(a):
    high = a.astype(jnp.bfloat16)
    return high, (a - high.astype(jnp.float32)).astype(jnp.bfloat16)


def left(table, parts):
    high, low = halve(jnp.concatenate(parts, axis=1))
    data = jnp.concatenate([high, low, high], axis=0)
    wide = jnp.dot(table, data, preferred_element_type=jnp.float32)
    return [wide[:, 128 * p : 128 * p + 128] for p in range(3)]


def right(parts, table):
    high, low = halve(jnp.concatenate(parts, axis=0))
    tall = jnp.dot(jnp.concatenate([high, low], axis=1), table, preferred_element_type=jnp.float32)
    tall = tall[:, :128] + tall[:, 128:]
    return [tall[SPAN * p : SPAN * p + SPAN] for p in range(3)]


def wrap(i, n):
    return jnp.where(i >= n, i - n, i)


def kernel(
    acts_h, outg_h, mom_h, wt_h, kept_h, lefts_h, rights_h,
    outm, outw,
    acts, outg, mom, wt, kept, lefts32, rights32, lefts, rights,
    part, rx, x1, x0, x2, zr, turned, names, tmsg, tin, every,
    lsem, csend, crecv, xsend, xrecv, zsend, zrecv, nsend, nrecv, tsend, trecv, gsend, grecv, told,
):
    rep = lax.axis_index("rep")
    f = lax.axis_index("fsdp")
    core = lax.rem(f, 2)
    x = lax.rem(f // 2, N_X)
    z = f // (2 * N_X)
    other = 1 - core
    xr, xl, xo = lax.rem(x + 1, N_X), lax.rem(x + 3, N_X), lax.rem(x + 2, N_X)

    def at(z_, x_, core_):
        return (rep, (z_ * N_X + x_) * 2 + core_)

    piece = [lax.rem(z + d, N_ZLO) for d in (1, 3, 2)] + [z]

    first = lax.rem(z + 1, 2)
    load_acts = []
    for k in range(2):
        par = first if k == 0 else 1 - first
        cols = pl.ds(pl.multiple_of(par * PARITY, 128), PARITY)
        load_acts.append(pltpu.make_async_copy(acts_h.at[:, cols], acts.at[:, cols], lsem.at[k]))
    load_outg = pltpu.make_async_copy(outg_h, outg, lsem.at[2])
    load_outg.start()
    load_acts[0].start()
    load_acts[1].start()
    small = [
        pltpu.make_async_copy(src, dst, lsem.at[3 + i])
        for i, (src, dst) in enumerate(((mom_h.at[0], mom), (wt_h, wt), (kept_h, kept), (lefts_h, lefts32), (rights_h, rights32)))
    ]
    for copy in small:
        copy.start()

    barrier = pltpu.get_barrier_semaphore()

    def greet_group(i, carry):
        member = wrap(f + i, N_FSDP)

        @pl.when(member != HUB)
        def _():
            pl.semaphore_signal(barrier, inc=1, device_id=(rep, member), device_id_type=MESH)

        return carry

    def greet_peers(i, carry):
        pl.semaphore_signal(
            barrier, inc=1, device_id=(wrap(rep + i, N_REP), f), device_id_type=MESH
        )
        return carry

    lax.fori_loop(1, N_FSDP, greet_group, 0)

    lane = lax.broadcasted_iota(jnp.int32, (32, 128), 1)

    owners = [xo, xr, xl, x]

    def chunk(half, o, grads):
        par, j = (first if half == 0 else 1 - first), owners[o]
        base = pl.multiple_of(par * PARITY + j * WIDE, 128)
        prod = jnp.dot(grads, acts[:, pl.ds(base, WIDE)], preferred_element_type=jnp.float32)
        for h in range(2):
            blk = prod[SPAN * h : SPAN * h + SPAN]
            zz = 2 * h + par
            b2 = blk[:, 256:384]
            part[0, zz, j, 0:64] = blk[:, 0:128]
            part[0, zz, j, 64:128] = blk[:, 128:256]
            part[0, zz, j, 128:160] = jnp.where(lane < 64, b2[0:32], pltpu.roll(b2[32:64], 64, 1))
            part[1, zz, j, 0:64] = blk[:, 384:512]
            part[1, zz, j, 64:128] = blk[:, 512:640]
            part[1, zz, j, 128:160] = jnp.where(lane < 64, pltpu.roll(b2[0:32], 64, 1), b2[32:64])
        for k in (2 * half, 2 * half + 1):
            swap(k, o).start()

    def swap(k, o):
        return pltpu.make_async_remote_copy(
            src_ref=part.at[other, piece[k], owners[o]], dst_ref=rx.at[k, o],
            send_sem=csend.at[4 * k + o], recv_sem=crecv.at[4 * k + o],
            device_id=at(z, x, other), device_id_type=MESH,
        )

    A, B = pl.ds(0, HALF), pl.ds(HALF, HALF)

    def hop(k, kind, way):
        side = xr if way == 0 else xl
        slab = xo if kind == 1 else side
        rows = (B if way == 0 else A) if kind == 0 else (A if way == 0 else B)
        land = (x0, x1, x2)[kind]
        i = (k * 3 + kind) * 2 + way
        return pltpu.make_async_remote_copy(
            src_ref=part.at[core, piece[k], slab, rows], dst_ref=land.at[k, way],
            send_sem=xsend.at[i], recv_sem=xrecv.at[i],
            device_id=at(z, side, core), device_id_type=MESH,
        )

    def zhop(k):
        return pltpu.make_async_remote_copy(
            src_ref=part.at[core, piece[k], x], dst_ref=zr.at[k],
            send_sem=zsend.at[k], recv_sem=zrecv.at[k],
            device_id=at(piece[k], x, core), device_id_type=MESH,
        )

    def take(k, o):
        swap(k, o).wait_recv()
        slab = owners[o]
        part[core, piece[k], slab] = part[core, piece[k], slab] + rx[k, o]

    def open_far(k):
        take(k, 0)
        hop(k, 1, 0).start()
        hop(k, 1, 1).start()

    def open_near(k):
        for way in range(2):
            take(k, 1 + way)
            hop(k, 0, way).start()

    def pass_on(k):
        for way in range(2):
            hop(k, 1, way).wait_recv()
            side, rows = (xr, A) if way == 0 else (xl, B)
            part[core, piece[k], side, rows] = part[core, piece[k], side, rows] + x1[k, way]
            hop(k, 2, way).start()

    def close_piece(k):
        take(k, 3)
        for way in range(2):
            hop(k, 0, way).wait_recv()
            hop(k, 2, way).wait_recv()
        part[core, piece[k], x, A] = part[core, piece[k], x, A] + (x0[k, 1] + x2[k, 0])
        part[core, piece[k], x, B] = part[core, piece[k], x, B] + (x0[k, 0] + x2[k, 1])
        if k < 3:
            zhop(k).start()

    order = [core, core + 1, core + 2, core + 3, 4 * other]
    lane1 = lax.broadcasted_iota(jnp.int32, (1, 128), 1)
    lane4 = lax.broadcasted_iota(jnp.int32, (4, 128), 1)
    lane8 = lax.broadcasted_iota(jnp.int32, (TILE, 128), 1)
    wide = lax.broadcasted_iota(jnp.int32, (SPAN, 128), 1)
    row = lax.broadcasted_iota(jnp.int32, (SPAN, 128), 0)
    place = (row // TILE) * TILE + lax.rem(wide, SPAN) // TILE
    upper = jnp.where(lane8 < SPAN, 0, SPAN)
    block = lax.rem(lane8, SPAN) // TILE

    def to_group(src, dst, send, recv, i):
        return pltpu.make_async_remote_copy(
            src_ref=src, dst_ref=dst, send_sem=send, recv_sem=recv,
            device_id=(rep, wrap(f + i, N_FSDP)), device_id_type=MESH,
        )

    def to_peer(src, dst, send, recv, i):
        return pltpu.make_async_remote_copy(
            src_ref=src, dst_ref=dst, send_sem=send, recv_sem=recv,
            device_id=(wrap(rep + i, N_REP), f), device_id_type=MESH,
        )

    def send_names():
        mine = jnp.zeros((1, 128), jnp.int32)
        for s in range(5):
            mine = jnp.where(lane1 == s, kept[0, s], mine)
        names[f] = mine

        def one(i, carry):
            to_group(names.at[f], names.at[f], nsend, nrecv, i).start()
            return carry

        lax.fori_loop(1, N_FSDP, one, 0)

    def all_names():
        ref = names.at[pl.ds(0, N_FSDP - 1)]
        return to_group(ref, ref, nsend, nrecv, 1)

    def pick_columns(tile, number):
        source = (number & 7) * TILE + lax.rem(lane8, TILE) + upper
        return jnp.take_along_axis(tile, source, axis=1)

    def merge(a, b, c):
        return jnp.where(block == 0, a, jnp.where(block == 1, b, c))

    def pack(tiles):
        return jnp.where(lax.rem(lane4, SPAN) < 24, tiles[0:4], pltpu.roll(tiles[4:8], 24, 1))

    def unpack(four):
        return jnp.concatenate([four, pltpu.roll(four, 104, 1)], axis=0)

    def two_chunks(i, carry):
        numbers, rows = [], []
        for c in range(2):
            m = 2 * i + c
            piece_acts = acts[:, pl.ds(pl.multiple_of(m * WIDE, 128), WIDE)]
            both = jnp.dot(
                turned[...], jnp.concatenate([piece_acts, piece_acts], axis=0),
                preferred_element_type=jnp.float32,
            )
            for h in range(2):
                owner = ((2 * h + m // 4) * N_X + lax.rem(m, 4)) * 2
                low = jnp.broadcast_to(names[owner], (TILE, 128))
                high = jnp.broadcast_to(names[owner + 1], (TILE, 128))
                ten = jnp.where(lane8 < 5, low, pltpu.roll(high, 5, 1))
                for p in range(5):
                    number = jnp.take_along_axis(ten, 2 * p + jnp.where(lane8 < SPAN, 0, 1), axis=1)
                    high_part = number >> 3
                    found = both[SPAN * h : SPAN * h + TILE, 128 * p : 128 * p + 128]
                    for a in range(1, 8):
                        at_row = SPAN * h + TILE * a
                        found = jnp.where(
                            high_part == a, both[at_row : at_row + TILE, 128 * p : 128 * p + 128], found
                        )
                    numbers.append(number)
                    rows.append(found)
        high, low = halve(jnp.concatenate(rows, axis=0))
        out = jnp.dot(
            jnp.concatenate([high, low], axis=1), rights[0:256], preferred_element_type=jnp.float32
        )
        out = out[:, :128] + out[:, 128:]
        for c in range(2):
            m = 2 * i + c
            for h in range(2):
                owner = ((2 * h + m // 4) * N_X + lax.rem(m, 4)) * 2
                base = 10 * c + 5 * h
                t = [
                    pick_columns(out[TILE * q : TILE * q + TILE], numbers[q])
                    for q in range(base, base + 5)
                ]
                tmsg[owner] = pack(merge(t[0], t[1], t[2]))
                tmsg[owner + 1] = pack(merge(t[3], t[4], pltpu.roll(t[2], SPAN, 1)))
        return carry

    def send_tiles():
        tin[f] = tmsg[f]

        def one(i, carry):
            to_group(tmsg.at[wrap(f + i, N_FSDP)], tin.at[f], tsend, trecv, i).start()
            return carry

        lax.fori_loop(1, N_FSDP, one, 0)

    def all_tiles():
        span = pl.ds(0, N_FSDP - 1)
        return to_group(tmsg.at[span], tin.at[span], tsend, trecv, 1)

    def pairs(ref):
        zero = jnp.zeros((SPAN, SPAN), jnp.float32)
        return [
            jnp.concatenate([ref[order[0]], ref[order[1]]], axis=1),
            jnp.concatenate([ref[order[2]], ref[order[3]]], axis=1),
            jnp.concatenate([ref[order[4]], zero], axis=1),
        ]

    def unpair(ref, parts):
        for j in range(5):
            half = parts[j // 2][:, SPAN * (j % 2) : SPAN * (j % 2) + SPAN]
            ref[order[j]] = half

    @pl.when(f != HUB)
    def _():
        pl.semaphore_wait(barrier, N_FSDP - 1)

    @pl.when(f == HUB - 1)
    def _():
        pl.semaphore_signal(told, inc=1, device_id=(rep, HUB), device_id_type=MESH)

    @pl.when(f == HUB)
    def _():
        pl.semaphore_wait(told, 1)
        lax.fori_loop(1, N_REP, greet_peers, 0)

    small[2].wait()
    send_names()
    load_outg.wait()
    flat = outg[...]
    grads = flat.astype(jnp.float32).T.astype(jnp.bfloat16)
    load_acts[0].wait()
    for o in range(3):
        chunk(0, o, grads)
    for i in (0, 1, 3, 4):
        small[i].wait()
    lefts[...] = lefts32[...].astype(jnp.bfloat16)
    rights[...] = rights32[...].astype(jnp.bfloat16)
    fwd_l, inv_l = lefts[0:64, 0:192], lefts[64:128, 0:192]
    fwd_r, inv_r = rights[0:256], rights[256:512]
    spun = jnp.dot(flat, rights[0:128], preferred_element_type=jnp.float32)
    spun_high, spun_low = halve((spun[:, :128] + spun[:, 128:]).T)
    turned[:, :128] = spun_high
    turned[:, 128:] = spun_low
    chunk(0, 3, grads)
    open_far(0)
    open_far(1)
    open_near(0)
    open_near(1)
    load_acts[1].wait()
    early = rep < N_REP // 4

    @pl.when(early)
    def _():
        for o in range(4):
            chunk(1, o, grads)
        open_far(2)
        open_far(3)
        open_near(2)
        open_near(3)

    all_names().wait_recv()
    lax.fori_loop(0, 2, two_chunks, 0)

    @pl.when(early)
    def _():
        pass_on(0)
        pass_on(1)

    lax.fori_loop(2, 4, two_chunks, 0)
    send_tiles()

    @pl.when(early)
    def _():
        pass_on(2)
        close_piece(0)
        pass_on(3)
        close_piece(1)
        close_piece(2)

    @pl.when(jnp.logical_not(early))
    def _():
        chunk(1, 0, grads)
        chunk(1, 1, grads)

    def tell(i, carry):
        member = wrap(f + i, N_FSDP)
        pl.semaphore_signal(told, inc=1, device_id=(rep, member), device_id_type=MESH)
        return carry

    @pl.when(f == HUB)
    def _():
        pl.semaphore_wait(barrier, N_REP - 1)
        lax.fori_loop(1, N_FSDP, tell, 0)

    scalars = [kept[0, s] for s in order]
    carried = [decay_rate * m for m in pairs(mom)]
    own = [
        jnp.where(wide < SPAN, scalars[2 * p], scalars[min(2 * p + 1, 4)]) for p in range(3)
    ]
    coef = right(left(fwd_l, carried), fwd_r)
    found = [
        pick_columns(
            jnp.sum(jnp.where(place == own[p], coef[p], 0.0).reshape(8, TILE, 128), axis=0), own[p][0:8]
        )
        for p in range(3)
    ]
    from_momentum = merge(*found)

    all_tiles().wait_recv()
    tiles = from_momentum + unpack(jnp.sum(tin[...], axis=0))
    message = pack(tiles)
    for j in range(5):
        spot = (lane4 == 56 + j) | (lane4 == 80 + j)
        message = jnp.where(spot, scalars[j].astype(jnp.float32), message)
    every[rep] = message

    @pl.when(f != HUB)
    def _():
        pl.semaphore_wait(told, 1)

    def send_one(i, carry):
        to_peer(every.at[rep], every.at[rep], gsend, grecv, i).start()
        return carry

    lax.fori_loop(1, N_REP, send_one, 0)

    def all_posts():
        ref = every.at[pl.ds(0, N_REP - 1)]
        return to_peer(ref, ref, gsend, grecv, 1)

    @pl.when(jnp.logical_not(early))
    def _():
        pass_on(0)
        pass_on(1)
        chunk(1, 2, grads)
        chunk(1, 3, grads)
        open_far(2)
        open_far(3)
        open_near(2)
        open_near(3)
        pass_on(2)
        close_piece(0)
        pass_on(3)
        close_piece(1)
        close_piece(2)

    src_tile = [upper + TILE * p + lax.rem(lane8, TILE) for p in range(3)]
    src_num = [56 + jnp.where(lane8 < SPAN, 2 * p, min(2 * p + 1, 4)) for p in range(3)]

    def spread_out(p):
        tile = jnp.take_along_axis(tiles, src_tile[p], axis=1)
        tall = jnp.broadcast_to(tile[None], (8, TILE, 128)).reshape(SPAN, 128)
        return jnp.where(place == own[p], tall, 0.0)

    decoded = left(inv_l, right([spread_out(p) for p in range(3)], inv_r))
    for p in range(3):
        carried[p] = carried[p] - decoded[p]
    weights = pairs(wt)
    close_piece(3)
    total = part[core, z, x]
    tail = jnp.concatenate([total[128:160], pltpu.roll(total[128:160], 64, 1)], axis=0)
    for p, grown in enumerate((total[0:64], total[64:128], tail)):
        carried[p] = carried[p] + grown
    for k in range(4):
        for o in range(4):
            swap(k, o).wait_send()
        for kind in range(3):
            for way in range(2):
                hop(k, kind, way).wait_send()
    for k in range(3):
        zhop(k).wait()
    rest = zr[0] + zr[1] + zr[2]
    tail = jnp.concatenate([rest[128:160], pltpu.roll(rest[128:160], 64, 1)], axis=0)
    unpair(outm.at[0], [carried[0] + rest[0:64], carried[1] + rest[64:128], carried[2] + tail])
    all_names().wait_send()
    all_tiles().wait_send()
    all_posts().wait_send()
    all_posts().wait_recv()

    place_f = place.astype(jnp.float32).reshape(8, TILE, 128)

    def gather_one(g, sums):
        got = unpack(every[g])
        new = []
        for p in range(3):
            tile = jnp.take_along_axis(got, src_tile[p], axis=1)
            num = jnp.take_along_axis(got, src_num[p], axis=1)
            new.append(sums[p] + jnp.where(num[None] == place_f, tile[None], 0.0))
        return tuple(new)

    sums = lax.fori_loop(
        0, N_REP, gather_one, tuple(jnp.zeros((8, TILE, 128), jnp.float32) for _ in range(3)),
        unroll=True,
    )
    update = left(inv_l, right([s.reshape(SPAN, 128) for s in sums], inv_r))
    fresh = []
    for p in range(3):
        square = jnp.sum(update[p] * update[p], axis=0, keepdims=True)
        low = wide[0:1] < SPAN
        mean_lo = jnp.sum(jnp.where(low, square, 0.0), axis=1, keepdims=True) / (SPAN * SPAN)
        mean_hi = jnp.sum(jnp.where(low, 0.0, square), axis=1, keepdims=True) / (SPAN * SPAN)
        spread = jnp.sqrt(jnp.where(low, mean_lo, mean_hi) + epsilon)
        fresh.append(weights[p] - step_size * update[p] / spread)
    unpair(outw, fresh)


def shards(activations, out_grad, momentum, weight, kept_tile):
    f32 = jnp.float32
    vm = pltpu.VMEM
    dma = pltpu.SemaphoreType.DMA
    return tuple(
        pl.pallas_call(
            kernel,
            out_shape=(
                pltpu.VMEM(momentum.shape, f32),
                pltpu.VMEM(weight.shape, f32),
            ),
            in_specs=[pl.BlockSpec(memory_space=pltpu.HBM)] * 7,
            out_specs=(pl.BlockSpec(memory_space=pltpu.VMEM),) * 2,
            scratch_shapes=[
                vm((TOK, COLS), jnp.bfloat16),
                vm((TOK, TOK), jnp.bfloat16),
                vm((5, SPAN, SPAN), f32),
                vm((5, SPAN, SPAN), f32),
                pltpu.SMEM((1, 5), jnp.int32),
                vm((128, 256), f32),
                vm((512, 256), f32),
                vm((128, 256), jnp.bfloat16),
                vm((512, 256), jnp.bfloat16),
                vm((2, N_ZLO, N_X, SLAB, 128), f32),
                vm((N_ZLO, N_X, SLAB, 128), f32),
                vm((4, 2, HALF, 128), f32),
                vm((4, 2, HALF, 128), f32),
                vm((4, 2, HALF, 128), f32),
                vm((3, SLAB, 128), f32),
                vm((TOK, 2 * TOK), jnp.bfloat16),
                vm((N_FSDP, 1, 128), jnp.int32),
                vm((N_FSDP, TILE // 2, 128), f32),
                vm((N_FSDP, TILE // 2, 128), f32),
                vm((N_REP, TILE // 2, 128), f32),
                dma((8,)),
                dma((16,)),
                dma((16,)),
                dma((24,)),
                dma((24,)),
                dma((3,)),
                dma((3,)),
                dma,
                dma,
                dma,
                dma,
                dma,
                dma,
                pltpu.SemaphoreType.REGULAR,
            ],
            compiler_params=pltpu.CompilerParams(
                collective_id=0, has_side_effects=True, vmem_limit_bytes=48 * 1024 * 1024
            ),
            name="demo_step",
        )(*(
            pltpu.with_memory_space_constraint(a, pltpu.HBM)
            for a in (activations, out_grad, momentum, weight, kept_tile, *map(jnp.asarray, tables()))
        ))
    )


def solution(mesh):
    placed = (
        P(("rep", "fsdp"), None),
        P(("rep", "fsdp"), None),
        P("rep", "fsdp", None, None),
        P("fsdp", None, None),
        P("rep", "fsdp"),
    )
    return jax.shard_map(
        shards,
        mesh=mesh,
        in_specs=placed,
        out_specs=(P("rep", "fsdp", None, None), P("fsdp", None, None)),
        check_vma=False,
    )
```

```python
import jax
import jax.numpy as jnp
import ml_dtypes
import numpy as np
from jax import lax
from jax.experimental import pallas as pl
from jax.experimental.pallas import tpu as pltpu
from jax.sharding import PartitionSpec as P

SPAN = 64
TILE = 8
N_X = 4
N_ZLO = 4
N_REP = 16
N_FSDP = 32
HUB = 1
SLAB = 160
HALF = SLAB // 2
TOK = 128
COLS = 5120
WIDE = 640
PARITY = 4 * WIDE

decay_rate = 0.9
step_size = 0.5
epsilon = 1e-06

MESH = pl.DeviceIdType.MESH


def tables():
    u = np.arange(SPAN, dtype=np.float64)[:, None]
    x = np.arange(SPAN, dtype=np.float64)[None, :]
    s = np.where(u == 0, np.sqrt(1.0 / SPAN), np.sqrt(2.0 / SPAN))
    basis = s * np.cos(np.pi * (2.0 * x + 1.0) * u / (2.0 * SPAN))
    zero = np.zeros((SPAN, SPAN))

    def halves(table):
        high = table.astype(ml_dtypes.bfloat16)
        return high, (table - high.astype(np.float64)).astype(ml_dtypes.bfloat16)

    def for_left(table):
        high, low = halves(np.concatenate([table, zero], 1))
        high, low = high[:, :SPAN], low[:, :SPAN]
        return np.concatenate([high, high, low, zero.astype(high.dtype)], 1)

    def for_right(table):
        high, low = halves(np.block([[table, zero], [zero, table]]))
        return np.block([[high, low], [high, np.zeros_like(low)]])

    lefts = np.concatenate([for_left(basis), for_left(basis.T)], 0)
    rights = np.concatenate([for_right(basis.T), for_right(basis)], 0)
    return lefts.astype(np.float32), rights.astype(np.float32)


def halve(a):
    high = a.astype(jnp.bfloat16)
    return high, (a - high.astype(jnp.float32)).astype(jnp.bfloat16)


def left(table, parts):
    high, low = halve(jnp.concatenate(parts, axis=1))
    data = jnp.concatenate([high, low, high], axis=0)
    wide = jnp.dot(table, data, preferred_element_type=jnp.float32)
    return [wide[:, 128 * p : 128 * p + 128] for p in range(3)]


def right(parts, table):
    high, low = halve(jnp.concatenate(parts, axis=0))
    tall = jnp.dot(jnp.concatenate([high, low], axis=1), table, preferred_element_type=jnp.float32)
    tall = tall[:, :128] + tall[:, 128:]
    return [tall[SPAN * p : SPAN * p + SPAN] for p in range(3)]


def wrap(i, n):
    return jnp.where(i >= n, i - n, i)


def kernel(
    acts_h, outg_h, mom_h, wt_h, kept_h, lefts_h, rights_h,
    outm, outw,
    acts, outg, mom, wt, kept, lefts32, rights32, lefts, rights,
    part, rx, x1, x0, x2, zr, turned, names, tmsg, tin, every,
    lsem, csend, crecv, xsend, xrecv, zsend, zrecv, nsend, nrecv, tsend, trecv, gsend, grecv, told,
):
    rep = lax.axis_index("rep")
    f = lax.axis_index("fsdp")
    core = lax.rem(f, 2)
    x = lax.rem(f // 2, N_X)
    z = f // (2 * N_X)
    other = 1 - core
    xr, xl, xo = lax.rem(x + 1, N_X), lax.rem(x + 3, N_X), lax.rem(x + 2, N_X)

    def at(z_, x_, core_):
        return (rep, (z_ * N_X + x_) * 2 + core_)

    piece = [lax.rem(z + d, N_ZLO) for d in (1, 3, 2)] + [z]

    first = lax.rem(z + 1, 2)
    load_acts = []
    for k in range(2):
        par = first if k == 0 else 1 - first
        cols = pl.ds(pl.multiple_of(par * PARITY, 128), PARITY)
        load_acts.append(pltpu.make_async_copy(acts_h.at[:, cols], acts.at[:, cols], lsem.at[k]))
    load_outg = pltpu.make_async_copy(outg_h, outg, lsem.at[2])
    load_outg.start()
    load_acts[0].start()
    load_acts[1].start()
    small = [
        pltpu.make_async_copy(src, dst, lsem.at[3 + i])
        for i, (src, dst) in enumerate(((mom_h.at[0], mom), (wt_h, wt), (kept_h, kept), (lefts_h, lefts32), (rights_h, rights32)))
    ]
    for copy in small:
        copy.start()

    barrier = pltpu.get_barrier_semaphore()

    def greet_group(i, carry):
        member = wrap(f + i, N_FSDP)

        @pl.when(member != HUB)
        def _():
            pl.semaphore_signal(barrier, inc=1, device_id=(rep, member), device_id_type=MESH)

        return carry

    def greet_peers(i, carry):
        pl.semaphore_signal(
            barrier, inc=1, device_id=(wrap(rep + i, N_REP), f), device_id_type=MESH
        )
        return carry

    lax.fori_loop(1, N_FSDP, greet_group, 0)

    lane = lax.broadcasted_iota(jnp.int32, (32, 128), 1)

    owners = [xo, xr, xl, x]

    def chunk(half, o, grads):
        par, j = (first if half == 0 else 1 - first), owners[o]
        base = pl.multiple_of(par * PARITY + j * WIDE, 128)
        prod = jnp.dot(grads, acts[:, pl.ds(base, WIDE)], preferred_element_type=jnp.float32)
        for h in range(2):
            blk = prod[SPAN * h : SPAN * h + SPAN]
            zz = 2 * h + par
            b2 = blk[:, 256:384]
            part[0, zz, j, 0:64] = blk[:, 0:128]
            part[0, zz, j, 64:128] = blk[:, 128:256]
            part[0, zz, j, 128:160] = jnp.where(lane < 64, b2[0:32], pltpu.roll(b2[32:64], 64, 1))
            part[1, zz, j, 0:64] = blk[:, 384:512]
            part[1, zz, j, 64:128] = blk[:, 512:640]
            part[1, zz, j, 128:160] = jnp.where(lane < 64, pltpu.roll(b2[0:32], 64, 1), b2[32:64])
        for k in (2 * half, 2 * half + 1):
            swap(k, o).start()

    def swap(k, o):
        return pltpu.make_async_remote_copy(
            src_ref=part.at[other, piece[k], owners[o]], dst_ref=rx.at[k, o],
            send_sem=csend.at[4 * k + o], recv_sem=crecv.at[4 * k + o],
            device_id=at(z, x, other), device_id_type=MESH,
        )

    A, B = pl.ds(0, HALF), pl.ds(HALF, HALF)

    def hop(k, kind, way):
        side = xr if way == 0 else xl
        slab = xo if kind == 1 else side
        rows = (B if way == 0 else A) if kind == 0 else (A if way == 0 else B)
        land = (x0, x1, x2)[kind]
        i = (k * 3 + kind) * 2 + way
        return pltpu.make_async_remote_copy(
            src_ref=part.at[core, piece[k], slab, rows], dst_ref=land.at[k, way],
            send_sem=xsend.at[i], recv_sem=xrecv.at[i],
            device_id=at(z, side, core), device_id_type=MESH,
        )

    def zhop(k):
        return pltpu.make_async_remote_copy(
            src_ref=part.at[core, piece[k], x], dst_ref=zr.at[k],
            send_sem=zsend.at[k], recv_sem=zrecv.at[k],
            device_id=at(piece[k], x, core), device_id_type=MESH,
        )

    def take(k, o):
        swap(k, o).wait_recv()
        slab = owners[o]
        part[core, piece[k], slab] = part[core, piece[k], slab] + rx[k, o]

    def open_far(k):
        take(k, 0)
        hop(k, 1, 0).start()
        hop(k, 1, 1).start()

    def open_near(k):
        for way in range(2):
            take(k, 1 + way)
            hop(k, 0, way).start()

    def pass_on(k):
        for way in range(2):
            hop(k, 1, way).wait_recv()
            side, rows = (xr, A) if way == 0 else (xl, B)
            part[core, piece[k], side, rows] = part[core, piece[k], side, rows] + x1[k, way]
            hop(k, 2, way).start()

    def close_piece(k):
        take(k, 3)
        for way in range(2):
            hop(k, 0, way).wait_recv()
            hop(k, 2, way).wait_recv()
        part[core, piece[k], x, A] = part[core, piece[k], x, A] + (x0[k, 1] + x2[k, 0])
        part[core, piece[k], x, B] = part[core, piece[k], x, B] + (x0[k, 0] + x2[k, 1])
        if k < 3:
            zhop(k).start()

    order = [core, core + 1, core + 2, core + 3, 4 * other]
    lane1 = lax.broadcasted_iota(jnp.int32, (1, 128), 1)
    lane4 = lax.broadcasted_iota(jnp.int32, (4, 128), 1)
    lane8 = lax.broadcasted_iota(jnp.int32, (TILE, 128), 1)
    wide = lax.broadcasted_iota(jnp.int32, (SPAN, 128), 1)
    row = lax.broadcasted_iota(jnp.int32, (SPAN, 128), 0)
    place = (row // TILE) * TILE + lax.rem(wide, SPAN) // TILE
    upper = jnp.where(lane8 < SPAN, 0, SPAN)
    block = lax.rem(lane8, SPAN) // TILE

    def to_group(src, dst, send, recv, i):
        return pltpu.make_async_remote_copy(
            src_ref=src, dst_ref=dst, send_sem=send, recv_sem=recv,
            device_id=(rep, wrap(f + i, N_FSDP)), device_id_type=MESH,
        )

    def to_peer(src, dst, send, recv, i):
        return pltpu.make_async_remote_copy(
            src_ref=src, dst_ref=dst, send_sem=send, recv_sem=recv,
            device_id=(wrap(rep + i, N_REP), f), device_id_type=MESH,
        )

    def send_names():
        mine = jnp.zeros((1, 128), jnp.int32)
        for s in range(5):
            mine = jnp.where(lane1 == s, kept[0, s], mine)
        names[f] = mine

        def one(i, carry):
            to_group(names.at[f], names.at[f], nsend, nrecv, i).start()
            return carry

        lax.fori_loop(1, N_FSDP, one, 0)

    def all_names():
        ref = names.at[pl.ds(0, N_FSDP - 1)]
        return to_group(ref, ref, nsend, nrecv, 1)

    def pick_columns(tile, number):
        source = (number & 7) * TILE + lax.rem(lane8, TILE) + upper
        return jnp.take_along_axis(tile, source, axis=1)

    def merge(a, b, c):
        return jnp.where(block == 0, a, jnp.where(block == 1, b, c))

    def pack(tiles):
        return jnp.where(lax.rem(lane4, SPAN) < 24, tiles[0:4], pltpu.roll(tiles[4:8], 24, 1))

    def unpack(four):
        return jnp.concatenate([four, pltpu.roll(four, 104, 1)], axis=0)

    def two_chunks(i, carry):
        numbers, rows = [], []
        for c in range(2):
            m = 2 * i + c
            piece_acts = acts[:, pl.ds(pl.multiple_of(m * WIDE, 128), WIDE)]
            both = jnp.dot(
                turned[...], jnp.concatenate([piece_acts, piece_acts], axis=0),
                preferred_element_type=jnp.float32,
            )
            for h in range(2):
                owner = ((2 * h + m // 4) * N_X + lax.rem(m, 4)) * 2
                low = jnp.broadcast_to(names[owner], (TILE, 128))
                high = jnp.broadcast_to(names[owner + 1], (TILE, 128))
                ten = jnp.where(lane8 < 5, low, pltpu.roll(high, 5, 1))
                for p in range(5):
                    number = jnp.take_along_axis(ten, 2 * p + jnp.where(lane8 < SPAN, 0, 1), axis=1)
                    high_part = number >> 3
                    found = both[SPAN * h : SPAN * h + TILE, 128 * p : 128 * p + 128]
                    for a in range(1, 8):
                        at_row = SPAN * h + TILE * a
                        found = jnp.where(
                            high_part == a, both[at_row : at_row + TILE, 128 * p : 128 * p + 128], found
                        )
                    numbers.append(number)
                    rows.append(found)
        high, low = halve(jnp.concatenate(rows, axis=0))
        out = jnp.dot(
            jnp.concatenate([high, low], axis=1), rights[0:256], preferred_element_type=jnp.float32
        )
        out = out[:, :128] + out[:, 128:]
        for c in range(2):
            m = 2 * i + c
            for h in range(2):
                owner = ((2 * h + m // 4) * N_X + lax.rem(m, 4)) * 2
                base = 10 * c + 5 * h
                t = [
                    pick_columns(out[TILE * q : TILE * q + TILE], numbers[q])
                    for q in range(base, base + 5)
                ]
                tmsg[owner] = pack(merge(t[0], t[1], t[2]))
                tmsg[owner + 1] = pack(merge(t[3], t[4], pltpu.roll(t[2], SPAN, 1)))
        return carry

    def send_tiles():
        tin[f] = tmsg[f]

        def one(i, carry):
            to_group(tmsg.at[wrap(f + i, N_FSDP)], tin.at[f], tsend, trecv, i).start()
            return carry

        lax.fori_loop(1, N_FSDP, one, 0)

    def all_tiles():
        span = pl.ds(0, N_FSDP - 1)
        return to_group(tmsg.at[span], tin.at[span], tsend, trecv, 1)

    def pairs(ref):
        zero = jnp.zeros((SPAN, SPAN), jnp.float32)
        return [
            jnp.concatenate([ref[order[0]], ref[order[1]]], axis=1),
            jnp.concatenate([ref[order[2]], ref[order[3]]], axis=1),
            jnp.concatenate([ref[order[4]], zero], axis=1),
        ]

    def unpair(ref, parts):
        for j in range(5):
            half = parts[j // 2][:, SPAN * (j % 2) : SPAN * (j % 2) + SPAN]
            ref[order[j]] = half

    @pl.when(f != HUB)
    def _():
        pl.semaphore_wait(barrier, N_FSDP - 1)

    @pl.when(f == HUB - 1)
    def _():
        pl.semaphore_signal(told, inc=1, device_id=(rep, HUB), device_id_type=MESH)

    @pl.when(f == HUB)
    def _():
        pl.semaphore_wait(told, 1)
        lax.fori_loop(1, N_REP, greet_peers, 0)

    small[2].wait()
    send_names()
    load_outg.wait()
    flat = outg[...]
    grads = flat.astype(jnp.float32).T.astype(jnp.bfloat16)
    load_acts[0].wait()
    for o in range(3):
        chunk(0, o, grads)
    for i in (0, 1, 3, 4):
        small[i].wait()
    lefts[...] = lefts32[...].astype(jnp.bfloat16)
    rights[...] = rights32[...].astype(jnp.bfloat16)
    fwd_l, inv_l = lefts[0:64, 0:192], lefts[64:128, 0:192]
    fwd_r, inv_r = rights[0:256], rights[256:512]
    spun = jnp.dot(flat, rights[0:128], preferred_element_type=jnp.float32)
    spun_high, spun_low = halve((spun[:, :128] + spun[:, 128:]).T)
    turned[:, :128] = spun_high
    turned[:, 128:] = spun_low
    chunk(0, 3, grads)
    load_acts[1].wait()
    early = rep < N_REP // 4

    def first_half():
        open_far(0)
        open_far(1)
        open_near(0)
        open_near(1)

    @pl.when(early)
    def _():
        first_half()
        for o in range(4):
            chunk(1, o, grads)
        open_far(2)
        open_far(3)
        open_near(2)
        open_near(3)

    all_names().wait_recv()
    lax.fori_loop(0, 2, two_chunks, 0)

    @pl.when(early)
    def _():
        pass_on(0)
        pass_on(1)

    pl.when(jnp.logical_not(early))(first_half)
    lax.fori_loop(2, 4, two_chunks, 0)
    send_tiles()

    @pl.when(early)
    def _():
        pass_on(2)
        close_piece(0)
        pass_on(3)
        close_piece(1)
        close_piece(2)

    @pl.when(jnp.logical_not(early))
    def _():
        chunk(1, 0, grads)
        chunk(1, 1, grads)

    def tell(i, carry):
        member = wrap(f + i, N_FSDP)
        pl.semaphore_signal(told, inc=1, device_id=(rep, member), device_id_type=MESH)
        return carry

    @pl.when(f == HUB)
    def _():
        pl.semaphore_wait(barrier, N_REP - 1)
        lax.fori_loop(1, N_FSDP, tell, 0)

    scalars = [kept[0, s] for s in order]
    carried = [decay_rate * m for m in pairs(mom)]
    own = [
        jnp.where(wide < SPAN, scalars[2 * p], scalars[min(2 * p + 1, 4)]) for p in range(3)
    ]
    coef = right(left(fwd_l, carried), fwd_r)
    found = [
        pick_columns(
            jnp.sum(jnp.where(place == own[p], coef[p], 0.0).reshape(8, TILE, 128), axis=0), own[p][0:8]
        )
        for p in range(3)
    ]
    from_momentum = merge(*found)

    all_tiles().wait_recv()
    tiles = from_momentum + unpack(jnp.sum(tin[...], axis=0))
    message = pack(tiles)
    for j in range(5):
        spot = (lane4 == 56 + j) | (lane4 == 80 + j)
        message = jnp.where(spot, scalars[j].astype(jnp.float32), message)
    every[rep] = message

    @pl.when(f != HUB)
    def _():
        pl.semaphore_wait(told, 1)

    def send_one(i, carry):
        to_peer(every.at[rep], every.at[rep], gsend, grecv, i).start()
        return carry

    lax.fori_loop(1, N_REP, send_one, 0)

    def all_posts():
        ref = every.at[pl.ds(0, N_REP - 1)]
        return to_peer(ref, ref, gsend, grecv, 1)

    @pl.when(jnp.logical_not(early))
    def _():
        pass_on(0)
        pass_on(1)
        chunk(1, 2, grads)
        chunk(1, 3, grads)
        open_far(2)
        open_far(3)
        open_near(2)
        open_near(3)
        pass_on(2)
        close_piece(0)
        pass_on(3)
        close_piece(1)
        close_piece(2)

    src_tile = [upper + TILE * p + lax.rem(lane8, TILE) for p in range(3)]
    src_num = [56 + jnp.where(lane8 < SPAN, 2 * p, min(2 * p + 1, 4)) for p in range(3)]

    def spread_out(p):
        tile = jnp.take_along_axis(tiles, src_tile[p], axis=1)
        tall = jnp.broadcast_to(tile[None], (8, TILE, 128)).reshape(SPAN, 128)
        return jnp.where(place == own[p], tall, 0.0)

    decoded = left(inv_l, right([spread_out(p) for p in range(3)], inv_r))
    for p in range(3):
        carried[p] = carried[p] - decoded[p]
    weights = pairs(wt)
    close_piece(3)
    total = part[core, z, x]
    tail = jnp.concatenate([total[128:160], pltpu.roll(total[128:160], 64, 1)], axis=0)
    for p, grown in enumerate((total[0:64], total[64:128], tail)):
        carried[p] = carried[p] + grown
    for k in range(4):
        for o in range(4):
            swap(k, o).wait_send()
        for kind in range(3):
            for way in range(2):
                hop(k, kind, way).wait_send()
    for k in range(3):
        zhop(k).wait()
    rest = zr[0] + zr[1] + zr[2]
    tail = jnp.concatenate([rest[128:160], pltpu.roll(rest[128:160], 64, 1)], axis=0)
    unpair(outm.at[0], [carried[0] + rest[0:64], carried[1] + rest[64:128], carried[2] + tail])
    all_names().wait_send()
    all_tiles().wait_send()
    all_posts().wait_send()
    all_posts().wait_recv()

    place_f = place.astype(jnp.float32).reshape(8, TILE, 128)

    def gather_one(g, sums):
        got = unpack(every[g])
        new = []
        for p in range(3):
            tile = jnp.take_along_axis(got, src_tile[p], axis=1)
            num = jnp.take_along_axis(got, src_num[p], axis=1)
            new.append(sums[p] + jnp.where(num[None] == place_f, tile[None], 0.0))
        return tuple(new)

    sums = lax.fori_loop(
        0, N_REP, gather_one, tuple(jnp.zeros((8, TILE, 128), jnp.float32) for _ in range(3)),
        unroll=True,
    )
    update = left(inv_l, right([s.reshape(SPAN, 128) for s in sums], inv_r))
    fresh = []
    for p in range(3):
        square = jnp.sum(update[p] * update[p], axis=0, keepdims=True)
        low = wide[0:1] < SPAN
        mean_lo = jnp.sum(jnp.where(low, square, 0.0), axis=1, keepdims=True) / (SPAN * SPAN)
        mean_hi = jnp.sum(jnp.where(low, 0.0, square), axis=1, keepdims=True) / (SPAN * SPAN)
        spread = jnp.sqrt(jnp.where(low, mean_lo, mean_hi) + epsilon)
        fresh.append(weights[p] - step_size * update[p] / spread)
    unpair(outw, fresh)


def shards(activations, out_grad, momentum, weight, kept_tile):
    f32 = jnp.float32
    vm = pltpu.VMEM
    dma = pltpu.SemaphoreType.DMA
    return tuple(
        pl.pallas_call(
            kernel,
            out_shape=(
                pltpu.VMEM(momentum.shape, f32),
                pltpu.VMEM(weight.shape, f32),
            ),
            in_specs=[pl.BlockSpec(memory_space=pltpu.HBM)] * 7,
            out_specs=(pl.BlockSpec(memory_space=pltpu.VMEM),) * 2,
            scratch_shapes=[
                vm((TOK, COLS), jnp.bfloat16),
                vm((TOK, TOK), jnp.bfloat16),
                vm((5, SPAN, SPAN), f32),
                vm((5, SPAN, SPAN), f32),
                pltpu.SMEM((1, 5), jnp.int32),
                vm((128, 256), f32),
                vm((512, 256), f32),
                vm((128, 256), jnp.bfloat16),
                vm((512, 256), jnp.bfloat16),
                vm((2, N_ZLO, N_X, SLAB, 128), f32),
                vm((N_ZLO, N_X, SLAB, 128), f32),
                vm((4, 2, HALF, 128), f32),
                vm((4, 2, HALF, 128), f32),
                vm((4, 2, HALF, 128), f32),
                vm((3, SLAB, 128), f32),
                vm((TOK, 2 * TOK), jnp.bfloat16),
                vm((N_FSDP, 1, 128), jnp.int32),
                vm((N_FSDP, TILE // 2, 128), f32),
                vm((N_FSDP, TILE // 2, 128), f32),
                vm((N_REP, TILE // 2, 128), f32),
                dma((8,)),
                dma((16,)),
                dma((16,)),
                dma((24,)),
                dma((24,)),
                dma((3,)),
                dma((3,)),
                dma,
                dma,
                dma,
                dma,
                dma,
                dma,
                pltpu.SemaphoreType.REGULAR,
            ],
            compiler_params=pltpu.CompilerParams(
                collective_id=0, has_side_effects=True, vmem_limit_bytes=48 * 1024 * 1024
            ),
            name="demo_step",
        )(*(
            pltpu.with_memory_space_constraint(a, pltpu.HBM)
            for a in (activations, out_grad, momentum, weight, kept_tile, *map(jnp.asarray, tables()))
        ))
    )


def solution(mesh):
    placed = (
        P(("rep", "fsdp"), None),
        P(("rep", "fsdp"), None),
        P("rep", "fsdp", None, None),
        P("fsdp", None, None),
        P("rep", "fsdp"),
    )
    return jax.shard_map(
        shards,
        mesh=mesh,
        in_specs=placed,
        out_specs=(P("rep", "fsdp", None, None), P("fsdp", None, None)),
        check_vma=False,
    )
```

```python
import jax
import jax.numpy as jnp
import ml_dtypes
import numpy as np
from jax import lax
from jax.experimental import pallas as pl
from jax.experimental.pallas import tpu as pltpu
from jax.sharding import PartitionSpec as P

SPAN = 64
TILE = 8
N_X = 4
N_ZLO = 4
N_REP = 16
N_FSDP = 32
HUB = 31
SLAB = 160
HALF = SLAB // 2
TOK = 128
COLS = 5120
WIDE = 640
PARITY = 4 * WIDE

decay_rate = 0.9
step_size = 0.5
epsilon = 1e-06

MESH = pl.DeviceIdType.MESH


def tables():
    u = np.arange(SPAN, dtype=np.float64)[:, None]
    x = np.arange(SPAN, dtype=np.float64)[None, :]
    s = np.where(u == 0, np.sqrt(1.0 / SPAN), np.sqrt(2.0 / SPAN))
    basis = s * np.cos(np.pi * (2.0 * x + 1.0) * u / (2.0 * SPAN))
    zero = np.zeros((SPAN, SPAN))

    def halves(table):
        high = table.astype(ml_dtypes.bfloat16)
        return high, (table - high.astype(np.float64)).astype(ml_dtypes.bfloat16)

    def for_left(table):
        high, low = halves(np.concatenate([table, zero], 1))
        high, low = high[:, :SPAN], low[:, :SPAN]
        return np.concatenate([high, high, low, zero.astype(high.dtype)], 1)

    def for_right(table):
        high, low = halves(np.block([[table, zero], [zero, table]]))
        return np.block([[high, low], [high, np.zeros_like(low)]])

    lefts = np.concatenate([for_left(basis), for_left(basis.T)], 0)
    rights = np.concatenate([for_right(basis.T), for_right(basis)], 0)
    return lefts.astype(np.float32), rights.astype(np.float32)


def halve(a):
    high = a.astype(jnp.bfloat16)
    return high, (a - high.astype(jnp.float32)).astype(jnp.bfloat16)


def left(table, parts):
    high, low = halve(jnp.concatenate(parts, axis=1))
    data = jnp.concatenate([high, low, high], axis=0)
    wide = jnp.dot(table, data, preferred_element_type=jnp.float32)
    return [wide[:, 128 * p : 128 * p + 128] for p in range(3)]


def right(parts, table):
    high, low = halve(jnp.concatenate(parts, axis=0))
    tall = jnp.dot(jnp.concatenate([high, low], axis=1), table, preferred_element_type=jnp.float32)
    tall = tall[:, :128] + tall[:, 128:]
    return [tall[SPAN * p : SPAN * p + SPAN] for p in range(3)]


def wrap(i, n):
    return jnp.where(i >= n, i - n, i)


def kernel(
    acts_h, outg_h, mom_h, wt_h, kept_h, lefts_h, rights_h,
    outm, outw,
    acts, outg, mom, wt, kept, lefts32, rights32, lefts, rights,
    part, rx, x1, x0, x2, zr, turned, names, tmsg, tin, every,
    lsem, csend, crecv, xsend, xrecv, zsend, zrecv, nsend, nrecv, tsend, trecv, gsend, grecv, told,
):
    rep = lax.axis_index("rep")
    f = lax.axis_index("fsdp")
    core = lax.rem(f, 2)
    x = lax.rem(f // 2, N_X)
    z = f // (2 * N_X)
    other = 1 - core
    xr, xl, xo = lax.rem(x + 1, N_X), lax.rem(x + 3, N_X), lax.rem(x + 2, N_X)

    def at(z_, x_, core_):
        return (rep, (z_ * N_X + x_) * 2 + core_)

    piece = [lax.rem(z + d, N_ZLO) for d in (1, 3, 2)] + [z]

    first = lax.rem(z + 1, 2)
    load_acts = []
    for k in range(2):
        par = first if k == 0 else 1 - first
        cols = pl.ds(pl.multiple_of(par * PARITY, 128), PARITY)
        load_acts.append(pltpu.make_async_copy(acts_h.at[:, cols], acts.at[:, cols], lsem.at[k]))
    load_outg = pltpu.make_async_copy(outg_h, outg, lsem.at[2])
    load_outg.start()
    load_acts[0].start()
    load_acts[1].start()
    small = [
        pltpu.make_async_copy(src, dst, lsem.at[3 + i])
        for i, (src, dst) in enumerate(((mom_h.at[0], mom), (wt_h, wt), (kept_h, kept), (lefts_h, lefts32), (rights_h, rights32)))
    ]
    for copy in small:
        copy.start()

    barrier = pltpu.get_barrier_semaphore()

    def greet_group(i, carry):
        member = wrap(f + i, N_FSDP)

        @pl.when(member != HUB)
        def _():
            pl.semaphore_signal(barrier, inc=1, device_id=(rep, member), device_id_type=MESH)

        return carry

    def greet_peers(i, carry):
        pl.semaphore_signal(
            barrier, inc=1, device_id=(wrap(rep + i, N_REP), f), device_id_type=MESH
        )
        return carry

    lax.fori_loop(1, N_FSDP, greet_group, 0)

    lane = lax.broadcasted_iota(jnp.int32, (32, 128), 1)

    owners = [xo, xr, xl, x]

    def chunk(half, o, grads):
        par, j = (first if half == 0 else 1 - first), owners[o]
        base = pl.multiple_of(par * PARITY + j * WIDE, 128)
        prod = jnp.dot(grads, acts[:, pl.ds(base, WIDE)], preferred_element_type=jnp.float32)
        for h in range(2):
            blk = prod[SPAN * h : SPAN * h + SPAN]
            zz = 2 * h + par
            b2 = blk[:, 256:384]
            part[0, zz, j, 0:64] = blk[:, 0:128]
            part[0, zz, j, 64:128] = blk[:, 128:256]
            part[0, zz, j, 128:160] = jnp.where(lane < 64, b2[0:32], pltpu.roll(b2[32:64], 64, 1))
            part[1, zz, j, 0:64] = blk[:, 384:512]
            part[1, zz, j, 64:128] = blk[:, 512:640]
            part[1, zz, j, 128:160] = jnp.where(lane < 64, pltpu.roll(b2[0:32], 64, 1), b2[32:64])
        for k in (2 * half, 2 * half + 1):
            swap(k, o).start()

    def swap(k, o):
        return pltpu.make_async_remote_copy(
            src_ref=part.at[other, piece[k], owners[o]], dst_ref=rx.at[k, o],
            send_sem=csend.at[4 * k + o], recv_sem=crecv.at[4 * k + o],
            device_id=at(z, x, other), device_id_type=MESH,
        )

    A, B = pl.ds(0, HALF), pl.ds(HALF, HALF)

    def hop(k, kind, way):
        side = xr if way == 0 else xl
        slab = xo if kind == 1 else side
        rows = (B if way == 0 else A) if kind == 0 else (A if way == 0 else B)
        land = (x0, x1, x2)[kind]
        i = (k * 3 + kind) * 2 + way
        return pltpu.make_async_remote_copy(
            src_ref=part.at[core, piece[k], slab, rows], dst_ref=land.at[k, way],
            send_sem=xsend.at[i], recv_sem=xrecv.at[i],
            device_id=at(z, side, core), device_id_type=MESH,
        )

    def zhop(k):
        return pltpu.make_async_remote_copy(
            src_ref=part.at[core, piece[k], x], dst_ref=zr.at[k],
            send_sem=zsend.at[k], recv_sem=zrecv.at[k],
            device_id=at(piece[k], x, core), device_id_type=MESH,
        )

    def take(k, o):
        swap(k, o).wait_recv()
        slab = owners[o]
        part[core, piece[k], slab] = part[core, piece[k], slab] + rx[k, o]

    def open_far(k):
        take(k, 0)
        hop(k, 1, 0).start()
        hop(k, 1, 1).start()

    def open_near(k):
        for way in range(2):
            take(k, 1 + way)
            hop(k, 0, way).start()

    def pass_on(k):
        for way in range(2):
            hop(k, 1, way).wait_recv()
            side, rows = (xr, A) if way == 0 else (xl, B)
            part[core, piece[k], side, rows] = part[core, piece[k], side, rows] + x1[k, way]
            hop(k, 2, way).start()

    def close_piece(k):
        take(k, 3)
        for way in range(2):
            hop(k, 0, way).wait_recv()
            hop(k, 2, way).wait_recv()
        part[core, piece[k], x, A] = part[core, piece[k], x, A] + (x0[k, 1] + x2[k, 0])
        part[core, piece[k], x, B] = part[core, piece[k], x, B] + (x0[k, 0] + x2[k, 1])
        if k < 3:
            zhop(k).start()

    order = [core, core + 1, core + 2, core + 3, 4 * other]
    lane1 = lax.broadcasted_iota(jnp.int32, (1, 128), 1)
    lane4 = lax.broadcasted_iota(jnp.int32, (4, 128), 1)
    lane8 = lax.broadcasted_iota(jnp.int32, (TILE, 128), 1)
    wide = lax.broadcasted_iota(jnp.int32, (SPAN, 128), 1)
    row = lax.broadcasted_iota(jnp.int32, (SPAN, 128), 0)
    place = (row // TILE) * TILE + lax.rem(wide, SPAN) // TILE
    upper = jnp.where(lane8 < SPAN, 0, SPAN)
    block = lax.rem(lane8, SPAN) // TILE

    def to_group(src, dst, send, recv, i):
        return pltpu.make_async_remote_copy(
            src_ref=src, dst_ref=dst, send_sem=send, recv_sem=recv,
            device_id=(rep, wrap(f + i, N_FSDP)), device_id_type=MESH,
        )

    def to_peer(src, dst, send, recv, i):
        return pltpu.make_async_remote_copy(
            src_ref=src, dst_ref=dst, send_sem=send, recv_sem=recv,
            device_id=(wrap(rep + i, N_REP), f), device_id_type=MESH,
        )

    def send_names():
        mine = jnp.zeros((1, 128), jnp.int32)
        for s in range(5):
            mine = jnp.where(lane1 == s, kept[0, s], mine)
        names[f] = mine

        def one(i, carry):
            to_group(names.at[f], names.at[f], nsend, nrecv, i).start()
            return carry

        lax.fori_loop(1, N_FSDP, one, 0)

    def all_names():
        ref = names.at[pl.ds(0, N_FSDP - 1)]
        return to_group(ref, ref, nsend, nrecv, 1)

    def pick_columns(tile, number):
        source = (number & 7) * TILE + lax.rem(lane8, TILE) + upper
        return jnp.take_along_axis(tile, source, axis=1)

    def merge(a, b, c):
        return jnp.where(block == 0, a, jnp.where(block == 1, b, c))

    def pack(tiles):
        return jnp.where(lax.rem(lane4, SPAN) < 24, tiles[0:4], pltpu.roll(tiles[4:8], 24, 1))

    def unpack(four):
        return jnp.concatenate([four, pltpu.roll(four, 104, 1)], axis=0)

    def two_chunks(i, carry):
        numbers, rows = [], []
        for c in range(2):
            m = 2 * i + c
            piece_acts = acts[:, pl.ds(pl.multiple_of(m * WIDE, 128), WIDE)]
            both = jnp.dot(
                turned[...], jnp.concatenate([piece_acts, piece_acts], axis=0),
                preferred_element_type=jnp.float32,
            )
            for h in range(2):
                owner = ((2 * h + m // 4) * N_X + lax.rem(m, 4)) * 2
                low = jnp.broadcast_to(names[owner], (TILE, 128))
                high = jnp.broadcast_to(names[owner + 1], (TILE, 128))
                ten = jnp.where(lane8 < 5, low, pltpu.roll(high, 5, 1))
                for p in range(5):
                    number = jnp.take_along_axis(ten, 2 * p + jnp.where(lane8 < SPAN, 0, 1), axis=1)
                    high_part = number >> 3
                    found = both[SPAN * h : SPAN * h + TILE, 128 * p : 128 * p + 128]
                    for a in range(1, 8):
                        at_row = SPAN * h + TILE * a
                        found = jnp.where(
                            high_part == a, both[at_row : at_row + TILE, 128 * p : 128 * p + 128], found
                        )
                    numbers.append(number)
                    rows.append(found)
        high, low = halve(jnp.concatenate(rows, axis=0))
        out = jnp.dot(
            jnp.concatenate([high, low], axis=1), rights[0:256], preferred_element_type=jnp.float32
        )
        out = out[:, :128] + out[:, 128:]
        for c in range(2):
            m = 2 * i + c
            for h in range(2):
                owner = ((2 * h + m // 4) * N_X + lax.rem(m, 4)) * 2
                base = 10 * c + 5 * h
                t = [
                    pick_columns(out[TILE * q : TILE * q + TILE], numbers[q])
                    for q in range(base, base + 5)
                ]
                tmsg[owner] = pack(merge(t[0], t[1], t[2]))
                tmsg[owner + 1] = pack(merge(t[3], t[4], pltpu.roll(t[2], SPAN, 1)))
        return carry

    def send_tiles():
        tin[f] = tmsg[f]

        def one(i, carry):
            to_group(tmsg.at[wrap(f + i, N_FSDP)], tin.at[f], tsend, trecv, i).start()
            return carry

        lax.fori_loop(1, N_FSDP, one, 0)

    def all_tiles():
        span = pl.ds(0, N_FSDP - 1)
        return to_group(tmsg.at[span], tin.at[span], tsend, trecv, 1)

    def pairs(ref):
        zero = jnp.zeros((SPAN, SPAN), jnp.float32)
        return [
            jnp.concatenate([ref[order[0]], ref[order[1]]], axis=1),
            jnp.concatenate([ref[order[2]], ref[order[3]]], axis=1),
            jnp.concatenate([ref[order[4]], zero], axis=1),
        ]

    def unpair(ref, parts):
        for j in range(5):
            half = parts[j // 2][:, SPAN * (j % 2) : SPAN * (j % 2) + SPAN]
            ref[order[j]] = half

    @pl.when(f != HUB)
    def _():
        pl.semaphore_wait(barrier, N_FSDP - 1)

    @pl.when(f == HUB - 1)
    def _():
        pl.semaphore_signal(told, inc=1, device_id=(rep, HUB), device_id_type=MESH)

    @pl.when(f == HUB)
    def _():
        pl.semaphore_wait(told, 1)
        lax.fori_loop(1, N_REP, greet_peers, 0)

    small[2].wait()
    send_names()
    load_outg.wait()
    flat = outg[...]
    grads = flat.astype(jnp.float32).T.astype(jnp.bfloat16)
    load_acts[0].wait()
    for o in range(3):
        chunk(0, o, grads)
    for i in (0, 1, 3, 4):
        small[i].wait()
    lefts[...] = lefts32[...].astype(jnp.bfloat16)
    rights[...] = rights32[...].astype(jnp.bfloat16)
    fwd_l, inv_l = lefts[0:64, 0:192], lefts[64:128, 0:192]
    fwd_r, inv_r = rights[0:256], rights[256:512]
    spun = jnp.dot(flat, rights[0:128], preferred_element_type=jnp.float32)
    spun_high, spun_low = halve((spun[:, :128] + spun[:, 128:]).T)
    turned[:, :128] = spun_high
    turned[:, 128:] = spun_low
    chunk(0, 3, grads)
    open_far(0)
    open_far(1)
    open_near(0)
    open_near(1)
    load_acts[1].wait()
    early = rep < N_REP // 4

    @pl.when(early)
    def _():
        for o in range(4):
            chunk(1, o, grads)
        open_far(2)
        open_far(3)
        open_near(2)
        open_near(3)

    all_names().wait_recv()
    lax.fori_loop(0, 2, two_chunks, 0)

    @pl.when(early)
    def _():
        pass_on(0)
        pass_on(1)

    lax.fori_loop(2, 4, two_chunks, 0)
    send_tiles()

    @pl.when(early)
    def _():
        pass_on(2)
        close_piece(0)
        pass_on(3)
        close_piece(1)
        close_piece(2)

    @pl.when(jnp.logical_not(early))
    def _():
        chunk(1, 0, grads)
        chunk(1, 1, grads)

    def tell(i, carry):
        member = wrap(f + i, N_FSDP)
        pl.semaphore_signal(told, inc=1, device_id=(rep, member), device_id_type=MESH)
        return carry

    @pl.when(f == HUB)
    def _():
        pl.semaphore_wait(barrier, N_REP - 1)
        lax.fori_loop(1, N_FSDP, tell, 0)

    scalars = [kept[0, s] for s in order]
    carried = [decay_rate * m for m in pairs(mom)]
    own = [
        jnp.where(wide < SPAN, scalars[2 * p], scalars[min(2 * p + 1, 4)]) for p in range(3)
    ]
    coef = right(left(fwd_l, carried), fwd_r)
    found = [
        pick_columns(
            jnp.sum(jnp.where(place == own[p], coef[p], 0.0).reshape(8, TILE, 128), axis=0), own[p][0:8]
        )
        for p in range(3)
    ]
    from_momentum = merge(*found)

    all_tiles().wait_recv()
    tiles = from_momentum + unpack(jnp.sum(tin[...], axis=0))
    message = pack(tiles)
    for j in range(5):
        spot = (lane4 == 56 + j) | (lane4 == 80 + j)
        message = jnp.where(spot, scalars[j].astype(jnp.float32), message)
    every[rep] = message

    @pl.when(f != HUB)
    def _():
        pl.semaphore_wait(told, 1)

    def send_one(i, carry):
        to_peer(every.at[rep], every.at[rep], gsend, grecv, i).start()
        return carry

    lax.fori_loop(1, N_REP, send_one, 0)

    def all_posts():
        ref = every.at[pl.ds(0, N_REP - 1)]
        return to_peer(ref, ref, gsend, grecv, 1)

    @pl.when(jnp.logical_not(early))
    def _():
        pass_on(0)
        pass_on(1)
        chunk(1, 2, grads)
        chunk(1, 3, grads)
        open_far(2)
        open_far(3)
        open_near(2)
        open_near(3)
        pass_on(2)
        close_piece(0)
        pass_on(3)
        close_piece(1)
        close_piece(2)

    src_tile = [upper + TILE * p + lax.rem(lane8, TILE) for p in range(3)]
    src_num = [56 + jnp.where(lane8 < SPAN, 2 * p, min(2 * p + 1, 4)) for p in range(3)]

    def spread_out(p):
        tile = jnp.take_along_axis(tiles, src_tile[p], axis=1)
        tall = jnp.broadcast_to(tile[None], (8, TILE, 128)).reshape(SPAN, 128)
        return jnp.where(place == own[p], tall, 0.0)

    decoded = left(inv_l, right([spread_out(p) for p in range(3)], inv_r))
    for p in range(3):
        carried[p] = carried[p] - decoded[p]
    weights = pairs(wt)
    close_piece(3)
    total = part[core, z, x]
    tail = jnp.concatenate([total[128:160], pltpu.roll(total[128:160], 64, 1)], axis=0)
    for p, grown in enumerate((total[0:64], total[64:128], tail)):
        carried[p] = carried[p] + grown
    for k in range(4):
        for o in range(4):
            swap(k, o).wait_send()
        for kind in range(3):
            for way in range(2):
                hop(k, kind, way).wait_send()
    for k in range(3):
        zhop(k).wait()
    rest = zr[0] + zr[1] + zr[2]
    tail = jnp.concatenate([rest[128:160], pltpu.roll(rest[128:160], 64, 1)], axis=0)
    unpair(outm.at[0], [carried[0] + rest[0:64], carried[1] + rest[64:128], carried[2] + tail])
    all_names().wait_send()
    all_tiles().wait_send()
    all_posts().wait_send()
    all_posts().wait_recv()

    place_f = place.astype(jnp.float32).reshape(8, TILE, 128)

    def gather_one(g, sums):
        got = unpack(every[g])
        new = []
        for p in range(3):
            tile = jnp.take_along_axis(got, src_tile[p], axis=1)
            num = jnp.take_along_axis(got, src_num[p], axis=1)
            new.append(sums[p] + jnp.where(num[None] == place_f, tile[None], 0.0))
        return tuple(new)

    sums = lax.fori_loop(
        0, N_REP, gather_one, tuple(jnp.zeros((8, TILE, 128), jnp.float32) for _ in range(3)),
        unroll=True,
    )
    update = left(inv_l, right([s.reshape(SPAN, 128) for s in sums], inv_r))
    fresh = []
    for p in range(3):
        square = jnp.sum(update[p] * update[p], axis=0, keepdims=True)
        low = wide[0:1] < SPAN
        mean_lo = jnp.sum(jnp.where(low, square, 0.0), axis=1, keepdims=True) / (SPAN * SPAN)
        mean_hi = jnp.sum(jnp.where(low, 0.0, square), axis=1, keepdims=True) / (SPAN * SPAN)
        spread = jnp.sqrt(jnp.where(low, mean_lo, mean_hi) + epsilon)
        fresh.append(weights[p] - step_size * update[p] / spread)
    unpair(outw, fresh)


def shards(activations, out_grad, momentum, weight, kept_tile):
    f32 = jnp.float32
    vm = pltpu.VMEM
    dma = pltpu.SemaphoreType.DMA
    return tuple(
        pl.pallas_call(
            kernel,
            out_shape=(
                pltpu.VMEM(momentum.shape, f32),
                pltpu.VMEM(weight.shape, f32),
            ),
            in_specs=[pl.BlockSpec(memory_space=pltpu.HBM)] * 7,
            out_specs=(pl.BlockSpec(memory_space=pltpu.VMEM),) * 2,
            scratch_shapes=[
                vm((TOK, COLS), jnp.bfloat16),
                vm((TOK, TOK), jnp.bfloat16),
                vm((5, SPAN, SPAN), f32),
                vm((5, SPAN, SPAN), f32),
                pltpu.SMEM((1, 5), jnp.int32),
                vm((128, 256), f32),
                vm((512, 256), f32),
                vm((128, 256), jnp.bfloat16),
                vm((512, 256), jnp.bfloat16),
                vm((2, N_ZLO, N_X, SLAB, 128), f32),
                vm((N_ZLO, N_X, SLAB, 128), f32),
                vm((4, 2, HALF, 128), f32),
                vm((4, 2, HALF, 128), f32),
                vm((4, 2, HALF, 128), f32),
                vm((3, SLAB, 128), f32),
                vm((TOK, 2 * TOK), jnp.bfloat16),
                vm((N_FSDP, 1, 128), jnp.int32),
                vm((N_FSDP, TILE // 2, 128), f32),
                vm((N_FSDP, TILE // 2, 128), f32),
                vm((N_REP, TILE // 2, 128), f32),
                dma((8,)),
                dma((16,)),
                dma((16,)),
                dma((24,)),
                dma((24,)),
                dma((3,)),
                dma((3,)),
                dma,
                dma,
                dma,
                dma,
                dma,
                dma,
                pltpu.SemaphoreType.REGULAR,
            ],
            compiler_params=pltpu.CompilerParams(
                collective_id=0, has_side_effects=True, vmem_limit_bytes=48 * 1024 * 1024
            ),
            name="demo_step",
        )(*(
            pltpu.with_memory_space_constraint(a, pltpu.HBM)
            for a in (activations, out_grad, momentum, weight, kept_tile, *map(jnp.asarray, tables()))
        ))
    )


def solution(mesh):
    placed = (
        P(("rep", "fsdp"), None),
        P(("rep", "fsdp"), None),
        P("rep", "fsdp", None, None),
        P("fsdp", None, None),
        P("rep", "fsdp"),
    )
    return jax.shard_map(
        shards,
        mesh=mesh,
        in_specs=placed,
        out_specs=(P("rep", "fsdp", None, None), P("fsdp", None, None)),
        check_vma=False,
    )
```
